32 devices in a mesh: grp: 2 (over y), aux: 4 (over x, core), pair: 4 (over z).
Axes of the slice: x: 2, y: 2, z: 4, core: 2. Of those that a mesh axis runs over, the one named last changes fastest.
Arguments:
- three_centre: bfloat16 [8, 4, 8, 3, 1, 128, 640], P(('grp', 'aux'), 'pair'), parts along dimension 0, may hold values from -0.23925781 to 0.23925781
- locality: int32 [8, 4, 8, 3, 1], P(('grp', 'aux'), 'pair'), parts along dimension 0, may hold values 0 or 1
- live_blocks: int32 [8, 4], P(('grp', 'aux'), 'pair'), parts along dimension 0, may hold values from 2 to 8
- occ_energy: float32 [16], P('grp'), parts along dimension 0, may hold values from -1.2 to -0.4
- virt_energy: float32 [20480], P('grp'), parts along dimension 0, may hold values from 0.2 to 3
- frequencies: float32 [4], P('grp'), parts along dimension 0, may hold values from 0.3 to 3
Outputs:
- polarizability: float32 [2, 8, 8, 128, 384], P(None, None, ('grp', 'aux'), 'pair'), parts along dimension 2
The draws below stay inside these ranges and needn't reach their ends.
There are 2 independent parts, one for each index of `grp`. The reference program is written for one: setup_inputs(seed, part) draws one part's arguments, and reference() takes and returns one part's arrays. A program takes and returns all parts, laid end to end along the dimension named above; each array names one. Nothing has to cross between parts.
All inputs are finite; a program needn't handle non-finite values. No bound on the sum of `locality` on one device may be relied on, other than what follows from the above.
Results may differ from the reference program's by a relative error of at most 0.00095.
Values may be sent and summed in bfloat16 or wider, within the bound.
No kernel may reach another device: no remote copies, remote signals or barrier semaphores. Data moves between devices by JAX's collectives and lax.ppermute only.
A program may use at most 64 MiB of HBM per device.

```python
import math
import jax
import jax.numpy as jnp
from jax import lax

ABLK = 128
PROWS = 640
W = 3
AB_DEV = 8
PER = 1
VIRT = 10240
NFREQ = 2
PB_DEV = 8
NAB = 32
VB = 16
OCC = 8
N_AUX = 4
N_PAIR = 4


def place_ends(values, stream_key, smallest, high):
    longest = values.shape.index(max(values.shape))
    spots = []
    for shift in (0, 1):
        where = [jax.random.randint(jax.random.fold_in(stream_key, axis), (), 0, length) for axis, length in enumerate(values.shape)]
        where[longest] = (where[longest] + shift) % values.shape[longest]
        spots.append(tuple(where))
    return values.at[spots[0]].set(smallest).at[spots[1]].set(high)


def shard_levels(key, shape, cuts, least, top_value):
    level, own = 1.0, jax.random.fold_in(key, 6)
    for dim, shards_of in cuts:
        heights = jnp.exp(jax.random.uniform(jax.random.fold_in(own, dim), (shards_of,), jnp.float32, least / len(cuts), top_value / len(cuts)))
        level = level * jnp.repeat(heights, shape[dim] // shards_of).reshape([-1 if axis == dim else 1 for axis in range(len(shape))])
    return level


def scatter_about(stream_key, dims, scale, limit, shards=(), held_as=jnp.bfloat16):
    array = jax.random.normal(stream_key, dims, jnp.float32) * scale
    if len(shards) > 0:
        array = shard_levels(stream_key, dims, shards, -0.22, 0.18) * array
    return jnp.clip(array, min=-limit, max=limit).astype(held_as)


def setup_inputs(seed: int = 0, part: int = 0) -> dict:
    splits = jax.random.split(jax.random.key(seed), 7)
    part_splits = jax.random.split(jax.random.fold_in(splits[6], part), 7)
    return {
        "three_centre": scatter_about(part_splits[0], (N_AUX, N_PAIR, AB_DEV, W, PER, ABLK, PROWS), 0.04, 0.23925781, ((0, 4), (1, 4))),
        "locality": place_ends((jax.random.randint(part_splits[1], (N_AUX, N_PAIR, AB_DEV, W, PER), 0, 4) < 3).astype(jnp.int32), jax.random.fold_in(part_splits[1], 1), 0, 1),
        "live_blocks": place_ends(jax.random.randint(part_splits[2], (N_AUX, N_PAIR), max(1, AB_DEV * PER // 4), AB_DEV * PER + 1), jax.random.fold_in(part_splits[2], 1), max(1, AB_DEV * PER // 4), AB_DEV * PER).astype(jnp.int32),
        "occ_energy": jnp.clip(jax.random.uniform(part_splits[3], (OCC,), jnp.float32, -1.2, -0.4), -1.2, -0.4),
        "virt_energy": jnp.clip(jax.random.uniform(part_splits[4], (VIRT,), jnp.float32, 0.2, 3.0), 0.2, 3.0),
        "frequencies": jnp.clip(jnp.exp(jax.random.uniform(part_splits[5], (NFREQ,), jnp.float32, math.log(0.3), math.log(3.0))), 0.3, 3.0),
    }


def weigh(tiles, present, gaps, frequencies):
    omega = frequencies.reshape((-1,) + (1,) * gaps.ndim)
    factor = 2.0 * gaps[None] / (gaps[None] * gaps[None] + omega * omega)
    root = jnp.sqrt(factor)
    scaled = tiles.astype(jnp.float32)[None] * root[..., None, :]
    return (scaled * present[None, ..., None, None]).astype(jnp.bfloat16)

def reference(three_centre, locality, live_blocks, occ_energy, virt_energy, frequencies):
    local_block = jnp.arange(AB_DEV, dtype=jnp.int32)[None, :, None, None]
    owner = jnp.arange(N_AUX, dtype=jnp.int32)[:, None, None, None]
    slot_ids = jnp.arange(W, dtype=jnp.int32)[None, None, :, None]
    members = jnp.arange(PER, dtype=jnp.int32)[None, None, None, :]
    block_ids = local_block * N_AUX + owner
    centre = block_ids - slot_ids
    inside = centre >= 0
    safe = jnp.maximum(centre, 0)
    region = safe // AB_DEV
    number = safe % AB_DEV + AB_DEV * members
    table = virt_energy.reshape(VB, PROWS)

    def column(col, total):
        tiles = lax.dynamic_index_in_dim(three_centre, col, 1, keepdims=False)
        mask = lax.dynamic_index_in_dim(locality, col, 1, keepdims=False)
        counts = lax.dynamic_index_in_dim(live_blocks, col, 1, keepdims=False)
        present = (inside & (mask > 0) & (number < counts[region])).astype(jnp.float32)
        global_block = (region * N_PAIR + col) * PB_DEV + number
        gaps = table[global_block % VB] - occ_energy[global_block // VB][..., None]
        scaled = weigh(tiles, present, gaps, frequencies)
        ordered = jnp.swapaxes(scaled, 1, 2).reshape(NFREQ, NAB, W, PER, ABLK, PROWS)
        bands = []
        for delta in range(W):
            band_sum = jnp.zeros((NFREQ, NAB, ABLK, ABLK), jnp.float32)
            for slot in range(W - delta):
                left = ordered[:, :, slot].astype(jnp.float32)
                right = ordered[:, delta:, slot + delta]
                right = jnp.pad(right, ((0, 0), (0, delta), (0, 0), (0, 0), (0, 0))).astype(jnp.float32)
                band_sum = band_sum + jnp.einsum('fnkxr,fnkyr->fnxy', left, right)
            bands.append(band_sum)
        return total + jnp.stack(bands, axis=2)
    start = jnp.zeros((NFREQ, NAB, W, ABLK, ABLK), jnp.float32)
    total = lax.fori_loop(0, N_PAIR, column, start)
    return jnp.transpose(total, (0, 1, 3, 2, 4)).reshape(NFREQ, AB_DEV, N_AUX, ABLK, W * ABLK)
```

```python
import functools

import jax
import jax.numpy as jnp
from jax import lax
from jax.experimental import pallas as pl
from jax.experimental.pallas import tpu as pltpu
from jax.sharding import PartitionSpec as P

HEAD = 2


def band_kernel(dims, first, delta, slots, n_own, *refs):
    n_aux, n_pair, blocks_dev, band, freq_count = dims
    meta, occ, freq, table, own = refs[:5]
    others = refs[5:-1]
    out = refs[-1]
    virt_blocks = table.shape[0]
    record = blocks_dev * band + 1
    aux_pos, pair_col = meta[0], meta[1]
    shift = ((aux_pos + delta) >= n_aux).astype(jnp.int32)
    there = pl.program_id(0) + first
    here = there - shift
    block = here * n_aux + aux_pos
    far = lax.rem(aux_pos + delta, n_aux)
    sums = [None] * freq_count
    for slot in slots:
        centre = block - slot
        safe = jnp.maximum(centre, 0)
        region = safe // blocks_dev
        number = lax.rem(safe, blocks_dev)
        own_row = jnp.maximum(here, 0)
        live = meta[HEAD + region * record + blocks_dev * band]
        left_on = meta[HEAD + aux_pos * record + own_row * band + slot]
        right_on = meta[HEAD + far * record + there * band + slot + delta]
        keep = (centre >= 0) & (number < live) & (left_on > 0) & (right_on > 0)
        present = keep.astype(jnp.float32)
        pair_block = (region * n_pair + pair_col) * blocks_dev + number
        gap = table[pl.ds(lax.rem(pair_block, virt_blocks), 1), :] - occ[pair_block // virt_blocks]
        left = own[0, slot].astype(jnp.float32)
        right = None if delta == 0 else others[slot][0].astype(jnp.float32)
        for w in range(freq_count):
            omega = freq[w]
            root = jnp.sqrt(2.0 * gap / (gap * gap + omega * omega))
            a = (left * (root * present)).astype(jnp.bfloat16)
            b = a if right is None else (right * root).astype(jnp.bfloat16)
            term = lax.dot_general(a, b, (((1,), (1,)), ((), ())), preferred_element_type=jnp.float32)
            sums[w] = term if sums[w] is None else sums[w] + term
    for w in range(freq_count):
        out[w, 0] = sums[w]


def band_rows(dims, first, count, delta, meta, occ, freq, table, tiles, others):
    n_aux, n_pair, blocks_dev, band, freq_count = dims
    aux_rows, pair_rows = tiles.shape[-2:]
    slots = range(band - delta)

    def own_index(i, meta):
        shift = ((meta[0] + delta) >= n_aux).astype(jnp.int32)
        return (jnp.maximum(i + first - shift, 0), 0, 0, 0)

    def far_index(offset):
        return lambda i, meta: (i + offset, 0, 0)

    smem = pl.BlockSpec(memory_space=pltpu.SMEM)
    return pl.pallas_call(
        functools.partial(band_kernel, dims, first, delta, slots, len(others)),
        out_shape=jax.ShapeDtypeStruct((freq_count, count, aux_rows, aux_rows), jnp.float32),
        grid_spec=pltpu.PrefetchScalarGridSpec(
            num_scalar_prefetch=1,
            grid=(count,),
            in_specs=[
                smem,
                smem,
                pl.BlockSpec(table.shape, lambda i, meta: (0, 0)),
                pl.BlockSpec((1, band - delta, aux_rows, pair_rows), own_index),
            ]
            + [pl.BlockSpec((1, aux_rows, pair_rows), far_index(offset)) for _, offset in others],
            out_specs=pl.BlockSpec((freq_count, 1, aux_rows, aux_rows), lambda i, meta: (0, i, 0, 0)),
        ),
        cost_estimate=pl.CostEstimate(
            flops=4 * count * len(slots) * aux_rows * aux_rows * pair_rows,
            bytes_accessed=count * len(slots) * aux_rows * pair_rows * 4,
            transcendentals=0,
        ),
    )(meta, occ, freq, table, tiles, *[array for array, _ in others])


def spread(rows, pair_col, n_pair, scale):
    height = rows.shape[2] // n_pair
    parts = []
    for k in range(1, n_pair):
        start = lax.rem(pair_col + k, n_pair) * height
        part = (lax.dynamic_slice_in_dim(rows, start, height, 2) * scale).astype(jnp.float16)
        parts.append(lax.ppermute(part, "pair", [(s, (s + k) % n_pair) for s in range(n_pair)]))
    return lax.dynamic_slice_in_dim(rows, pair_col * height, height, 2), parts


def gather_sum(pieces, scale):
    own, parts = pieces
    far = sum(part.astype(jnp.float32) for part in parts)
    return own + far * (1.0 / scale)


def on_device(three_centre, locality, live_blocks, occ_energy, virt_energy, frequencies):
    n_aux = lax.axis_size("aux")
    n_pair = lax.axis_size("pair")
    aux_pos = lax.axis_index("aux")
    pair_col = lax.axis_index("pair")
    tiles = three_centre[0, 0, :, :, 0]
    blocks_dev, band, aux_rows, pair_rows = tiles.shape
    freq_count = frequencies.shape[0]
    dims = (n_aux, n_pair, blocks_dev, band, freq_count)
    half = blocks_dev // 2
    scale = 128.0 / n_pair
    table = virt_energy.reshape(-1, pair_rows)
    record = jnp.concatenate([locality[0, 0].reshape(-1), live_blocks[0]])
    records = lax.all_gather(record, "aux", tiled=True)
    meta = jnp.concatenate([jnp.stack([aux_pos, pair_col]).astype(jnp.int32), records])

    down1 = [(s, (s - 1) % n_aux) for s in range(n_aux)]
    down2 = [(s, (s - 2) % n_aux) for s in range(n_aux)]
    swap = [(s, s ^ 1) for s in range(n_aux)]
    c2 = [lax.ppermute(tiles[h : h + half, 2], "aux", down2) for h in (0, half)]
    b1 = [lax.ppermute(tiles[h : h + half, 1], "aux", down1) for h in (0, half)]
    args = (meta, occ_energy, frequencies, table, tiles)
    z0 = spread(band_rows(dims, 0, blocks_dev, 0, *args, []), pair_col, n_pair, scale)
    even = aux_pos % 2 == 0
    z2, b2 = [], []
    for n, h in enumerate((0, half)):
        b2.append(lax.ppermute(jnp.where(even, c2[n], tiles[h : h + half, 2]), "aux", swap))
        z2.append(spread(band_rows(dims, h, half, 2, *args, [(c2[n], 0)]), pair_col, n_pair, scale))
    z1 = []
    for n, h in enumerate((0, half)):
        z1.append(
            spread(band_rows(dims, h, half, 1, *args, [(b1[n], 0), (b2[n], 0)]), pair_col, n_pair, scale)
        )

    def settle(pieces, delta):
        rows = jnp.concatenate([gather_sum(piece, scale) for piece in pieces], axis=1)
        return jnp.where(aux_pos + delta >= n_aux, jnp.roll(rows, -1, axis=1), rows) if delta else rows

    out = jnp.concatenate([settle([z0], 0), settle(z1, 1), settle(z2, 2)], axis=-1)
    return out[:, :, None]


def solution(mesh):
    return jax.shard_map(
        on_device,
        mesh=mesh,
        in_specs=(
            P(("grp", "aux"), "pair", None, None, None, None, None),
            P(("grp", "aux"), "pair", None, None, None),
            P(("grp", "aux"), "pair"),
            P("grp"),
            P("grp"),
            P("grp"),
        ),
        out_specs=P(None, None, ("grp", "aux"), "pair", None),
        check_vma=False,
    )
```

```python
import functools

import jax
import jax.numpy as jnp
from jax import lax
from jax.experimental import pallas as pl
from jax.experimental.pallas import tpu as pltpu
from jax.sharding import PartitionSpec as P

HEAD = 2
ANY = pl.BlockSpec(memory_space=pl.ANY)
SMEM = pl.BlockSpec(memory_space=pltpu.SMEM)
VMEM = pl.BlockSpec(memory_space=pltpu.VMEM)


def chunks_of(count, sizes):
    ends = [count * sum(sizes[: n + 1]) // sum(sizes) for n in range(len(sizes))]
    return [(a, b - a) for a, b in zip([0] + ends[:-1], ends)]


def pack_kernel(plan, n_aux, tiles, *refs):
    outs, sem = refs[:-1], refs[-1]
    aux_pos = lax.axis_index("aux")
    blocks_dev = tiles.shape[0]
    copies = []
    for out, (slot, back, first) in zip(outs, plan):
        shift = (aux_pos < back).astype(jnp.int32)
        for i in range(out.shape[0]):
            row = jnp.minimum(first + i + shift, blocks_dev - 1)
            copies.append(pltpu.make_async_copy(tiles.at[row, slot], out.at[i], sem.at[len(copies)]))
    for copy in copies:
        copy.start()
    for copy in copies:
        copy.wait()


def pack(tiles, n_aux, plan, counts):
    return pl.pallas_call(
        functools.partial(pack_kernel, plan, n_aux),
        out_shape=[jax.ShapeDtypeStruct((count,) + tiles.shape[-2:], tiles.dtype) for count in counts],
        in_specs=[ANY],
        out_specs=[ANY] * len(counts),
        scratch_shapes=[pltpu.SemaphoreType.DMA((sum(counts),))],
    )(tiles)


def band_kernel(dims, first, delta, *refs):
    n_aux, n_pair, blocks_dev, band, freq_count = dims
    meta, occ, freq, table, own = refs[:5]
    far = refs[5:-4]
    out, own_buf, far_buf, sem = refs[-4:]
    count = out.shape[1]
    slots = band - delta
    virt_blocks = table.shape[0]
    record = blocks_dev * band + 1
    aux_pos, pair_col = meta[0], meta[1]
    shift = ((aux_pos + delta) >= n_aux).astype(jnp.int32)
    behind = lax.rem(2 * n_aux - delta, n_aux)
    even = lax.rem(aux_pos, 2) == 0

    def own_copy(i):
        return pltpu.make_async_copy(own.at[first + i, pl.ds(0, slots)], own_buf.at[i], sem.at[0, i])

    def far_copy(i, slot, array):
        return pltpu.make_async_copy(array.at[i], far_buf.at[i, slot], sem.at[1 + slot, i])

    for i in range(count):
        own_copy(i).start()
        if delta > 0:
            far_copy(i, 0, far[0]).start()
        if delta == 1:
            even_from, odd_from = far[1], far[2]

            @pl.when(even)
            def _():
                far_copy(i, 1, even_from.at[pl.ds(first, count)]).start()

            @pl.when(jnp.logical_not(even))
            def _():
                far_copy(i, 1, odd_from.at[pl.ds(first, count)]).start()

    for i in range(count):
        here = first + i
        block = here * n_aux + aux_pos
        there = here + shift
        safe_there = jnp.minimum(there, blocks_dev - 1)
        own_copy(i).wait()
        sums = [None] * freq_count
        for slot in range(slots):
            if delta > 0:
                far_copy(i, slot, far[0]).wait()
            centre = block - slot
            safe = jnp.maximum(centre, 0)
            region = safe // blocks_dev
            number = lax.rem(safe, blocks_dev)
            live = meta[HEAD + lax.rem(aux_pos - region + n_aux, n_aux) * record + blocks_dev * band]
            left_on = meta[HEAD + here * band + slot]
            right_on = meta[HEAD + behind * record + safe_there * band + slot + delta]
            keep = (centre >= 0) & (number < live) & (left_on > 0) & (right_on > 0) & (there < blocks_dev)
            present = keep.astype(jnp.float32)
            pair_block = (region * n_pair + pair_col) * blocks_dev + number
            gap = table[pl.ds(lax.rem(pair_block, virt_blocks), 1), :] - occ[pair_block // virt_blocks]
            left = own_buf[i, slot].astype(jnp.float32)
            right = None if delta == 0 else far_buf[i, slot].astype(jnp.float32)
            for w in range(freq_count):
                omega = freq[w]
                root = jnp.sqrt(2.0 * gap / (gap * gap + omega * omega))
                a = (left * (root * present)).astype(jnp.bfloat16)
                b = a if right is None else (right * root).astype(jnp.bfloat16)
                term = lax.dot_general(a, b, (((1,), (1,)), ((), ())), preferred_element_type=jnp.float32)
                sums[w] = term if sums[w] is None else sums[w] + term
        for w in range(freq_count):
            out[w, i] = sums[w]


def band_rows(dims, first, count, delta, meta, occ, freq, table, tiles, far):
    n_aux, n_pair, blocks_dev, band, freq_count = dims
    aux_rows, pair_rows = tiles.shape[-2:]
    slots = band - delta
    far_shape = (count, slots, aux_rows, pair_rows) if far else (1, 1, 16, 128)
    return pl.pallas_call(
        functools.partial(band_kernel, dims, first, delta),
        out_shape=jax.ShapeDtypeStruct((freq_count, count, aux_rows, aux_rows), jnp.float32),
        in_specs=[SMEM, SMEM, SMEM, VMEM, ANY] + [ANY] * len(far),
        out_specs=VMEM,
        scratch_shapes=[
            pltpu.VMEM((count, slots, aux_rows, pair_rows), tiles.dtype),
            pltpu.VMEM(far_shape, tiles.dtype),
            pltpu.SemaphoreType.DMA((1 + slots, count)),
        ],
        compiler_params=pltpu.CompilerParams(vmem_limit_bytes=24 << 20),
        cost_estimate=pl.CostEstimate(flops=1000, bytes_accessed=1000, transcendentals=0),
    )(meta, occ, freq, table, tiles, *far)


def spread(rows, pair_col, n_pair, scale):
    freq_count, count, aux_rows, width = rows.shape
    height = aux_rows // n_pair
    keep = rows.reshape(freq_count, count, n_pair, height, width)
    step = 1
    while step < n_pair:
        half = keep.shape[2] // 2
        keep = keep.reshape(freq_count, count, half, 2, height, width)
        bit = (pair_col // step) % 2
        part = lax.dynamic_index_in_dim(keep, 1 - bit, 3, keepdims=False)
        mine = lax.dynamic_index_in_dim(keep, bit, 3, keepdims=False)
        sent = (part * scale).astype(jnp.float16)
        got = lax.ppermute(sent, "pair", [(s, s ^ step) for s in range(n_pair)])
        keep = mine + got.astype(jnp.float32) * (1.0 / scale)
        step *= 2
    return keep[:, :, 0]


def on_device(three_centre, locality, live_blocks, occ_energy, virt_energy, frequencies):
    n_aux = lax.axis_size("aux")
    n_pair = lax.axis_size("pair")
    aux_pos = lax.axis_index("aux")
    pair_col = lax.axis_index("pair")
    tiles = three_centre[0, 0, :, :, 0]
    blocks_dev, band, aux_rows, pair_rows = tiles.shape
    freq_count = frequencies.shape[0]
    dims = (n_aux, n_pair, blocks_dev, band, freq_count)
    scale = 128.0 / n_pair
    table = virt_energy.reshape(-1, pair_rows)
    record = jnp.concatenate([locality[0, 0].reshape(-1), live_blocks[0]])
    records = [record] + [
        lax.ppermute(record, "aux", [(s, (s + k) % n_aux) for s in range(n_aux)]) for k in range(1, n_aux)
    ]
    meta = jnp.concatenate([jnp.stack([aux_pos, pair_col]).astype(jnp.int32)] + records)

    two = chunks_of(blocks_dev, (4, 4))
    one = chunks_of(blocks_dev, (5, 3))
    plan = [(2, 2, f) for f, _ in two] + [(1, 1, f) for f, _ in one] + [(2, 0, 0)]
    packed = pack(tiles, n_aux, plan, [c for _, c in two + one] + [blocks_dev])
    packed, meta = lax.optimization_barrier((packed, meta))
    down1 = [(s, (s - 1) % n_aux) for s in range(n_aux)]
    down2 = [(s, (s - 2) % n_aux) for s in range(n_aux)]
    c2 = [lax.ppermute(packed[n], "aux", down2) for n in range(2)]
    b1 = [lax.ppermute(packed[2 + n], "aux", down1) for n in range(2)]
    to_even = lax.ppermute(packed[4], "aux", [(s, s - 1) for s in range(1, n_aux, 2)])
    args = (meta, occ_energy, frequencies, table, tiles)
    z0 = spread(band_rows(dims, 0, blocks_dev, 0, *args, []), pair_col, n_pair, scale)
    to_odd, z2 = [], []
    for n, (first, count) in enumerate(two):
        to_odd.append(lax.ppermute(c2[n], "aux", [(s, s + 1) for s in range(0, n_aux, 2)]))
        z2.append(spread(band_rows(dims, first, count, 2, *args, [c2[n]]), pair_col, n_pair, scale))
    to_odd = jnp.concatenate(to_odd)
    z1 = []
    for n, (first, count) in enumerate(one):
        far = [b1[n], to_even, to_odd]
        z1.append(spread(band_rows(dims, first, count, 1, *args, far), pair_col, n_pair, scale))
    out = jnp.concatenate([z0, jnp.concatenate(z1, axis=1), jnp.concatenate(z2, axis=1)], axis=-1)
    return out[:, :, None]


def solution(mesh):
    return jax.shard_map(
        on_device,
        mesh=mesh,
        in_specs=(
            P(("grp", "aux"), "pair", None, None, None, None, None),
            P(("grp", "aux"), "pair", None, None, None),
            P(("grp", "aux"), "pair"),
            P("grp"),
            P("grp"),
            P("grp"),
        ),
        out_specs=P(None, None, ("grp", "aux"), "pair", None),
        check_vma=False,
    )
```

```python
import functools

import jax
import jax.numpy as jnp
from jax import lax
from jax.experimental import pallas as pl
from jax.experimental.pallas import tpu as pltpu
from jax.sharding import PartitionSpec as P

HEAD = 2
LIMIT = 61 << 20
COST = pl.CostEstimate(flops=1000, bytes_accessed=1000, transcendentals=0)
ANY = pl.BlockSpec(memory_space=pl.ANY)
HBM = pl.BlockSpec(memory_space=pltpu.HBM)
SMEM = pl.BlockSpec(memory_space=pltpu.SMEM)
VMEM = pl.BlockSpec(memory_space=pltpu.VMEM)


def chunks_of(count, sizes):
    ends = [count * sum(sizes[: n + 1]) // sum(sizes) for n in range(len(sizes))]
    return [(a, b - a) for a, b in zip([0] + ends[:-1], ends)]


def pack_kernel(plan, tiles, *refs):
    outs, held, sem_in, sem_out = refs[:-3], refs[-3], refs[-2], refs[-1]
    aux_pos = lax.axis_index("aux")
    blocks_dev = tiles.shape[0]
    loads = [pltpu.make_async_copy(tiles.at[m], held.at[m], sem_in.at[m]) for m in range(blocks_dev)]
    copies = []
    for out, (slot, back, first) in zip(outs, plan):
        shift = (aux_pos < back).astype(jnp.int32)
        for i in range(out.shape[0]):
            row = jnp.minimum(first + i + shift, blocks_dev - 1)
            copies.append(pltpu.make_async_copy(held.at[row, slot], out.at[i], sem_out.at[len(copies)]))
    for load in loads:
        load.start()
    for load in loads:
        load.wait()
    for copy in copies:
        copy.start()
    for copy in copies:
        copy.wait()


def pack(tiles, plan, counts):
    return pl.pallas_call(
        functools.partial(pack_kernel, plan),
        out_shape=[jax.ShapeDtypeStruct((count,) + tiles.shape[-2:], tiles.dtype) for count in counts],
        in_specs=[HBM],
        out_specs=[HBM] * len(counts),
        scratch_shapes=[
            pltpu.VMEM(tiles.shape, tiles.dtype),
            pltpu.SemaphoreType.DMA((tiles.shape[0],)),
            pltpu.SemaphoreType.DMA((sum(counts),)),
        ],
        compiler_params=pltpu.CompilerParams(vmem_limit_bytes=LIMIT),
        cost_estimate=COST,
    )(tiles)


def band_kernel(dims, first, delta, pick, *refs):
    n_aux, n_pair, blocks_dev, band, freq_count = dims
    meta, occ, freq, table, own = refs[:5]
    far = refs[5:-4]
    out, mark, held, sem = refs[-4:]
    count = out.shape[1]
    slots = band - delta
    loads = [
        pltpu.make_async_copy(own.at[first + i, pl.ds(0, slots)], held.at[i], sem.at[i]) for i in range(count)
    ]
    for load in loads:
        load.start()
    virt_blocks = table.shape[0]
    record = blocks_dev * band + 1
    aux_pos, pair_col = meta[0], meta[1]
    shift = ((aux_pos + delta) >= n_aux).astype(jnp.int32)
    behind = lax.rem(2 * n_aux - delta, n_aux)
    even = lax.rem(aux_pos, 2) == 0
    mark[0] = pair_col
    for load in loads:
        load.wait()
    for i in range(count):
        here = first + i
        block = here * n_aux + aux_pos
        there = here + shift
        safe_there = jnp.minimum(there, blocks_dev - 1)
        sums = [None] * freq_count
        for slot in range(slots):
            centre = block - slot
            safe = jnp.maximum(centre, 0)
            region = safe // blocks_dev
            number = lax.rem(safe, blocks_dev)
            live = meta[HEAD + lax.rem(aux_pos - region + n_aux, n_aux) * record + blocks_dev * band]
            left_on = meta[HEAD + here * band + slot]
            right_on = meta[HEAD + behind * record + safe_there * band + slot + delta]
            keep = (centre >= 0) & (number < live) & (left_on > 0) & (right_on > 0) & (there < blocks_dev)
            present = keep.astype(jnp.float32)
            pair_block = (region * n_pair + pair_col) * blocks_dev + number
            gap = table[pl.ds(lax.rem(pair_block, virt_blocks), 1), :] - occ[pair_block // virt_blocks]
            left = held[i, slot].astype(jnp.float32)
            right = None
            if delta > 0:
                places = [far[n][row] for n, row in pick[i][slot]]
                right = places[0] if len(places) == 1 else jnp.where(even, places[0], places[1])
                right = right.astype(jnp.float32)
            for w in range(freq_count):
                omega = freq[w]
                root = jnp.sqrt(2.0 * gap / (gap * gap + omega * omega))
                a = (left * (root * present)).astype(jnp.bfloat16)
                b = a if right is None else (right * root).astype(jnp.bfloat16)
                term = lax.dot_general(a, b, (((1,), (1,)), ((), ())), preferred_element_type=jnp.float32)
                sums[w] = term if sums[w] is None else sums[w] + term
        for w in range(freq_count):
            out[w, i] = sums[w]


def band_rows(dims, first, count, delta, args, far=(), pick=None, after=()):
    meta, occ, freq, table, tiles = args
    n_aux, n_pair, blocks_dev, band, freq_count = dims
    aux_rows, pair_rows = tiles.shape[-2:]

    def body(*refs):
        ins = refs[: 5 + len(far)]
        band_kernel(dims, first, delta, pick, *ins, *refs[-4:])

    return pl.pallas_call(
        body,
        out_shape=[
            jax.ShapeDtypeStruct((freq_count, count, aux_rows, aux_rows), jnp.float32),
            jax.ShapeDtypeStruct((1,), jnp.int32),
        ],
        in_specs=[SMEM, SMEM, SMEM, VMEM, HBM] + [VMEM] * len(far) + [ANY] * len(after),
        out_specs=[VMEM, SMEM],
        scratch_shapes=[
            pltpu.VMEM((count, band - delta, aux_rows, pair_rows), tiles.dtype),
            pltpu.SemaphoreType.DMA((count,)),
        ],
        compiler_params=pltpu.CompilerParams(vmem_limit_bytes=LIMIT),
        cost_estimate=COST,
    )(meta, occ, freq, table, tiles, *far, *after)


def trade(keep, pair_col, step, n_pair, scale):
    freq_count, count, shares, height, width = keep.shape
    keep = keep.reshape(freq_count, count, shares // 2, 2, height, width)
    bit = (pair_col // step) % 2
    part = lax.dynamic_index_in_dim(keep, 1 - bit, 3, keepdims=False)
    mine = lax.dynamic_index_in_dim(keep, bit, 3, keepdims=False)
    sent = (part * scale).astype(jnp.float16)
    got = lax.ppermute(sent, "pair", [(s, s ^ step) for s in range(n_pair)])
    return mine, got


class Sum:
    def __init__(self, rows, n_pair, scale):
        freq_count, count, aux_rows, width = rows.shape
        self.keep = rows.reshape(freq_count, count, n_pair, aux_rows // n_pair, width)
        self.n_pair, self.scale, self.step = n_pair, scale, 1

    def advance(self, mark):
        if self.step < self.n_pair:
            mine, got = trade(self.keep, mark[0], self.step, self.n_pair, self.scale)
            self.keep = mine + got.astype(jnp.float32) * (1.0 / self.scale)
            self.step *= 2

    def finish(self, mark):
        while self.step < self.n_pair:
            self.advance(mark)
        return self.keep[:, :, 0]


def on_device(three_centre, locality, live_blocks, occ_energy, virt_energy, frequencies):
    n_aux = lax.axis_size("aux")
    n_pair = lax.axis_size("pair")
    aux_pos = lax.axis_index("aux")
    pair_col = lax.axis_index("pair")
    tiles = three_centre[0, 0, :, :, 0]
    blocks_dev, band, aux_rows, pair_rows = tiles.shape
    freq_count = frequencies.shape[0]
    dims = (n_aux, n_pair, blocks_dev, band, freq_count)
    scale = 128.0 / n_pair
    table = virt_energy.reshape(-1, pair_rows)
    record = jnp.concatenate([locality[0, 0].reshape(-1), live_blocks[0]])
    records = [record] + [
        lax.ppermute(record, "aux", [(s, (s + k) % n_aux) for s in range(n_aux)]) for k in range(1, n_aux)
    ]
    meta = jnp.concatenate([jnp.stack([aux_pos, pair_col]).astype(jnp.int32)] + records)

    two = chunks_of(blocks_dev, (4, 4))
    one = chunks_of(blocks_dev, (5, 3))
    plan = [(2, 2, f) for f, _ in two] + [(1, 1, f) for f, _ in one] + [(2, 0, 0)]
    packed = pack(tiles, plan, [c for _, c in two + one] + [blocks_dev])
    down1 = [(s, (s - 1) % n_aux) for s in range(n_aux)]
    down2 = [(s, (s - 2) % n_aux) for s in range(n_aux)]
    c2 = [lax.ppermute(packed[n], "aux", down2) for n in range(2)]
    b1 = [lax.ppermute(packed[2 + n], "aux", down1) for n in range(2)]
    to_even = lax.ppermute(packed[4], "aux", [(s, s - 1) for s in range(1, n_aux, 2)])
    to_odd = [lax.ppermute(c, "aux", [(s, s + 1) for s in range(0, n_aux, 2)]) for c in c2]
    args = (meta, occ_energy, frequencies, table, tiles)
    rows, mark = band_rows(dims, 0, blocks_dev, 0, args)
    sums = [Sum(rows, n_pair, scale)]
    sums[0].advance(mark)
    for n, (first, count) in enumerate(two):
        pick = [[[(0, i)]] for i in range(count)]
        rows, mark = band_rows(dims, first, count, 2, args, [c2[n]], pick, [rows])
        sums.append(Sum(rows, n_pair, scale))
        for part in sums:
            part.advance(mark)
    where = [(n, i) for n, (_, count) in enumerate(two) for i in range(count)]
    for n, (first, count) in enumerate(one):
        pick = []
        for i in range(count):
            piece, row = where[first + i]
            pick.append([[(0, i)], [(1, first + i), (2 + piece, row)]])
        rows, mark = band_rows(dims, first, count, 1, args, [b1[n], to_even, *to_odd], pick, [rows])
        sums.append(Sum(rows, n_pair, scale))
        for part in sums:
            part.advance(mark)
    done = [part.finish(mark) for part in sums]
    out = jnp.concatenate(
        [done[0], jnp.concatenate(done[3:], axis=1), jnp.concatenate(done[1:3], axis=1)], axis=-1
    )
    return out[:, :, None]


def solution(mesh):
    return jax.shard_map(
        on_device,
        mesh=mesh,
        in_specs=(
            P(("grp", "aux"), "pair", None, None, None, None, None),
            P(("grp", "aux"), "pair", None, None, None),
            P(("grp", "aux"), "pair"),
            P("grp"),
            P("grp"),
            P("grp"),
        ),
        out_specs=P(None, None, ("grp", "aux"), "pair", None),
        check_vma=False,
    )
```

```python
import functools

import jax
import jax.numpy as jnp
from jax import lax
from jax.experimental import pallas as pl
from jax.experimental.pallas import tpu as pltpu
from jax.sharding import PartitionSpec as P

LIMIT = 61 << 20
COST = pl.CostEstimate(flops=1000, bytes_accessed=1000, transcendentals=0)
PARAMS = pltpu.CompilerParams(vmem_limit_bytes=LIMIT)
ANY = pl.BlockSpec(memory_space=pl.ANY)
HBM = pl.BlockSpec(memory_space=pltpu.HBM)
SMEM = pl.BlockSpec(memory_space=pltpu.SMEM)
VMEM = pl.BlockSpec(memory_space=pltpu.VMEM)
DMA = pltpu.SemaphoreType.DMA


def chunks_of(count, sizes):
    ends = [count * sum(sizes[: n + 1]) // sum(sizes) for n in range(len(sizes))]
    return [(a, b - a) for a, b in zip([0] + ends[:-1], ends)]


def dot(a, b):
    return lax.dot_general(a, b, (((1,), (1,)), ((), ())), preferred_element_type=jnp.float32)


def pack_kernel(plan, n_after, tiles, *refs):
    outs, held, sem_in, sem_out = refs[n_after:-3], refs[-3], refs[-2], refs[-1]
    aux_pos = lax.axis_index("aux")
    blocks_dev = tiles.shape[0]
    loads, stores = [], []
    for out, (slot, back, first) in zip(outs, plan):
        shift = (aux_pos < back).astype(jnp.int32)
        for i in range(out.shape[0]):
            n = len(loads)
            row = jnp.minimum(first + i + shift, blocks_dev - 1)
            loads.append(pltpu.make_async_copy(tiles.at[row, slot], held.at[n], sem_in.at[n]))
            stores.append(pltpu.make_async_copy(held.at[n], out.at[i], sem_out.at[n]))
    for load in loads:
        load.start()
    for load, store in zip(loads, stores):
        load.wait()
        store.start()
    for store in stores:
        store.wait()


def pack(tiles, plan, counts, after):
    total = sum(counts)
    return pl.pallas_call(
        functools.partial(pack_kernel, plan, len(after)),
        out_shape=[jax.ShapeDtypeStruct((count,) + tiles.shape[-2:], tiles.dtype) for count in counts],
        in_specs=[HBM] + [ANY] * len(after),
        out_specs=[HBM] * len(counts),
        scratch_shapes=[pltpu.VMEM((total,) + tiles.shape[-2:], tiles.dtype), DMA((total,)), DMA((total,))],
        compiler_params=PARAMS,
        cost_estimate=COST,
    )(tiles, *after)


def root_row(band, freq_count, delta, slot, w):
    before = 0 if delta is None else band + sum(band - d for d in range(1, delta))
    return (before + slot) * freq_count + w


def root_rows(band, freq_count):
    rows = freq_count * (band + sum(band - d for d in range(1, band)))
    return -(-rows // 8) * 8


def first_kernel(dims, *refs):
    n_aux, n_pair, blocks_dev, band, freq_count = dims
    records = refs[:n_aux]
    occ, freq, table, own = refs[n_aux : n_aux + 4]
    out, roots, last, held, sem, sem_out = refs[-6:]
    pair_rows = own.shape[-1]
    virt_blocks = table.shape[1] // pair_rows
    aux_pos, pair_col = lax.axis_index("aux"), lax.axis_index("pair")
    loads = [pltpu.make_async_copy(own.at[m], held.at[m], sem.at[m]) for m in range(blocks_dev)]
    stores = [pltpu.make_async_copy(held.at[m, band - 1], last.at[m], sem_out.at[m]) for m in range(blocks_dev)]
    for load in loads:
        load.start()

    def of_region(region):
        live = records[0][blocks_dev * band]
        for k in range(1, n_aux):
            live = jnp.where(lax.rem(aux_pos - region + n_aux, n_aux) == k, records[k][blocks_dev * band], live)
        return live

    masked = {}
    for m in range(blocks_dev):
        block = m * n_aux + aux_pos
        for slot in range(band):
            centre = block - slot
            safe = jnp.maximum(centre, 0)
            region = safe // blocks_dev
            number = lax.rem(safe, blocks_dev)
            pair_block = (region * n_pair + pair_col) * blocks_dev + number
            start = pl.multiple_of(lax.rem(pair_block, virt_blocks) * pair_rows, pair_rows)
            gap = table[:, pl.ds(start, pair_rows)] - occ[pair_block // virt_blocks]
            alive = (centre >= 0) & (number < of_region(region)) & (records[0][m * band + slot] > 0)
            for w in range(freq_count):
                omega = freq[w]
                root = jnp.sqrt(2.0 * gap / (gap * gap + omega * omega))
                roots[m, pl.ds(root_row(band, freq_count, None, slot, w), 1), :] = root
                masked[m, slot, w] = root * alive.astype(jnp.float32)
                for delta in range(1, band - slot):
                    there = m + ((aux_pos + delta) >= n_aux).astype(jnp.int32)
                    row = jnp.minimum(there, blocks_dev - 1) * band + slot + delta
                    both = alive & (there < blocks_dev) & (records[(n_aux - delta) % n_aux][row] > 0)
                    spot = root_row(band, freq_count, delta, slot, w)
                    roots[m, pl.ds(spot, 1), :] = root * both.astype(jnp.float32)
    for load in loads:
        load.wait()
    for store in stores:
        store.start()
    for m in range(blocks_dev):
        for w in range(freq_count):
            total = None
            for slot in range(band):
                a = (held[m, slot].astype(jnp.float32) * masked[m, slot, w]).astype(jnp.bfloat16)
                term = dot(a, a)
                total = term if total is None else total + term
            out[w, m] = total
    for store in stores:
        store.wait()


def first_rows(dims, records, occ, freq, table, tiles, after):
    n_aux, n_pair, blocks_dev, band, freq_count = dims
    aux_rows, pair_rows = tiles.shape[-2:]
    return pl.pallas_call(
        functools.partial(first_kernel, dims),
        out_shape=[
            jax.ShapeDtypeStruct((freq_count, blocks_dev, aux_rows, aux_rows), jnp.float32),
            jax.ShapeDtypeStruct((blocks_dev, root_rows(band, freq_count), pair_rows), jnp.float32),
            jax.ShapeDtypeStruct((blocks_dev, aux_rows, pair_rows), tiles.dtype),
        ],
        in_specs=[SMEM] * (n_aux + 2) + [VMEM, HBM] + [ANY] * len(after),
        out_specs=[VMEM, VMEM, HBM],
        scratch_shapes=[pltpu.VMEM(tiles.shape, tiles.dtype), DMA((blocks_dev,)), DMA((blocks_dev,))],
        compiler_params=PARAMS,
        cost_estimate=COST,
    )(*records, occ, freq, table, tiles, *after)


def pieces_of(arrays, first, count):
    parts, start = [], 0
    for n, array in enumerate(arrays):
        low, high = max(first, start), min(first + count, start + array.shape[0])
        if low < high:
            parts.append((n, low - start, low - first, high - low))
        start += array.shape[0]
    return parts


def band_kernel(dims, first, delta, groups, roots, own, *refs):
    n_aux, n_pair, blocks_dev, band, freq_count = dims
    out, held, held_far, sem, sem_far = refs[-5:]
    count, slots = out.shape[1], band - delta
    even = lax.rem(lax.axis_index("aux"), 2) == 0

    def far_copies(slot, group):
        return [
            pltpu.make_async_copy(
                refs[n].at[pl.ds(low, length)], held_far.at[slot, pl.ds(to, length)], sem_far.at[slot, k]
            )
            for k, (n, low, to, length) in enumerate(group)
        ]

    near = [
        pltpu.make_async_copy(own.at[first + i, pl.ds(0, slots)], held.at[i], sem.at[i]) for i in range(count)
    ]
    for copy in near + far_copies(0, groups[0]):
        copy.start()
    if slots > 1:

        @pl.when(even)
        def _():
            for copy in far_copies(1, groups[1]):
                copy.start()
            for copy in far_copies(1, groups[1]):
                copy.wait()

        @pl.when(jnp.logical_not(even))
        def _():
            for copy in far_copies(1, groups[2]):
                copy.start()
            for copy in far_copies(1, groups[2]):
                copy.wait()

    for copy in near + far_copies(0, groups[0]):
        copy.wait()
    for i in range(count):
        m = first + i
        sums = [None] * freq_count
        for slot in range(slots):
            left = held[i, slot].astype(jnp.float32)
            right = held_far[slot, i].astype(jnp.float32)
            for w in range(freq_count):
                kept = roots[m, pl.ds(root_row(band, freq_count, delta, slot, w), 1), :]
                root = roots[m, pl.ds(root_row(band, freq_count, None, slot, w), 1), :]
                term = dot((left * kept).astype(jnp.bfloat16), (right * root).astype(jnp.bfloat16))
                sums[w] = term if sums[w] is None else sums[w] + term
        for w in range(freq_count):
            out[w, i] = sums[w]


def band_rows(dims, first, count, delta, roots, tiles, far, after):
    n_aux, n_pair, blocks_dev, band, freq_count = dims
    aux_rows, pair_rows = tiles.shape[-2:]
    slots = band - delta
    groups, arrays = [], []
    for group in far:
        parts = pieces_of(group, first, count)
        groups.append([(len(arrays) + n, low, to, length) for n, low, to, length in parts])
        arrays += group
    return pl.pallas_call(
        functools.partial(band_kernel, dims, first, delta, groups),
        out_shape=jax.ShapeDtypeStruct((freq_count, count, aux_rows, aux_rows), jnp.float32),
        in_specs=[VMEM, HBM] + [HBM] * len(arrays) + [ANY] * len(after),
        out_specs=VMEM,
        scratch_shapes=[
            pltpu.VMEM((count, slots, aux_rows, pair_rows), tiles.dtype),
            pltpu.VMEM((slots, count, aux_rows, pair_rows), tiles.dtype),
            DMA((count,)),
            DMA((slots, max(len(group) for group in groups))),
        ],
        compiler_params=PARAMS,
        cost_estimate=COST,
    )(roots, tiles, *arrays, *after)


def halve(keep, pair_col, step, n_pair, scale):
    freq_count, count, shares, height, width = keep.shape
    keep = keep.reshape(freq_count, count, shares // 2, 2, height, width)
    bit = (pair_col // step) & 1
    part = lax.dynamic_index_in_dim(keep, 1 - bit, 3, keepdims=False)
    mine = lax.dynamic_index_in_dim(keep, bit, 3, keepdims=False)
    sent = (part * scale).astype(jnp.float16)
    got = lax.ppermute(sent, "pair", [(s, s ^ step) for s in range(n_pair)])
    return mine + got.astype(jnp.float32) * (1.0 / scale), got


def totals(rows, pair_col, n_pair, scale):
    freq_count, count, aux_rows, width = rows.shape
    keep = rows.reshape(freq_count, count, n_pair, aux_rows // n_pair, width)
    stages, step = [], 1
    while step < n_pair:
        keep, got = halve(keep, pair_col, step, n_pair, scale)
        stages.append(got[0, 0, 0].astype(jnp.float32))
        step *= 2
    return stages[0], keep[:, :, 0]


def on_device(three_centre, locality, live_blocks, occ_energy, virt_energy, frequencies):
    n_aux = lax.axis_size("aux")
    n_pair = lax.axis_size("pair")
    pair_col = lax.axis_index("pair").astype(jnp.uint32).astype(jnp.int32)
    tiles = three_centre[0, 0, :, :, 0]
    blocks_dev, band, aux_rows, pair_rows = tiles.shape
    freq_count = frequencies.shape[0]
    dims = (n_aux, n_pair, blocks_dev, band, freq_count)
    scale = 128.0 / n_pair
    record = jnp.concatenate([locality[0, 0].reshape(-1), live_blocks[0]])
    records = [record] + [
        lax.ppermute(record, "aux", [(s, (s + k) % n_aux) for s in range(n_aux)]) for k in range(1, n_aux)
    ]
    two = chunks_of(blocks_dev, (4, 4))
    one = chunks_of(blocks_dev, (8,))
    plan = [(2, 2, first) for first, _ in two] + [(1, 1, first) for first, _ in one]
    packed = pack(tiles, plan, [count for _, count in two + one], records[1:])
    down = [[(s, (s - d) % n_aux) for s in range(n_aux)] for d in range(3)]
    c2 = [lax.ppermute(p, "aux", down[2]) for p in packed[: len(two)]]
    b1 = [lax.ppermute(p, "aux", down[1]) for p in packed[len(two) :]]
    table = virt_energy.reshape(1, -1)
    rows0, roots, last = first_rows(dims, records, occ_energy, frequencies, table, tiles, packed[:1])
    z0 = totals(rows0, pair_col, n_pair, scale)
    to_even = [lax.ppermute(last, "aux", [(s, s - 1) for s in range(1, n_aux, 2)])]
    to_odd = [lax.ppermute(c, "aux", [(s, s + 1) for s in range(0, n_aux, 2)]) for c in c2]
    rows2 = band_rows(dims, 0, blocks_dev, 2, roots, tiles, [c2], [z0[0]])
    z2 = totals(rows2, pair_col, n_pair, scale)
    z1, after = [], z2[0]
    for first, count in one:
        rows1 = band_rows(dims, first, count, 1, roots, tiles, [b1, to_even, to_odd], [after])
        z1.append(totals(rows1, pair_col, n_pair, scale))
        after = rows1
    out = jnp.concatenate([z0[1], jnp.concatenate([z[1] for z in z1], axis=1), z2[1]], axis=-1)
    return out[:, :, None]


def solution(mesh):
    return jax.shard_map(
        on_device,
        mesh=mesh,
        in_specs=(
            P(("grp", "aux"), "pair", None, None, None, None, None),
            P(("grp", "aux"), "pair", None, None, None),
            P(("grp", "aux"), "pair"),
            P("grp"),
            P("grp"),
            P("grp"),
        ),
        out_specs=P(None, None, ("grp", "aux"), "pair", None),
        check_vma=False,
    )
```

```python
import functools

import jax
import jax.numpy as jnp
from jax import lax
from jax.experimental import pallas as pl
from jax.experimental.pallas import tpu as pltpu
from jax.sharding import PartitionSpec as P

LIMIT = 61 << 20
COST = pl.CostEstimate(flops=1000, bytes_accessed=1000, transcendentals=0)
PARAMS = pltpu.CompilerParams(vmem_limit_bytes=LIMIT)
ANY = pl.BlockSpec(memory_space=pl.ANY)
HBM = pl.BlockSpec(memory_space=pltpu.HBM)
SMEM = pl.BlockSpec(memory_space=pltpu.SMEM)
VMEM = pl.BlockSpec(memory_space=pltpu.VMEM)
DMA = pltpu.SemaphoreType.DMA


def chunks_of(count, sizes):
    ends = [count * sum(sizes[: n + 1]) // sum(sizes) for n in range(len(sizes))]
    return [(a, b - a) for a, b in zip([0] + ends[:-1], ends)]


def dot(a, b):
    return lax.dot_general(a, b, (((1,), (1,)), ((), ())), preferred_element_type=jnp.float32)


def pack_kernel(plan, tiles, *refs):
    outs, held, sem_in, sem_out = refs[:-3], refs[-3], refs[-2], refs[-1]
    aux_pos = lax.axis_index("aux")
    blocks_dev = tiles.shape[0]
    loads, stores = [], []
    for out, parts in zip(outs, plan):
        rows = [(slot, back, first + i) for slot, back, first, count in parts for i in range(count)]
        for at, (slot, back, m) in enumerate(rows):
            n = len(loads)
            row = jnp.minimum(m + (aux_pos < back).astype(jnp.int32), blocks_dev - 1)
            loads.append(pltpu.make_async_copy(tiles.at[row, slot], held.at[n], sem_in.at[n]))
            stores.append(pltpu.make_async_copy(held.at[n], out.at[at], sem_out.at[n]))
    for load in loads:
        load.start()
    for load, store in zip(loads, stores):
        load.wait()
        store.start()
    for store in stores:
        store.wait()


def pack(tiles, plan):
    counts = [sum(part[3] for part in parts) for parts in plan]
    total = sum(counts)
    return pl.pallas_call(
        functools.partial(pack_kernel, plan),
        out_shape=[jax.ShapeDtypeStruct((count,) + tiles.shape[-2:], tiles.dtype) for count in counts],
        in_specs=[HBM],
        out_specs=[HBM] * len(counts),
        scratch_shapes=[pltpu.VMEM((total,) + tiles.shape[-2:], tiles.dtype), DMA((total,)), DMA((total,))],
        compiler_params=PARAMS,
        cost_estimate=COST,
    )(tiles)


def tie(arrays, after):
    return pl.pallas_call(
        lambda *refs: None,
        out_shape=[jax.ShapeDtypeStruct(array.shape, array.dtype) for array in arrays],
        in_specs=[HBM] * len(arrays) + [ANY] * len(after),
        out_specs=[HBM] * len(arrays),
        input_output_aliases={n: n for n in range(len(arrays))},
        compiler_params=PARAMS,
        cost_estimate=COST,
    )(*arrays, *after)


def root_row(band, freq_count, delta, slot, w):
    before = 0 if delta is None else band + sum(band - d for d in range(1, delta))
    return (before + slot) * freq_count + w


def root_rows(band, freq_count):
    rows = freq_count * (band + sum(band - d for d in range(1, band)))
    return -(-rows // 8) * 8


def first_kernel(dims, *refs):
    n_aux, n_pair, blocks_dev, band, freq_count = dims
    records = refs[:n_aux]
    occ, freq, table, own = refs[n_aux : n_aux + 4]
    out, roots, held, sem = refs[-4:]
    pair_rows = own.shape[-1]
    virt_blocks = table.shape[1] // pair_rows
    aux_pos, pair_col = lax.axis_index("aux"), lax.axis_index("pair")
    loads = [pltpu.make_async_copy(own.at[m], held.at[m], sem.at[m]) for m in range(blocks_dev)]
    for load in loads:
        load.start()

    def of_region(region):
        live = records[0][blocks_dev * band]
        for k in range(1, n_aux):
            live = jnp.where(lax.rem(aux_pos - region + n_aux, n_aux) == k, records[k][blocks_dev * band], live)
        return live

    masked = {}
    for m in range(blocks_dev):
        block = m * n_aux + aux_pos
        for slot in range(band):
            centre = block - slot
            safe = jnp.maximum(centre, 0)
            region = safe // blocks_dev
            number = lax.rem(safe, blocks_dev)
            pair_block = (region * n_pair + pair_col) * blocks_dev + number
            start = pl.multiple_of(lax.rem(pair_block, virt_blocks) * pair_rows, pair_rows)
            gap = table[:, pl.ds(start, pair_rows)] - occ[pair_block // virt_blocks]
            alive = (centre >= 0) & (number < of_region(region)) & (records[0][m * band + slot] > 0)
            for w in range(freq_count):
                omega = freq[w]
                root = jnp.sqrt(2.0 * gap / (gap * gap + omega * omega))
                roots[m, pl.ds(root_row(band, freq_count, None, slot, w), 1), :] = root
                masked[m, slot, w] = root * alive.astype(jnp.float32)
                for delta in range(1, band - slot):
                    there = m + ((aux_pos + delta) >= n_aux).astype(jnp.int32)
                    row = jnp.minimum(there, blocks_dev - 1) * band + slot + delta
                    both = alive & (there < blocks_dev) & (records[(n_aux - delta) % n_aux][row] > 0)
                    spot = root_row(band, freq_count, delta, slot, w)
                    roots[m, pl.ds(spot, 1), :] = root * both.astype(jnp.float32)
    for load in loads:
        load.wait()
    for m in range(blocks_dev):
        for w in range(freq_count):
            total = None
            for slot in range(band):
                a = (held[m, slot].astype(jnp.float32) * masked[m, slot, w]).astype(jnp.bfloat16)
                term = dot(a, a)
                total = term if total is None else total + term
            out[w, m] = total


def first_rows(dims, records, occ, freq, table, tiles, after):
    n_aux, n_pair, blocks_dev, band, freq_count = dims
    aux_rows, pair_rows = tiles.shape[-2:]
    return pl.pallas_call(
        functools.partial(first_kernel, dims),
        out_shape=[
            jax.ShapeDtypeStruct((freq_count, blocks_dev, aux_rows, aux_rows), jnp.float32),
            jax.ShapeDtypeStruct((blocks_dev, root_rows(band, freq_count), pair_rows), jnp.float32),
        ],
        in_specs=[SMEM] * (n_aux + 2) + [VMEM, HBM] + [ANY] * len(after),
        out_specs=[VMEM, VMEM],
        scratch_shapes=[pltpu.VMEM(tiles.shape, tiles.dtype), DMA((blocks_dev,))],
        compiler_params=PARAMS,
        cost_estimate=COST,
    )(*records, occ, freq, table, tiles, *after)


def pieces_of(arrays, first, count):
    parts, start = [], 0
    for n, array in enumerate(arrays):
        low, high = max(first, start), min(first + count, start + array.shape[0])
        if low < high:
            parts.append((n, low - start, low - first, high - low))
        start += array.shape[0]
    return parts


def band_kernel(dims, first, delta, slots, groups, add, roots, own, *refs):
    n_aux, n_pair, blocks_dev, band, freq_count = dims
    out, held, held_far, sem, sem_far = refs[-5:]
    count = out.shape[1]
    low, high = min(slots), max(slots) + 1
    copies = [
        pltpu.make_async_copy(own.at[first + i, pl.ds(low, high - low)], held.at[i], sem.at[i])
        for i in range(count)
    ]
    for s, group in enumerate(groups):
        for k, (n, at, to, length) in enumerate(group):
            copies.append(
                pltpu.make_async_copy(
                    refs[n].at[pl.ds(at, length)], held_far.at[s, pl.ds(to, length)], sem_far.at[s, k]
                )
            )
    for copy in copies:
        copy.start()
    for copy in copies:
        copy.wait()
    for i in range(count):
        m = first + i
        sums = [refs[add][w, i] if add is not None else None for w in range(freq_count)]
        for s, slot in enumerate(slots):
            left = held[i, slot - low].astype(jnp.float32)
            right = held_far[s, i].astype(jnp.float32)
            for w in range(freq_count):
                kept = roots[m, pl.ds(root_row(band, freq_count, delta, slot, w), 1), :]
                root = roots[m, pl.ds(root_row(band, freq_count, None, slot, w), 1), :]
                term = dot((left * kept).astype(jnp.bfloat16), (right * root).astype(jnp.bfloat16))
                sums[w] = term if sums[w] is None else sums[w] + term
        for w in range(freq_count):
            out[w, i] = sums[w]


def band_rows(dims, first, count, delta, slots, roots, tiles, far, after, add=None):
    n_aux, n_pair, blocks_dev, band, freq_count = dims
    aux_rows, pair_rows = tiles.shape[-2:]
    groups, arrays = [], []
    for group, offset in far:
        parts = pieces_of(group, first + offset, count)
        groups.append([(len(arrays) + n, low, to, length) for n, low, to, length in parts])
        arrays += group
    extra = [] if add is None else [add]
    spot = None if add is None else len(arrays)
    return pl.pallas_call(
        functools.partial(band_kernel, dims, first, delta, slots, groups, spot),
        out_shape=jax.ShapeDtypeStruct((freq_count, count, aux_rows, aux_rows), jnp.float32),
        in_specs=[VMEM, HBM] + [HBM] * len(arrays) + [VMEM] * len(extra) + [ANY] * len(after),
        out_specs=VMEM,
        scratch_shapes=[
            pltpu.VMEM((count, max(slots) + 1 - min(slots), aux_rows, pair_rows), tiles.dtype),
            pltpu.VMEM((len(slots), count, aux_rows, pair_rows), tiles.dtype),
            DMA((count,)),
            DMA((len(slots), max(len(group) for group in groups))),
        ],
        compiler_params=PARAMS,
        cost_estimate=COST,
    )(roots, tiles, *arrays, *extra, *after)


def halve(keep, pair_col, step, n_pair, rings, scale):
    freq_count, count, shares, height, width = keep.shape
    keep = keep.reshape(freq_count, count, shares // 2, 2, height, width)
    bit = (pair_col // step) & 1
    part = lax.dynamic_index_in_dim(keep, 1 - bit, 3, keepdims=False)
    mine = lax.dynamic_index_in_dim(keep, bit, 3, keepdims=False)
    sent = (part * scale).astype(jnp.float16)
    pairs = [(ring * n_pair + s, ring * n_pair + (s ^ step)) for ring in rings for s in range(n_pair)]
    got = lax.ppermute(sent, ("aux", "pair"), pairs)
    return mine + got.astype(jnp.float32) * (1.0 / scale), got


def totals(rows, pair_col, n_pair, rings, scale):
    freq_count, count, aux_rows, width = rows.shape
    keep = rows.reshape(freq_count, count, n_pair, aux_rows // n_pair, width)
    stages, step = [], 1
    while step < n_pair:
        keep, got = halve(keep, pair_col, step, n_pair, rings, scale)
        stages.append(got[0, 0, 0].astype(jnp.float32))
        step *= 2
    return stages[0], keep[:, :, 0]


def on_device(three_centre, locality, live_blocks, occ_energy, virt_energy, frequencies):
    n_aux = lax.axis_size("aux")
    n_pair = lax.axis_size("pair")
    pair_col = lax.axis_index("pair").astype(jnp.uint32).astype(jnp.int32)
    tiles = three_centre[0, 0, :, :, 0]
    blocks_dev, band, aux_rows, pair_rows = tiles.shape
    freq_count = frequencies.shape[0]
    dims = (n_aux, n_pair, blocks_dev, band, freq_count)
    scale = 128.0 / n_pair
    record = jnp.concatenate([locality[0, 0].reshape(-1), live_blocks[0]])
    records = [record] + [
        lax.ppermute(record, "aux", [(s, (s + k) % n_aux) for s in range(n_aux)]) for k in range(1, n_aux)
    ]
    two = chunks_of(blocks_dev, (4, 4))
    whole = list(range(n_aux))
    evens, odds = whole[::2], whole[1::2]
    plan = [[(2, 2, first, count)] for first, count in two] + [[(1, 1, 0, blocks_dev)]]
    plan.append([(1, 0, 0, blocks_dev), (2, 0, 0, blocks_dev)])
    *to_two, to_one, lower = tie(pack(tiles, plan), records[1:])
    c2 = [lax.ppermute(p, "aux", [(s, (s - 2) % n_aux) for s in whole]) for p in to_two]
    b1 = lax.ppermute(to_one, "aux", [(s, (s - 1) % n_aux) for s in evens])
    to_even = lax.ppermute(lower, "aux", [(s, s - 1) for s in odds])
    table = virt_energy.reshape(1, -1)
    rows0, roots = first_rows(dims, records, occ_energy, frequencies, table, tiles, to_two[:1])

    def rows_of(delta, slots, far, after, add=None):
        return band_rows(dims, 0, blocks_dev, delta, slots, roots, tiles, far, after, add)

    z0 = totals(rows0, pair_col, n_pair, whole, scale)
    rows_even = rows_of(1, [0, 1], [([to_even], 0), ([to_even], blocks_dev)], [rows0])
    z_even = totals(rows_even, pair_col, n_pair, evens, scale)
    rows2 = rows_of(2, [0], [(c2, 0)], [z0[0], z_even[0]])
    z2 = totals(rows2, pair_col, n_pair, whole, scale)
    to_odd = [lax.ppermute(c, "aux", [(s, s + 1) for s in evens]) for c in tie(c2, [rows2])]
    part = rows_of(1, [1], [(to_odd, 0)], [rows2])
    rows_odd = rows_of(1, [0], [([b1], 0)], [z2[0]], part)
    z_odd = totals(rows_odd, pair_col, n_pair, odds, scale)
    even = lax.axis_index("aux") % 2 == 0
    out = jnp.concatenate([z0[1], jnp.where(even, z_even[1], z_odd[1]), z2[1]], axis=-1)
    return out[:, :, None]


def solution(mesh):
    return jax.shard_map(
        on_device,
        mesh=mesh,
        in_specs=(
            P(("grp", "aux"), "pair", None, None, None, None, None),
            P(("grp", "aux"), "pair", None, None, None),
            P(("grp", "aux"), "pair"),
            P("grp"),
            P("grp"),
            P("grp"),
        ),
        out_specs=P(None, None, ("grp", "aux"), "pair", None),
        check_vma=False,
    )
```

```python
import functools

import jax
import jax.numpy as jnp
from jax import lax
from jax.experimental import pallas as pl
from jax.experimental.pallas import tpu as pltpu
from jax.sharding import PartitionSpec as P

LIMIT = 16 << 20
COST = pl.CostEstimate(flops=1000, bytes_accessed=1000, transcendentals=0)
PARAMS = pltpu.CompilerParams(vmem_limit_bytes=LIMIT)
ANY = pl.BlockSpec(memory_space=pl.ANY)
HBM = pl.BlockSpec(memory_space=pltpu.HBM)
SMEM = pl.BlockSpec(memory_space=pltpu.SMEM)
VMEM = pl.BlockSpec(memory_space=pltpu.VMEM)
DMA = pltpu.SemaphoreType.DMA


def chunks_of(count, sizes):
    ends = [count * sum(sizes[: n + 1]) // sum(sizes) for n in range(len(sizes))]
    return [(a, b - a) for a, b in zip([0] + ends[:-1], ends)]


def dot(a, b):
    return lax.dot_general(a, b, (((1,), (1,)), ((), ())), preferred_element_type=jnp.float32)


def pack_kernel(plan, tiles, *refs):
    blocks_dev, band = tiles.shape[:2]
    own, outs, sem_in, sem_out = refs[:band], refs[band:-2], refs[-2], refs[-1]
    aux_pos = lax.axis_index("aux")
    loads = {
        slot: [
            pltpu.make_async_copy(tiles.at[m, slot], own[slot].at[m], sem_in.at[slot, m]) for m in range(blocks_dev)
        ]
        for slot in range(band)
    }
    for slot in reversed(range(band)):
        for load in loads[slot]:
            load.start()
    stores = []
    ready = set()
    for out, (slot, back, first, count) in zip(outs, plan):
        if slot not in ready:
            ready.add(slot)
            for load in loads[slot]:
                load.wait()
        for i in range(count):
            row = jnp.minimum(first + i + (aux_pos < back).astype(jnp.int32), blocks_dev - 1)
            store = pltpu.make_async_copy(own[slot].at[row], out.at[i], sem_out.at[len(stores)])
            store.start()
            stores.append(store)
    for slot in range(band):
        if slot not in ready:
            for load in loads[slot]:
                load.wait()
    for store in stores:
        store.wait()


def pack(tiles, plan):
    counts = [part[3] for part in plan]
    blocks_dev, band, aux_rows, pair_rows = tiles.shape
    return pl.pallas_call(
        functools.partial(pack_kernel, plan),
        out_shape=[
            jax.ShapeDtypeStruct((count, aux_rows, pair_rows), tiles.dtype)
            for count in [blocks_dev] * band + counts
        ],
        in_specs=[ANY],
        out_specs=[VMEM] * band + [ANY] * len(counts),
        scratch_shapes=[DMA((band, blocks_dev)), DMA((sum(counts),))],
        compiler_params=PARAMS,
        cost_estimate=COST,
    )(tiles)


def tie(arrays, after):
    return pl.pallas_call(
        lambda *refs: None,
        out_shape=[jax.ShapeDtypeStruct(array.shape, array.dtype) for array in arrays],
        in_specs=[ANY] * (len(arrays) + len(after)),
        out_specs=[ANY] * len(arrays),
        input_output_aliases={n: n for n in range(len(arrays))},
        compiler_params=PARAMS,
        cost_estimate=COST,
    )(*arrays, *after)


def root_row(band, freq_count, delta, slot, w):
    before = 0 if delta is None else band + sum(band - d for d in range(1, delta))
    return (before + slot) * freq_count + w


def root_rows(band, freq_count):
    rows = freq_count * (band + sum(band - d for d in range(1, band)))
    return -(-rows // 8) * 8


def first_kernel(dims, *refs):
    n_aux, n_pair, blocks_dev, band, freq_count = dims
    records = refs[:n_aux]
    occ, freq, table = refs[n_aux : n_aux + 3]
    own = refs[n_aux + 3 : n_aux + 3 + band]
    out, roots = refs[-2:]
    pair_rows = own[0].shape[-1]
    virt_blocks = table.shape[1] // pair_rows
    aux_pos, pair_col = lax.axis_index("aux"), lax.axis_index("pair")

    def of_region(region):
        live = records[0][blocks_dev * band]
        for k in range(1, n_aux):
            live = jnp.where(lax.rem(aux_pos - region + n_aux, n_aux) == k, records[k][blocks_dev * band], live)
        return live

    masked = {}
    for m in range(blocks_dev):
        block = m * n_aux + aux_pos
        for slot in range(band):
            centre = block - slot
            safe = jnp.maximum(centre, 0)
            region = safe // blocks_dev
            number = lax.rem(safe, blocks_dev)
            pair_block = (region * n_pair + pair_col) * blocks_dev + number
            start = pl.multiple_of(lax.rem(pair_block, virt_blocks) * pair_rows, pair_rows)
            gap = table[:, pl.ds(start, pair_rows)] - occ[pair_block // virt_blocks]
            alive = (centre >= 0) & (number < of_region(region)) & (records[0][m * band + slot] > 0)
            for w in range(freq_count):
                omega = freq[w]
                root = jnp.sqrt(2.0 * gap / (gap * gap + omega * omega))
                roots[m, pl.ds(root_row(band, freq_count, None, slot, w), 1), :] = root
                masked[m, slot, w] = root * alive.astype(jnp.float32)
                for delta in range(1, band - slot):
                    there = m + ((aux_pos + delta) >= n_aux).astype(jnp.int32)
                    row = jnp.minimum(there, blocks_dev - 1) * band + slot + delta
                    both = alive & (there < blocks_dev) & (records[(n_aux - delta) % n_aux][row] > 0)
                    spot = root_row(band, freq_count, delta, slot, w)
                    roots[m, pl.ds(spot, 1), :] = root * both.astype(jnp.float32)
    for m in range(blocks_dev):
        for w in range(freq_count):
            total = None
            for slot in range(band):
                a = (own[slot][m].astype(jnp.float32) * masked[m, slot, w]).astype(jnp.bfloat16)
                term = dot(a, a)
                total = term if total is None else total + term
            out[w, m] = total


def first_rows(dims, records, occ, freq, table, own, after):
    n_aux, n_pair, blocks_dev, band, freq_count = dims
    aux_rows, pair_rows = own[0].shape[-2:]
    return pl.pallas_call(
        functools.partial(first_kernel, dims),
        out_shape=[
            jax.ShapeDtypeStruct((freq_count, blocks_dev, aux_rows, aux_rows), jnp.float32),
            jax.ShapeDtypeStruct((blocks_dev, root_rows(band, freq_count), pair_rows), jnp.float32),
        ],
        in_specs=[SMEM] * (n_aux + 2) + [VMEM] * (1 + band) + [ANY] * len(after),
        out_specs=[VMEM, VMEM],
        compiler_params=PARAMS,
        cost_estimate=COST,
    )(*records, occ, freq, table, *own, *after)


def band_kernel(dims, delta, slots, rights, add, roots, *refs):
    n_aux, n_pair, blocks_dev, band, freq_count = dims
    out = refs[-1]
    for m in range(blocks_dev):
        sums = [refs[add][w, m] if add is not None else None for w in range(freq_count)]
        for s, slot in enumerate(slots):
            n, row = rights[s][m]
            left = refs[s][m].astype(jnp.float32)
            right = refs[n][row].astype(jnp.float32)
            for w in range(freq_count):
                kept = roots[m, pl.ds(root_row(band, freq_count, delta, slot, w), 1), :]
                root = roots[m, pl.ds(root_row(band, freq_count, None, slot, w), 1), :]
                term = dot((left * kept).astype(jnp.bfloat16), (right * root).astype(jnp.bfloat16))
                sums[w] = term if sums[w] is None else sums[w] + term
        for w in range(freq_count):
            out[w, m] = sums[w]


def band_rows(dims, delta, slots, roots, own, far, after, add=None):
    n_aux, n_pair, blocks_dev, band, freq_count = dims
    aux_rows = own[0].shape[-2]
    arrays = [own[slot] for slot in slots]
    rights = []
    for group in far:
        rights.append([(len(arrays) + n, row) for n, array in enumerate(group) for row in range(array.shape[0])])
        arrays += group
    spot = None if add is None else len(arrays)
    arrays += [] if add is None else [add]
    return pl.pallas_call(
        functools.partial(band_kernel, dims, delta, slots, rights, spot),
        out_shape=jax.ShapeDtypeStruct((freq_count, blocks_dev, aux_rows, aux_rows), jnp.float32),
        in_specs=[VMEM] * (1 + len(arrays)) + [ANY] * len(after),
        out_specs=VMEM,
        compiler_params=PARAMS,
        cost_estimate=COST,
    )(roots, *arrays, *after)


def halve(keep, pair_col, step, n_pair, rings, scale):
    freq_count, count, shares, height, width = keep.shape
    keep = keep.reshape(freq_count, count, shares // 2, 2, height, width)
    bit = (pair_col // step) & 1
    part = lax.dynamic_index_in_dim(keep, 1 - bit, 3, keepdims=False)
    mine = lax.dynamic_index_in_dim(keep, bit, 3, keepdims=False)
    sent = (part * scale).astype(jnp.float16)
    pairs = [(ring * n_pair + s, ring * n_pair + (s ^ step)) for ring in rings for s in range(n_pair)]
    got = lax.ppermute(sent, ("aux", "pair"), pairs)
    return mine + got.astype(jnp.float32) * (1.0 / scale), got


def totals(rows, pair_col, n_pair, rings, scale):
    freq_count, count, aux_rows, width = rows.shape
    keep = rows.reshape(freq_count, count, n_pair, aux_rows // n_pair, width)
    stages, step = [], 1
    while step < n_pair:
        keep, got = halve(keep, pair_col, step, n_pair, rings, scale)
        stages.append(got[0, 0, 0].astype(jnp.float32))
        step *= 2
    return stages[0], keep[:, :, 0]


def on_device(three_centre, locality, live_blocks, occ_energy, virt_energy, frequencies):
    n_aux = lax.axis_size("aux")
    n_pair = lax.axis_size("pair")
    pair_col = lax.axis_index("pair").astype(jnp.uint32).astype(jnp.int32)
    tiles = three_centre[0, 0, :, :, 0]
    blocks_dev, band, aux_rows, pair_rows = tiles.shape
    freq_count = frequencies.shape[0]
    dims = (n_aux, n_pair, blocks_dev, band, freq_count)
    scale = 128.0 / n_pair
    record = jnp.concatenate([locality[0, 0].reshape(-1), live_blocks[0]])
    records = [record] + [
        lax.ppermute(record, "aux", [(s, (s + k) % n_aux) for s in range(n_aux)]) for k in range(1, n_aux)
    ]
    two = chunks_of(blocks_dev, (4, 4))
    whole = list(range(n_aux))
    evens, odds = whole[::2], whole[1::2]
    plan = [(2, 2, first, count) for first, count in two]
    plan += [(2, 0, 0, blocks_dev), (1, 1, 0, blocks_dev), (1, 0, 0, blocks_dev)]
    packed = pack(tiles, plan)
    own, packed = packed[:band], packed[band:]
    *to_two, lower2, to_one, lower1 = tie(packed, records[1:])
    c2 = [lax.ppermute(p, "aux", [(s, (s - 2) % n_aux) for s in whole]) for p in to_two]
    b1 = lax.ppermute(to_one, "aux", [(s, (s - 1) % n_aux) for s in evens])
    to_even = [lax.ppermute(p, "aux", [(s, s - 1) for s in odds]) for p in (lower1, lower2)]
    table = virt_energy.reshape(1, -1)
    rows0, roots = first_rows(dims, records, occ_energy, frequencies, table, own, to_two[:1])

    def rows_of(delta, slots, far, after, add=None):
        return band_rows(dims, delta, slots, roots, own, far, after, add)

    z0 = totals(rows0, pair_col, n_pair, whole, scale)
    rows_even = rows_of(1, [0, 1], [[p] for p in to_even], [rows0])
    z_even = totals(rows_even, pair_col, n_pair, evens, scale)
    rows2 = rows_of(2, [0], [c2], [z0[0], z_even[0]])
    z2 = totals(rows2, pair_col, n_pair, whole, scale)
    to_odd = [lax.ppermute(c, "aux", [(s, s + 1) for s in evens]) for c in tie(c2, [rows2])]
    part = rows_of(1, [1], [to_odd], [rows2])
    rows_odd = rows_of(1, [0], [[b1]], [z2[0]], part)
    z_odd = totals(rows_odd, pair_col, n_pair, odds, scale)
    even = lax.axis_index("aux") % 2 == 0
    out = jnp.concatenate([z0[1], jnp.where(even, z_even[1], z_odd[1]), z2[1]], axis=-1)
    return out[:, :, None]


def solution(mesh):
    return jax.shard_map(
        on_device,
        mesh=mesh,
        in_specs=(
            P(("grp", "aux"), "pair", None, None, None, None, None),
            P(("grp", "aux"), "pair", None, None, None),
            P(("grp", "aux"), "pair"),
            P("grp"),
            P("grp"),
            P("grp"),
        ),
        out_specs=P(None, None, ("grp", "aux"), "pair", None),
        check_vma=False,
    )
```

```python
import functools

import jax
import jax.numpy as jnp
from jax import lax
from jax.experimental import pallas as pl
from jax.experimental.pallas import tpu as pltpu
from jax.sharding import PartitionSpec as P

LIMIT = 16 << 20
SPLIT = (2, 6)
COST = pl.CostEstimate(flops=1000, bytes_accessed=1000, transcendentals=0)
PARAMS = pltpu.CompilerParams(vmem_limit_bytes=LIMIT)
ANY = pl.BlockSpec(memory_space=pl.ANY)
HBM = pl.BlockSpec(memory_space=pltpu.HBM)
SMEM = pl.BlockSpec(memory_space=pltpu.SMEM)
VMEM = pl.BlockSpec(memory_space=pltpu.VMEM)
DMA = pltpu.SemaphoreType.DMA


def chunks_of(count, sizes):
    ends = [count * sum(sizes[: n + 1]) // sum(sizes) for n in range(len(sizes))]
    return [(a, b - a) for a, b in zip([0] + ends[:-1], ends)]


def dot(a, b):
    return lax.dot_general(a, b, (((1,), (1,)), ((), ())), preferred_element_type=jnp.float32)


def pack_kernel(plan, tiles, first_slot, rest, *outs):
    blocks_dev, band = tiles.shape[:2]
    aux_pos = lax.axis_index("aux")
    for out, (slot, back, first, count) in zip(outs, plan):
        shift = (aux_pos < back).astype(jnp.int32)
        for i in range(count):
            out[i] = tiles[jnp.minimum(first + i + shift, blocks_dev - 1), slot]
    for m in range(blocks_dev):
        first_slot[m] = tiles[m, 0]
        for slot in range(1, band):
            rest[(slot - 1) * blocks_dev + m] = tiles[m, slot]


def pack(tiles, plan):
    blocks_dev, band, aux_rows, pair_rows = tiles.shape
    counts = [blocks_dev, (band - 1) * blocks_dev] + [part[3] for part in plan]
    return pl.pallas_call(
        functools.partial(pack_kernel, plan),
        out_shape=[jax.ShapeDtypeStruct((count, aux_rows, pair_rows), tiles.dtype) for count in counts],
        in_specs=[VMEM],
        out_specs=[VMEM] * len(counts),
        compiler_params=PARAMS,
        cost_estimate=COST,
    )(tiles)


def tie(arrays, after):
    return pl.pallas_call(
        lambda *refs: None,
        out_shape=[jax.ShapeDtypeStruct(array.shape, array.dtype) for array in arrays],
        in_specs=[ANY] * (len(arrays) + len(after)),
        out_specs=[ANY] * len(arrays),
        input_output_aliases={n: n for n in range(len(arrays))},
        compiler_params=PARAMS,
        cost_estimate=COST,
    )(*arrays, *after)


def root_row(band, freq_count, delta, slot, w):
    before = 0 if delta is None else band + sum(band - d for d in range(1, delta))
    return (before + slot) * freq_count + w


def root_rows(band, freq_count):
    rows = freq_count * (band + sum(band - d for d in range(1, band)))
    return -(-rows // 8) * 8


def own_tile(own, slot, m, blocks_dev):
    return own[0][m] if slot == 0 else own[1][(slot - 1) * blocks_dev + m]


def first_kernel(dims, *refs):
    n_aux, n_pair, blocks_dev, band, freq_count = dims
    records = refs[:n_aux]
    occ, freq, table = refs[n_aux : n_aux + 3]
    own = refs[n_aux + 3 : n_aux + 5]
    out, roots = refs[-2:]
    pair_rows = own[0].shape[-1]
    virt_blocks = table.shape[1] // pair_rows
    aux_pos, pair_col = lax.axis_index("aux"), lax.axis_index("pair")

    def of_region(region):
        live = records[0][blocks_dev * band]
        for k in range(1, n_aux):
            live = jnp.where(lax.rem(aux_pos - region + n_aux, n_aux) == k, records[k][blocks_dev * band], live)
        return live

    masked = {}
    for m in range(blocks_dev):
        block = m * n_aux + aux_pos
        for slot in range(band):
            centre = block - slot
            safe = jnp.maximum(centre, 0)
            region = safe // blocks_dev
            number = lax.rem(safe, blocks_dev)
            pair_block = (region * n_pair + pair_col) * blocks_dev + number
            start = pl.multiple_of(lax.rem(pair_block, virt_blocks) * pair_rows, pair_rows)
            gap = table[:, pl.ds(start, pair_rows)] - occ[pair_block // virt_blocks]
            alive = (centre >= 0) & (number < of_region(region)) & (records[0][m * band + slot] > 0)
            for w in range(freq_count):
                omega = freq[w]
                root = jnp.sqrt(2.0 * gap / (gap * gap + omega * omega))
                roots[m, pl.ds(root_row(band, freq_count, None, slot, w), 1), :] = root
                masked[m, slot, w] = root * alive.astype(jnp.float32)
                for delta in range(1, band - slot):
                    there = m + ((aux_pos + delta) >= n_aux).astype(jnp.int32)
                    row = jnp.minimum(there, blocks_dev - 1) * band + slot + delta
                    both = alive & (there < blocks_dev) & (records[(n_aux - delta) % n_aux][row] > 0)
                    spot = root_row(band, freq_count, delta, slot, w)
                    roots[m, pl.ds(spot, 1), :] = root * both.astype(jnp.float32)
    for m in range(blocks_dev):
        for w in range(freq_count):
            total = None
            for slot in range(band):
                a = (own_tile(own, slot, m, blocks_dev).astype(jnp.float32) * masked[m, slot, w]).astype(jnp.bfloat16)
                term = dot(a, a)
                total = term if total is None else total + term
            out[w, m] = total


def first_rows(dims, records, occ, freq, table, own, after):
    n_aux, n_pair, blocks_dev, band, freq_count = dims
    aux_rows, pair_rows = own[0].shape[-2:]
    return pl.pallas_call(
        functools.partial(first_kernel, dims),
        out_shape=[
            jax.ShapeDtypeStruct((freq_count, blocks_dev, aux_rows, aux_rows), jnp.float32),
            jax.ShapeDtypeStruct((blocks_dev, root_rows(band, freq_count), pair_rows), jnp.float32),
        ],
        in_specs=[SMEM] * (n_aux + 2) + [VMEM] * 3 + [ANY] * len(after),
        out_specs=[VMEM, VMEM],
        compiler_params=PARAMS,
        cost_estimate=COST,
    )(*records, occ, freq, table, *own, *after)


def band_kernel(dims, delta, slots, rights, add, roots, *refs):
    n_aux, n_pair, blocks_dev, band, freq_count = dims
    out = refs[-1]
    for m in range(blocks_dev):
        sums = [refs[add][w, m] if add is not None else None for w in range(freq_count)]
        for s, slot in enumerate(slots):
            n, row = rights[s][m]
            left = own_tile(refs, slot, m, blocks_dev).astype(jnp.float32)
            right = refs[n][row].astype(jnp.float32)
            for w in range(freq_count):
                kept = roots[m, pl.ds(root_row(band, freq_count, delta, slot, w), 1), :]
                root = roots[m, pl.ds(root_row(band, freq_count, None, slot, w), 1), :]
                term = dot((left * kept).astype(jnp.bfloat16), (right * root).astype(jnp.bfloat16))
                sums[w] = term if sums[w] is None else sums[w] + term
        for w in range(freq_count):
            out[w, m] = sums[w]


def band_rows(dims, delta, slots, roots, own, far, after, add=None):
    n_aux, n_pair, blocks_dev, band, freq_count = dims
    aux_rows = own[0].shape[-2]
    arrays = list(own)
    rights = []
    for group in far:
        rows = [(len(arrays) + n, row) for n, array in enumerate(group) for row in range(array.shape[0])]
        rights.append(rows[-blocks_dev:] if len(rights) > 0 else rows[:blocks_dev])
        arrays += group
    spot = None if add is None else len(arrays)
    arrays += [] if add is None else [add]
    return pl.pallas_call(
        functools.partial(band_kernel, dims, delta, slots, rights, spot),
        out_shape=jax.ShapeDtypeStruct((freq_count, blocks_dev, aux_rows, aux_rows), jnp.float32),
        in_specs=[VMEM] * (1 + len(arrays)) + [ANY] * len(after),
        out_specs=VMEM,
        compiler_params=PARAMS,
        cost_estimate=COST,
    )(roots, *arrays, *after)


def halve(keep, pair_col, step, n_pair, rings, scale):
    freq_count, count, shares, height, width = keep.shape
    keep = keep.reshape(freq_count, count, shares // 2, 2, height, width)
    bit = (pair_col // step) & 1
    part = lax.dynamic_index_in_dim(keep, 1 - bit, 3, keepdims=False)
    mine = lax.dynamic_index_in_dim(keep, bit, 3, keepdims=False)
    sent = (part * scale).astype(jnp.float16)
    pairs = [(ring * n_pair + s, ring * n_pair + (s ^ step)) for ring in rings for s in range(n_pair)]
    got = lax.ppermute(sent, ("aux", "pair"), pairs)
    return mine + got.astype(jnp.float32) * (1.0 / scale), got


def totals(rows, pair_col, n_pair, rings, scale):
    freq_count, count, aux_rows, width = rows.shape
    keep = rows.reshape(freq_count, count, n_pair, aux_rows // n_pair, width)
    stages, step = [], 1
    while step < n_pair:
        keep, got = halve(keep, pair_col, step, n_pair, rings, scale)
        stages.append(got[0, 0, 0].astype(jnp.float32))
        step *= 2
    return stages[0], keep[:, :, 0]


def on_device(three_centre, locality, live_blocks, occ_energy, virt_energy, frequencies):
    n_aux = lax.axis_size("aux")
    n_pair = lax.axis_size("pair")
    pair_col = lax.axis_index("pair").astype(jnp.uint32).astype(jnp.int32)
    tiles = three_centre[0, 0, :, :, 0]
    blocks_dev, band, aux_rows, pair_rows = tiles.shape
    freq_count = frequencies.shape[0]
    dims = (n_aux, n_pair, blocks_dev, band, freq_count)
    scale = 128.0 / n_pair
    record = jnp.concatenate([locality[0, 0].reshape(-1), live_blocks[0]])
    records = [record] + [
        lax.ppermute(record, "aux", [(s, (s + k) % n_aux) for s in range(n_aux)]) for k in range(1, n_aux)
    ]
    two = chunks_of(blocks_dev, SPLIT)
    whole = list(range(n_aux))
    evens, odds = whole[::2], whole[1::2]
    plan = [(2, 2, first, count) for first, count in two] + [(1, 1, 0, blocks_dev)]
    first_slot, rest, near_two, far_two, to_one = pack(tiles, plan)
    own = (first_slot, rest)
    down2 = [(s, (s - 2) % n_aux) for s in whole]
    c2 = [lax.ppermute(near_two, "aux", down2)]
    (far_two,) = tie([far_two], records[1:] + c2)
    c2.append(lax.ppermute(far_two, "aux", down2))
    b1 = lax.ppermute(to_one, "aux", [(s, (s - 1) % n_aux) for s in evens])
    to_even = lax.ppermute(rest, "aux", [(s, s - 1) for s in odds])
    table = virt_energy.reshape(1, -1)
    rows0, roots = first_rows(dims, records, occ_energy, frequencies, table, own, [far_two])

    def rows_of(delta, slots, far, after, add=None):
        return band_rows(dims, delta, slots, roots, own, far, after, add)

    z0 = totals(rows0, pair_col, n_pair, whole, scale)
    rows_even = rows_of(1, [0, 1], [[to_even], [to_even]], [rows0])
    z_even = totals(rows_even, pair_col, n_pair, evens, scale)
    rows2 = rows_of(2, [0], [c2], [z0[0], z_even[0]])
    z2 = totals(rows2, pair_col, n_pair, whole, scale)
    to_odd = [lax.ppermute(c, "aux", [(s, s + 1) for s in evens]) for c in tie(c2, [rows2])]
    part = rows_of(1, [1], [to_odd], [rows2])
    rows_odd = rows_of(1, [0], [[b1]], [z2[0]])
    z_odd = totals(rows_odd + part, pair_col, n_pair, odds, scale)
    even = lax.axis_index("aux") % 2 == 0
    out = jnp.concatenate([z0[1], jnp.where(even, z_even[1], z_odd[1]), z2[1]], axis=-1)
    return out[:, :, None]


def solution(mesh):
    return jax.shard_map(
        on_device,
        mesh=mesh,
        in_specs=(
            P(("grp", "aux"), "pair", None, None, None, None, None),
            P(("grp", "aux"), "pair", None, None, None),
            P(("grp", "aux"), "pair"),
            P("grp"),
            P("grp"),
            P("grp"),
        ),
        out_specs=P(None, None, ("grp", "aux"), "pair", None),
        check_vma=False,
    )
```

```python
import functools

import jax
import jax.numpy as jnp
from jax import lax
from jax.experimental import pallas as pl
from jax.experimental.pallas import tpu as pltpu
from jax.sharding import PartitionSpec as P

LIMIT = 16 << 20
SPLIT = (1, 7)
COST = pl.CostEstimate(flops=1000, bytes_accessed=1000, transcendentals=0)
PARAMS = pltpu.CompilerParams(vmem_limit_bytes=LIMIT)
ANY = pl.BlockSpec(memory_space=pl.ANY)
HBM = pl.BlockSpec(memory_space=pltpu.HBM)
SMEM = pl.BlockSpec(memory_space=pltpu.SMEM)
VMEM = pl.BlockSpec(memory_space=pltpu.VMEM)
DMA = pltpu.SemaphoreType.DMA


def chunks_of(count, sizes):
    ends = [count * sum(sizes[: n + 1]) // sum(sizes) for n in range(len(sizes))]
    return [(a, b - a) for a, b in zip([0] + ends[:-1], ends)]


def dot(a, b):
    return lax.dot_general(a, b, (((1,), (1,)), ((), ())), preferred_element_type=jnp.float32)


def pack_kernel(plan, tiles, first_slot, rest, *outs):
    blocks_dev, band = tiles.shape[:2]
    aux_pos = lax.axis_index("aux")
    for out, (slot, back, first, count) in zip(outs, plan):
        shift = (aux_pos < back).astype(jnp.int32)
        for i in range(count):
            out[i] = tiles[jnp.minimum(first + i + shift, blocks_dev - 1), slot]
    for m in range(blocks_dev):
        first_slot[m] = tiles[m, 0]
        for slot in range(1, band):
            rest[(slot - 1) * blocks_dev + m] = tiles[m, slot]


def pack(tiles, plan):
    blocks_dev, band, aux_rows, pair_rows = tiles.shape
    counts = [blocks_dev, (band - 1) * blocks_dev] + [part[3] for part in plan]
    return pl.pallas_call(
        functools.partial(pack_kernel, plan),
        out_shape=[jax.ShapeDtypeStruct((count, aux_rows, pair_rows), tiles.dtype) for count in counts],
        in_specs=[VMEM],
        out_specs=[VMEM] * len(counts),
        compiler_params=PARAMS,
        cost_estimate=COST,
    )(tiles)


def tie(arrays, after):
    return pl.pallas_call(
        lambda *refs: None,
        out_shape=[jax.ShapeDtypeStruct(array.shape, array.dtype) for array in arrays],
        in_specs=[ANY] * (len(arrays) + len(after)),
        out_specs=[ANY] * len(arrays),
        input_output_aliases={n: n for n in range(len(arrays))},
        compiler_params=PARAMS,
        cost_estimate=COST,
    )(*arrays, *after)


def root_row(band, freq_count, delta, slot, w):
    before = 0 if delta is None else band + sum(band - d for d in range(1, delta))
    return (before + slot) * freq_count + w


def root_rows(band, freq_count):
    rows = freq_count * (band + sum(band - d for d in range(1, band)))
    return -(-rows // 8) * 8


def own_tile(own, slot, m, blocks_dev):
    return own[0][m] if slot == 0 else own[1][(slot - 1) * blocks_dev + m]


def first_kernel(dims, *refs):
    n_aux, n_pair, blocks_dev, band, freq_count = dims
    records = refs[:n_aux]
    occ, freq, table = refs[n_aux : n_aux + 3]
    own, far = refs[n_aux + 3 : n_aux + 5], refs[n_aux + 5]
    out, roots = refs[-2:]
    pair_rows = own[0].shape[-1]
    virt_blocks = table.shape[1] // pair_rows
    aux_pos, pair_col = lax.axis_index("aux"), lax.axis_index("pair")

    def of_region(region):
        live = records[0][blocks_dev * band]
        for k in range(1, n_aux):
            live = jnp.where(lax.rem(aux_pos - region + n_aux, n_aux) == k, records[k][blocks_dev * band], live)
        return live

    masked, plain, one = {}, {}, {}
    for m in range(blocks_dev):
        block = m * n_aux + aux_pos
        for slot in range(band):
            centre = block - slot
            safe = jnp.maximum(centre, 0)
            region = safe // blocks_dev
            number = lax.rem(safe, blocks_dev)
            pair_block = (region * n_pair + pair_col) * blocks_dev + number
            start = pl.multiple_of(lax.rem(pair_block, virt_blocks) * pair_rows, pair_rows)
            gap = table[:, pl.ds(start, pair_rows)] - occ[pair_block // virt_blocks]
            alive = (centre >= 0) & (number < of_region(region)) & (records[0][m * band + slot] > 0)
            for w in range(freq_count):
                omega = freq[w]
                root = jnp.sqrt(2.0 * gap / (gap * gap + omega * omega))
                roots[m, pl.ds(root_row(band, freq_count, None, slot, w), 1), :] = root
                masked[m, slot, w] = root * alive.astype(jnp.float32)
                plain[m, slot, w] = root
                for delta in range(1, band - slot):
                    there = m + ((aux_pos + delta) >= n_aux).astype(jnp.int32)
                    row = jnp.minimum(there, blocks_dev - 1) * band + slot + delta
                    both = alive & (there < blocks_dev) & (records[(n_aux - delta) % n_aux][row] > 0)
                    spot = root_row(band, freq_count, delta, slot, w)
                    kept = root * both.astype(jnp.float32)
                    roots[m, pl.ds(spot, 1), :] = kept
                    if delta == 1:
                        one[m, slot, w] = kept
    for m in range(blocks_dev):
        for w in range(freq_count):
            total = None
            for slot in range(band):
                a = (own_tile(own, slot, m, blocks_dev).astype(jnp.float32) * masked[m, slot, w]).astype(jnp.bfloat16)
                term = dot(a, a)
                total = term if total is None else total + term
            out[w, m, :, : total.shape[1]] = total
            total = None
            for slot in range(band - 1):
                a = (own_tile(own, slot, m, blocks_dev).astype(jnp.float32) * one[m, slot, w]).astype(jnp.bfloat16)
                b = (far[slot * blocks_dev + m].astype(jnp.float32) * plain[m, slot, w]).astype(jnp.bfloat16)
                term = dot(a, b)
                total = term if total is None else total + term
            out[w, m, :, total.shape[1] :] = total


def first_rows(dims, records, occ, freq, table, own, far, after):
    n_aux, n_pair, blocks_dev, band, freq_count = dims
    aux_rows, pair_rows = own[0].shape[-2:]
    return pl.pallas_call(
        functools.partial(first_kernel, dims),
        out_shape=[
            jax.ShapeDtypeStruct((freq_count, blocks_dev, aux_rows, 2 * aux_rows), jnp.float32),
            jax.ShapeDtypeStruct((blocks_dev, root_rows(band, freq_count), pair_rows), jnp.float32),
        ],
        in_specs=[SMEM] * (n_aux + 2) + [VMEM] * 4 + [ANY] * len(after),
        out_specs=[VMEM, VMEM],
        compiler_params=PARAMS,
        cost_estimate=COST,
    )(*records, occ, freq, table, *own, far, *after)


def band_kernel(dims, delta, slots, rights, add, roots, *refs):
    n_aux, n_pair, blocks_dev, band, freq_count = dims
    out = refs[-1]
    for m in range(blocks_dev):
        sums = [refs[add][w, m] if add is not None else None for w in range(freq_count)]
        for s, slot in enumerate(slots):
            n, row = rights[s][m]
            left = own_tile(refs, slot, m, blocks_dev).astype(jnp.float32)
            right = refs[n][row].astype(jnp.float32)
            for w in range(freq_count):
                kept = roots[m, pl.ds(root_row(band, freq_count, delta, slot, w), 1), :]
                root = roots[m, pl.ds(root_row(band, freq_count, None, slot, w), 1), :]
                term = dot((left * kept).astype(jnp.bfloat16), (right * root).astype(jnp.bfloat16))
                sums[w] = term if sums[w] is None else sums[w] + term
        for w in range(freq_count):
            out[w, m] = sums[w]


def band_rows(dims, delta, slots, roots, own, far, after, add=None):
    n_aux, n_pair, blocks_dev, band, freq_count = dims
    aux_rows = own[0].shape[-2]
    arrays = list(own)
    rights = []
    for group in far:
        rows = [(len(arrays) + n, row) for n, array in enumerate(group) for row in range(array.shape[0])]
        rights.append(rows[-blocks_dev:] if len(rights) > 0 else rows[:blocks_dev])
        arrays += group
    spot = None if add is None else len(arrays)
    arrays += [] if add is None else [add]
    return pl.pallas_call(
        functools.partial(band_kernel, dims, delta, slots, rights, spot),
        out_shape=jax.ShapeDtypeStruct((freq_count, blocks_dev, aux_rows, aux_rows), jnp.float32),
        in_specs=[VMEM] * (1 + len(arrays)) + [ANY] * len(after),
        out_specs=VMEM,
        compiler_params=PARAMS,
        cost_estimate=COST,
    )(roots, *arrays, *after)


def halve(keep, pair_col, step, n_pair, rings, scale):
    freq_count, count, shares, height, width = keep.shape
    keep = keep.reshape(freq_count, count, shares // 2, 2, height, width)
    bit = lax.shift_right_logical(pair_col, jnp.uint32(step.bit_length() - 1)) & jnp.uint32(1)

    def pick(which):
        zero = jnp.uint32(0)
        sizes = (freq_count, count, shares // 2, 1, height, width)
        return lax.dynamic_slice(keep, [zero, zero, zero, which, zero, zero], sizes)[:, :, :, 0]

    part, mine = pick(bit ^ jnp.uint32(1)), pick(bit)
    sent = (part * scale).astype(jnp.float16)
    pairs = [(ring * n_pair + s, ring * n_pair + (s ^ step)) for ring in rings for s in range(n_pair)]
    got = lax.ppermute(sent, ("aux", "pair"), pairs)
    return mine + got.astype(jnp.float32) * (1.0 / scale), got


def totals(rows, pair_col, n_pair, rings, scale):
    freq_count, count, aux_rows, width = rows.shape
    keep = rows.reshape(freq_count, count, n_pair, aux_rows // n_pair, width)
    stages, step = [], 1
    while step < n_pair:
        keep, got = halve(keep, pair_col, step, n_pair, rings, scale)
        stages.append(got[0, 0, 0].astype(jnp.float32))
        step *= 2
    return stages[0], keep[:, :, 0]


def on_device(three_centre, locality, live_blocks, occ_energy, virt_energy, frequencies):
    n_aux = lax.axis_size("aux")
    n_pair = lax.axis_size("pair")
    pair_col = lax.axis_index("pair").astype(jnp.uint32)
    tiles = three_centre[0, 0, :, :, 0]
    blocks_dev, band, aux_rows, pair_rows = tiles.shape
    freq_count = frequencies.shape[0]
    dims = (n_aux, n_pair, blocks_dev, band, freq_count)
    scale = 128.0 / n_pair
    record = jnp.concatenate([locality[0, 0].reshape(-1), live_blocks[0]])
    records = [record] + [
        lax.ppermute(record, "aux", [(s, (s + k) % n_aux) for s in range(n_aux)]) for k in range(1, n_aux)
    ]
    two = chunks_of(blocks_dev, SPLIT)
    whole = list(range(n_aux))
    evens, odds = whole[::2], whole[1::2]
    plan = [(2, 2, first, count) for first, count in two] + [(1, 1, 0, blocks_dev)]
    first_slot, rest, near_two, far_two, to_one = pack(tiles, plan)
    own = (first_slot, rest)
    down2 = [(s, (s - 2) % n_aux) for s in whole]
    c2 = [lax.ppermute(near_two, "aux", down2)]
    (far_two,) = tie([far_two], records[1:] + c2)
    c2.append(lax.ppermute(far_two, "aux", down2))
    b1 = lax.ppermute(to_one, "aux", [(s, (s - 1) % n_aux) for s in evens])
    to_even = lax.ppermute(rest, "aux", [(s, s - 1) for s in odds])
    table = virt_energy.reshape(1, -1)
    rows0, roots = first_rows(dims, records, occ_energy, frequencies, table, own, to_even, [far_two])

    def rows_of(delta, slots, far, after, add=None):
        return band_rows(dims, delta, slots, roots, own, far, after, add)

    z0 = totals(rows0, pair_col, n_pair, whole, scale)
    rows2 = rows_of(2, [0], [c2], [z0[0]])
    z2 = totals(rows2, pair_col, n_pair, whole, scale)
    to_odd = [lax.ppermute(c, "aux", [(s, s + 1) for s in evens]) for c in tie(c2, [rows2])]
    part = rows_of(1, [1], [to_odd], [rows2])
    rows_odd = rows_of(1, [0], [[b1]], [z2[0]])
    z_odd = totals(rows_odd + part, pair_col, n_pair, odds, scale)
    even = lax.axis_index("aux").astype(jnp.uint32) & jnp.uint32(1) == 0
    one = jnp.where(even, z0[1][..., aux_rows:], z_odd[1])
    out = jnp.concatenate([z0[1][..., :aux_rows], one, z2[1]], axis=-1)
    return out[:, :, None]


def solution(mesh):
    return jax.shard_map(
        on_device,
        mesh=mesh,
        in_specs=(
            P(("grp", "aux"), "pair", None, None, None, None, None),
            P(("grp", "aux"), "pair", None, None, None),
            P(("grp", "aux"), "pair"),
            P("grp"),
            P("grp"),
            P("grp"),
        ),
        out_specs=P(None, None, ("grp", "aux"), "pair", None),
        check_vma=False,
    )
```

```python
import functools

import jax
import jax.numpy as jnp
from jax import lax
from jax.experimental import pallas as pl
from jax.experimental.pallas import tpu as pltpu
from jax.sharding import PartitionSpec as P

LIMIT = 16 << 20
SPLIT = (4, 4)
COST = pl.CostEstimate(flops=1000, bytes_accessed=1000, transcendentals=0)
PARAMS = pltpu.CompilerParams(vmem_limit_bytes=LIMIT)
ANY = pl.BlockSpec(memory_space=pl.ANY)
HBM = pl.BlockSpec(memory_space=pltpu.HBM)
SMEM = pl.BlockSpec(memory_space=pltpu.SMEM)
VMEM = pl.BlockSpec(memory_space=pltpu.VMEM)
DMA = pltpu.SemaphoreType.DMA


def chunks_of(count, sizes):
    ends = [count * sum(sizes[: n + 1]) // sum(sizes) for n in range(len(sizes))]
    return [(a, b - a) for a, b in zip([0] + ends[:-1], ends)]


def dot(a, b):
    return lax.dot_general(a, b, (((1,), (1,)), ((), ())), preferred_element_type=jnp.float32)


def pack_kernel(plan, tiles, first_slot, rest, *outs):
    blocks_dev, band = tiles.shape[:2]
    aux_pos = lax.axis_index("aux")
    for out, (slot, back, first, count) in zip(outs, plan):
        shift = (aux_pos < back).astype(jnp.int32)
        for i in range(count):
            out[i] = tiles[jnp.minimum(first + i + shift, blocks_dev - 1), slot]
    for m in range(blocks_dev):
        first_slot[m] = tiles[m, 0]
        for slot in range(1, band):
            rest[(slot - 1) * blocks_dev + m] = tiles[m, slot]


def pack(tiles, plan):
    blocks_dev, band, aux_rows, pair_rows = tiles.shape
    counts = [blocks_dev, (band - 1) * blocks_dev] + [part[3] for part in plan]
    return pl.pallas_call(
        functools.partial(pack_kernel, plan),
        out_shape=[jax.ShapeDtypeStruct((count, aux_rows, pair_rows), tiles.dtype) for count in counts],
        in_specs=[VMEM],
        out_specs=[VMEM] * len(counts),
        compiler_params=PARAMS,
        cost_estimate=COST,
    )(tiles)


def tie(arrays, after):
    return pl.pallas_call(
        lambda *refs: None,
        out_shape=[jax.ShapeDtypeStruct(array.shape, array.dtype) for array in arrays],
        in_specs=[ANY] * (len(arrays) + len(after)),
        out_specs=[ANY] * len(arrays),
        input_output_aliases={n: n for n in range(len(arrays))},
        compiler_params=PARAMS,
        cost_estimate=COST,
    )(*arrays, *after)


def root_row(band, freq_count, delta, slot, w):
    before = 0 if delta is None else band + sum(band - d for d in range(1, delta))
    return (before + slot) * freq_count + w


def root_rows(band, freq_count):
    rows = freq_count * (band + sum(band - d for d in range(1, band)))
    return -(-rows // 8) * 8


def own_tile(own, slot, m, blocks_dev):
    return own[0][m] if slot == 0 else own[1][(slot - 1) * blocks_dev + m]


def first_kernel(dims, *refs):
    n_aux, n_pair, blocks_dev, band, freq_count = dims
    records = refs[:n_aux]
    occ, freq, table = refs[n_aux : n_aux + 3]
    own, far = refs[n_aux + 3 : n_aux + 5], refs[n_aux + 5]
    out, out_one, roots = refs[-3:]
    pair_rows = own[0].shape[-1]
    virt_blocks = table.shape[1] // pair_rows
    aux_pos, pair_col = lax.axis_index("aux"), lax.axis_index("pair")

    def of_region(region):
        live = records[0][blocks_dev * band]
        for k in range(1, n_aux):
            live = jnp.where(lax.rem(aux_pos - region + n_aux, n_aux) == k, records[k][blocks_dev * band], live)
        return live

    masked, plain, one = {}, {}, {}
    for m in range(blocks_dev):
        block = m * n_aux + aux_pos
        for slot in range(band):
            centre = block - slot
            safe = jnp.maximum(centre, 0)
            region = safe // blocks_dev
            number = lax.rem(safe, blocks_dev)
            pair_block = (region * n_pair + pair_col) * blocks_dev + number
            start = pl.multiple_of(lax.rem(pair_block, virt_blocks) * pair_rows, pair_rows)
            gap = table[:, pl.ds(start, pair_rows)] - occ[pair_block // virt_blocks]
            alive = (centre >= 0) & (number < of_region(region)) & (records[0][m * band + slot] > 0)
            for w in range(freq_count):
                omega = freq[w]
                root = jnp.sqrt(2.0 * gap / (gap * gap + omega * omega))
                roots[m, pl.ds(root_row(band, freq_count, None, slot, w), 1), :] = root
                masked[m, slot, w] = root * alive.astype(jnp.float32)
                plain[m, slot, w] = root
                for delta in range(1, band - slot):
                    there = m + ((aux_pos + delta) >= n_aux).astype(jnp.int32)
                    row = jnp.minimum(there, blocks_dev - 1) * band + slot + delta
                    both = alive & (there < blocks_dev) & (records[(n_aux - delta) % n_aux][row] > 0)
                    spot = root_row(band, freq_count, delta, slot, w)
                    kept = root * both.astype(jnp.float32)
                    roots[m, pl.ds(spot, 1), :] = kept
                    if delta == 1:
                        one[m, slot, w] = kept
    for m in range(blocks_dev):
        for w in range(freq_count):
            total = None
            for slot in range(band):
                a = (own_tile(own, slot, m, blocks_dev).astype(jnp.float32) * masked[m, slot, w]).astype(jnp.bfloat16)
                term = dot(a, a)
                total = term if total is None else total + term
            out[w, m] = total
            total = None
            for slot in range(band - 1):
                a = (own_tile(own, slot, m, blocks_dev).astype(jnp.float32) * one[m, slot, w]).astype(jnp.bfloat16)
                b = (far[slot * blocks_dev + m].astype(jnp.float32) * plain[m, slot, w]).astype(jnp.bfloat16)
                term = dot(a, b)
                total = term if total is None else total + term
            out_one[w, m] = total


def first_rows(dims, records, occ, freq, table, own, far, after):
    n_aux, n_pair, blocks_dev, band, freq_count = dims
    aux_rows, pair_rows = own[0].shape[-2:]
    return pl.pallas_call(
        functools.partial(first_kernel, dims),
        out_shape=[
            jax.ShapeDtypeStruct((freq_count, blocks_dev, aux_rows, aux_rows), jnp.float32),
            jax.ShapeDtypeStruct((freq_count, blocks_dev, aux_rows, aux_rows), jnp.float32),
            jax.ShapeDtypeStruct((blocks_dev, root_rows(band, freq_count), pair_rows), jnp.float32),
        ],
        in_specs=[SMEM] * (n_aux + 2) + [VMEM] * 4 + [ANY] * len(after),
        out_specs=[VMEM, VMEM, VMEM],
        compiler_params=PARAMS,
        cost_estimate=COST,
    )(*records, occ, freq, table, *own, far, *after)


def band_kernel(dims, delta, slots, rights, add, roots, *refs):
    n_aux, n_pair, blocks_dev, band, freq_count = dims
    out = refs[-1]
    for m in range(blocks_dev):
        sums = [refs[add][w, m] if add is not None else None for w in range(freq_count)]
        for s, slot in enumerate(slots):
            n, row = rights[s][m]
            left = own_tile(refs, slot, m, blocks_dev).astype(jnp.float32)
            right = refs[n][row].astype(jnp.float32)
            for w in range(freq_count):
                kept = roots[m, pl.ds(root_row(band, freq_count, delta, slot, w), 1), :]
                root = roots[m, pl.ds(root_row(band, freq_count, None, slot, w), 1), :]
                term = dot((left * kept).astype(jnp.bfloat16), (right * root).astype(jnp.bfloat16))
                sums[w] = term if sums[w] is None else sums[w] + term
        for w in range(freq_count):
            out[w, m] = sums[w]


def band_rows(dims, delta, slots, roots, own, far, after, add=None):
    n_aux, n_pair, blocks_dev, band, freq_count = dims
    aux_rows = own[0].shape[-2]
    arrays = list(own)
    rights = []
    for group in far:
        rows = [(len(arrays) + n, row) for n, array in enumerate(group) for row in range(array.shape[0])]
        rights.append(rows[-blocks_dev:] if len(rights) > 0 else rows[:blocks_dev])
        arrays += group
    spot = None if add is None else len(arrays)
    arrays += [] if add is None else [add]
    return pl.pallas_call(
        functools.partial(band_kernel, dims, delta, slots, rights, spot),
        out_shape=jax.ShapeDtypeStruct((freq_count, blocks_dev, aux_rows, aux_rows), jnp.float32),
        in_specs=[VMEM] * (1 + len(arrays)) + [ANY] * len(after),
        out_specs=VMEM,
        compiler_params=PARAMS,
        cost_estimate=COST,
    )(roots, *arrays, *after)


def halve(keep, pair_col, step, n_pair, rings, scale):
    freq_count, count, shares, height, width = keep.shape
    keep = keep.reshape(freq_count, count, shares // 2, 2, height, width)
    bit = lax.shift_right_logical(pair_col, jnp.uint32(step.bit_length() - 1)) & jnp.uint32(1)

    def pick(which):
        zero = jnp.uint32(0)
        sizes = (freq_count, count, shares // 2, 1, height, width)
        return lax.dynamic_slice(keep, [zero, zero, zero, which, zero, zero], sizes)[:, :, :, 0]

    part, mine = pick(bit ^ jnp.uint32(1)), pick(bit)
    sent = (part * scale).astype(jnp.float16)
    pairs = [(ring * n_pair + s, ring * n_pair + (s ^ step)) for ring in rings for s in range(n_pair)]
    got = lax.ppermute(sent, ("aux", "pair"), pairs)
    return mine + got.astype(jnp.float32) * (1.0 / scale), got


def totals(rows, pair_col, n_pair, rings, scale):
    freq_count, count, aux_rows, width = rows.shape
    keep = rows.reshape(freq_count, count, n_pair, aux_rows // n_pair, width)
    stages, step = [], 1
    while step < n_pair:
        keep, got = halve(keep, pair_col, step, n_pair, rings, scale)
        stages.append(got[0, 0, 0].astype(jnp.float32))
        step *= 2
    return stages, keep[:, :, 0]


def on_device(three_centre, locality, live_blocks, occ_energy, virt_energy, frequencies):
    n_aux = lax.axis_size("aux")
    n_pair = lax.axis_size("pair")
    pair_col = lax.axis_index("pair").astype(jnp.uint32)
    tiles = three_centre[0, 0, :, :, 0]
    blocks_dev, band, aux_rows, pair_rows = tiles.shape
    freq_count = frequencies.shape[0]
    dims = (n_aux, n_pair, blocks_dev, band, freq_count)
    scale = 128.0 / n_pair
    record = jnp.concatenate([locality[0, 0].reshape(-1), live_blocks[0]])
    records = [record] + [
        lax.ppermute(record, "aux", [(s, (s + k) % n_aux) for s in range(n_aux)]) for k in range(1, n_aux)
    ]
    two = chunks_of(blocks_dev, SPLIT)
    whole = list(range(n_aux))
    evens, odds = whole[::2], whole[1::2]
    plan = [(2, 2, first, count) for first, count in two] + [(1, 1, 0, blocks_dev)]
    first_slot, rest, near_two, far_two, to_one = pack(tiles, plan)
    own = (first_slot, rest)
    down2 = [(s, (s - 2) % n_aux) for s in whole]
    c2 = [lax.ppermute(p, "aux", down2) for p in tie([near_two, far_two], records[1:])]
    to_even = lax.ppermute(rest, "aux", [(s, s - 1) for s in odds])
    table = virt_energy.reshape(1, -1)
    rows0, rows_even, roots = first_rows(dims, records, occ_energy, frequencies, table, own, to_even, [])

    def rows_of(delta, slots, far, after, add=None):
        return band_rows(dims, delta, slots, roots, own, far, after, add)

    b1 = lax.ppermute(tie([to_one], [roots])[0], "aux", [(s, (s - 1) % n_aux) for s in evens])
    bits0, z0 = totals(rows0, pair_col, n_pair, whole, scale)
    bits_even, z_even = totals(rows_even, pair_col, n_pair, evens, scale)
    rows2 = rows_of(2, [0], [c2], [bits0[-1], bits_even[-1]])
    bits2, z2 = totals(rows2, pair_col, n_pair, whole, scale)
    to_odd = [lax.ppermute(c, "aux", [(s, s + 1) for s in evens]) for c in tie(c2, [rows2])]
    part = rows_of(1, [1], [to_odd], [rows2])
    rows_odd = rows_of(1, [0], [[b1]], [bits2[0]], part)
    _, z_odd = totals(rows_odd, pair_col, n_pair, odds, scale)
    even = lax.axis_index("aux").astype(jnp.uint32) & jnp.uint32(1) == 0
    out = jnp.concatenate([z0, jnp.where(even, z_even, z_odd), z2], axis=-1)
    return out[:, :, None]


def solution(mesh):
    return jax.shard_map(
        on_device,
        mesh=mesh,
        in_specs=(
            P(("grp", "aux"), "pair", None, None, None, None, None),
            P(("grp", "aux"), "pair", None, None, None),
            P(("grp", "aux"), "pair"),
            P("grp"),
            P("grp"),
            P("grp"),
        ),
        out_specs=P(None, None, ("grp", "aux"), "pair", None),
        check_vma=False,
    )
```

```python
import functools

import jax
import jax.numpy as jnp
from jax import lax
from jax.experimental import pallas as pl
from jax.experimental.pallas import tpu as pltpu
from jax.sharding import PartitionSpec as P

LIMIT = 16 << 20
SPLIT = (1, 7)
COST = pl.CostEstimate(flops=1000, bytes_accessed=1000, transcendentals=0)
PARAMS = pltpu.CompilerParams(vmem_limit_bytes=LIMIT)
ANY = pl.BlockSpec(memory_space=pl.ANY)
HBM = pl.BlockSpec(memory_space=pltpu.HBM)
SMEM = pl.BlockSpec(memory_space=pltpu.SMEM)
VMEM = pl.BlockSpec(memory_space=pltpu.VMEM)
DMA = pltpu.SemaphoreType.DMA


def chunks_of(count, sizes):
    ends = [count * sum(sizes[: n + 1]) // sum(sizes) for n in range(len(sizes))]
    return [(a, b - a) for a, b in zip([0] + ends[:-1], ends)]


def dot(a, b):
    return lax.dot_general(a, b, (((1,), (1,)), ((), ())), preferred_element_type=jnp.float32)


def pack_kernel(plan, tiles, first_slot, rest, *outs):
    blocks_dev, band = tiles.shape[:2]
    aux_pos = lax.axis_index("aux")
    for out, (slot, back, first, count) in zip(outs, plan):
        shift = (aux_pos < back).astype(jnp.int32)
        for i in range(count):
            out[i] = tiles[jnp.minimum(first + i + shift, blocks_dev - 1), slot]
    for m in range(blocks_dev):
        first_slot[m] = tiles[m, 0]
        for slot in range(1, band):
            rest[(slot - 1) * blocks_dev + m] = tiles[m, slot]


def pack(tiles, plan):
    blocks_dev, band, aux_rows, pair_rows = tiles.shape
    counts = [blocks_dev, (band - 1) * blocks_dev] + [part[3] for part in plan]
    return pl.pallas_call(
        functools.partial(pack_kernel, plan),
        out_shape=[jax.ShapeDtypeStruct((count, aux_rows, pair_rows), tiles.dtype) for count in counts],
        in_specs=[VMEM],
        out_specs=[VMEM] * len(counts),
        compiler_params=PARAMS,
        cost_estimate=COST,
    )(tiles)


def tie(arrays, after):
    return pl.pallas_call(
        lambda *refs: None,
        out_shape=[jax.ShapeDtypeStruct(array.shape, array.dtype) for array in arrays],
        in_specs=[ANY] * (len(arrays) + len(after)),
        out_specs=[ANY] * len(arrays),
        input_output_aliases={n: n for n in range(len(arrays))},
        compiler_params=PARAMS,
        cost_estimate=COST,
    )(*arrays, *after)


def root_row(band, freq_count, delta, slot, w):
    before = 0 if delta is None else band + sum(band - d for d in range(1, delta))
    return (before + slot) * freq_count + w


def root_rows(band, freq_count):
    return -(-(root_row(band, freq_count, band, 0, 0) + freq_count) // 8) * 8


def own_tile(own, slot, m, blocks_dev):
    return own[0][m] if slot == 0 else own[1][(slot - 1) * blocks_dev + m]


def first_kernel(dims, *refs):
    n_aux, n_pair, blocks_dev, band, freq_count = dims
    records = refs[:n_aux]
    occ, freq, table = refs[n_aux : n_aux + 3]
    own, far = refs[n_aux + 3 : n_aux + 5], refs[n_aux + 5]
    out, out_one, roots = refs[-3:]
    pair_rows = own[0].shape[-1]
    virt_blocks = table.shape[1] // pair_rows
    aux_pos, pair_col = lax.axis_index("aux"), lax.axis_index("pair")

    def of_region(region):
        live = records[0][blocks_dev * band]
        for k in range(1, n_aux):
            live = jnp.where(lax.rem(aux_pos - region + n_aux, n_aux) == k, records[k][blocks_dev * band], live)
        return live

    masked, plain, one = {}, {}, {}
    for m in range(blocks_dev):
        block = m * n_aux + aux_pos
        for slot in range(band):
            centre = block - slot
            safe = jnp.maximum(centre, 0)
            region = safe // blocks_dev
            number = lax.rem(safe, blocks_dev)
            pair_block = (region * n_pair + pair_col) * blocks_dev + number
            start = pl.multiple_of(lax.rem(pair_block, virt_blocks) * pair_rows, pair_rows)
            gap = table[:, pl.ds(start, pair_rows)] - occ[pair_block // virt_blocks]
            alive = (centre >= 0) & (number < of_region(region)) & (records[0][m * band + slot] > 0)
            for w in range(freq_count):
                omega = freq[w]
                root = jnp.sqrt(2.0 * gap / (gap * gap + omega * omega))
                roots[m, pl.ds(root_row(band, freq_count, None, slot, w), 1), :] = root
                masked[m, slot, w] = root * alive.astype(jnp.float32)
                plain[m, slot, w] = root
                for delta in range(1, band - slot):
                    there = m + ((aux_pos + delta) >= n_aux).astype(jnp.int32)
                    row = jnp.minimum(there, blocks_dev - 1) * band + slot + delta
                    both = alive & (there < blocks_dev) & (records[(n_aux - delta) % n_aux][row] > 0)
                    spot = root_row(band, freq_count, delta, slot, w)
                    kept = root * both.astype(jnp.float32)
                    roots[m, pl.ds(spot, 1), :] = kept
                    if delta == 1:
                        one[m, slot, w] = kept
                if slot == 0:
                    there = m + ((aux_pos + 2) >= n_aux).astype(jnp.int32)
                    row = jnp.minimum(there, blocks_dev - 1) * band + 2
                    both = (centre >= 0) & (number < of_region(region)) & (there < blocks_dev)
                    both = both & (records[n_aux - 1][m * band + 1] > 0) & (records[n_aux - 2][row] > 0)
                    spot = root_row(band, freq_count, band, 0, w)
                    roots[m, pl.ds(spot, 1), :] = root * both.astype(jnp.float32)
    for m in range(blocks_dev):
        for w in range(freq_count):
            total = None
            for slot in range(band):
                a = (own_tile(own, slot, m, blocks_dev).astype(jnp.float32) * masked[m, slot, w]).astype(jnp.bfloat16)
                term = dot(a, a)
                total = term if total is None else total + term
            out[w, m] = total
            total = None
            for slot in range(band - 1):
                a = (own_tile(own, slot, m, blocks_dev).astype(jnp.float32) * one[m, slot, w]).astype(jnp.bfloat16)
                b = (far[slot * blocks_dev + m].astype(jnp.float32) * plain[m, slot, w]).astype(jnp.bfloat16)
                term = dot(a, b)
                total = term if total is None else total + term
            out_one[w, m] = total


def first_rows(dims, records, occ, freq, table, own, far, after):
    n_aux, n_pair, blocks_dev, band, freq_count = dims
    aux_rows, pair_rows = own[0].shape[-2:]
    return pl.pallas_call(
        functools.partial(first_kernel, dims),
        out_shape=[
            jax.ShapeDtypeStruct((freq_count, blocks_dev, aux_rows, aux_rows), jnp.float32),
            jax.ShapeDtypeStruct((freq_count, blocks_dev, aux_rows, aux_rows), jnp.float32),
            jax.ShapeDtypeStruct((blocks_dev, root_rows(band, freq_count), pair_rows), jnp.float32),
        ],
        in_specs=[SMEM] * (n_aux + 2) + [VMEM] * 4 + [ANY] * len(after),
        out_specs=[VMEM, VMEM, VMEM],
        compiler_params=PARAMS,
        cost_estimate=COST,
    )(*records, occ, freq, table, *own, far, *after)


def band_kernel(dims, delta, slots, rights, add, roots, *refs):
    n_aux, n_pair, blocks_dev, band, freq_count = dims
    out = refs[-1]
    for m in range(blocks_dev):
        sums = [refs[add][w, m] if add is not None else None for w in range(freq_count)]
        for s, slot in enumerate(slots):
            n, row = rights[s][m]
            left = own_tile(refs, slot, m, blocks_dev).astype(jnp.float32)
            right = refs[n][row].astype(jnp.float32)
            for w in range(freq_count):
                kept = roots[m, pl.ds(root_row(band, freq_count, delta, slot, w), 1), :]
                root = roots[m, pl.ds(root_row(band, freq_count, None, slot, w), 1), :]
                term = dot((left * kept).astype(jnp.bfloat16), (right * root).astype(jnp.bfloat16))
                sums[w] = term if sums[w] is None else sums[w] + term
        for w in range(freq_count):
            out[w, m] = sums[w]


def band_rows(dims, delta, slots, roots, own, far, after, add=None):
    n_aux, n_pair, blocks_dev, band, freq_count = dims
    aux_rows = own[0].shape[-2]
    arrays = list(own)
    rights = []
    for group in far:
        rows = [(len(arrays) + n, row) for n, array in enumerate(group) for row in range(array.shape[0])]
        rights.append(rows[-blocks_dev:] if len(rights) > 0 else rows[:blocks_dev])
        arrays += group
    spot = None if add is None else len(arrays)
    arrays += [] if add is None else [add]
    return pl.pallas_call(
        functools.partial(band_kernel, dims, delta, slots, rights, spot),
        out_shape=jax.ShapeDtypeStruct((freq_count, blocks_dev, aux_rows, aux_rows), jnp.float32),
        in_specs=[VMEM] * (1 + len(arrays)) + [ANY] * len(after),
        out_specs=VMEM,
        compiler_params=PARAMS,
        cost_estimate=COST,
    )(roots, *arrays, *after)


def second_kernel(dims, pieces, roots, own, lower, *refs):
    n_aux, n_pair, blocks_dev, band, freq_count = dims
    out, out_next = refs[-2:]
    for m in range(blocks_dev):
        n, row = pieces[m]
        left = own[m].astype(jnp.float32)
        right = refs[n][row].astype(jnp.float32)
        other = lower[m].astype(jnp.float32)
        for w in range(freq_count):
            kept = roots[m, pl.ds(root_row(band, freq_count, 2, 0, w), 1), :]
            root = roots[m, pl.ds(root_row(band, freq_count, None, 0, w), 1), :]
            next_kept = roots[m, pl.ds(root_row(band, freq_count, band, 0, w), 1), :]
            scaled = (right * root).astype(jnp.bfloat16)
            out[w, m] = dot((left * kept).astype(jnp.bfloat16), scaled)
            out_next[w, m] = dot((other * next_kept).astype(jnp.bfloat16), scaled)


def second_rows(dims, roots, own, lower, c2, after):
    n_aux, n_pair, blocks_dev, band, freq_count = dims
    aux_rows = own[0].shape[-2]
    pieces = [(n, row) for n, array in enumerate(c2) for row in range(array.shape[0])]
    return pl.pallas_call(
        functools.partial(second_kernel, dims, pieces),
        out_shape=[jax.ShapeDtypeStruct((freq_count, blocks_dev, aux_rows, aux_rows), jnp.float32)] * 2,
        in_specs=[VMEM] * (3 + len(c2)) + [ANY] * len(after),
        out_specs=[VMEM] * 2,
        compiler_params=PARAMS,
        cost_estimate=COST,
    )(roots, own[0], lower, *c2, *after)


def halve(keep, pair_col, step, n_pair, rings, scale):
    freq_count, count, shares, height, width = keep.shape
    keep = keep.reshape(freq_count, count, shares // 2, 2, height, width)
    bit = lax.shift_right_logical(pair_col, jnp.uint32(step.bit_length() - 1)) & jnp.uint32(1)

    def pick(which):
        zero = jnp.uint32(0)
        sizes = (freq_count, count, shares // 2, 1, height, width)
        return lax.dynamic_slice(keep, [zero, zero, zero, which, zero, zero], sizes)[:, :, :, 0]

    part, mine = pick(bit ^ jnp.uint32(1)), pick(bit)
    sent = (part * scale).astype(jnp.float16)
    pairs = [(ring * n_pair + s, ring * n_pair + (s ^ step)) for ring in rings for s in range(n_pair)]
    got = lax.ppermute(sent, ("aux", "pair"), pairs)
    return mine + got.astype(jnp.float32) * (1.0 / scale), got


def totals(rows, pair_col, n_pair, rings, scale):
    freq_count, count, aux_rows, width = rows.shape
    keep = rows.reshape(freq_count, count, n_pair, aux_rows // n_pair, width)
    stages, step = [], 1
    while step < n_pair:
        keep, got = halve(keep, pair_col, step, n_pair, rings, scale)
        stages.append(got[0, 0, 0].astype(jnp.float32))
        step *= 2
    return stages, keep[:, :, 0]


def on_device(three_centre, locality, live_blocks, occ_energy, virt_energy, frequencies):
    n_aux = lax.axis_size("aux")
    n_pair = lax.axis_size("pair")
    pair_col = lax.axis_index("pair").astype(jnp.uint32)
    tiles = three_centre[0, 0, :, :, 0]
    blocks_dev, band, aux_rows, pair_rows = tiles.shape
    freq_count = frequencies.shape[0]
    dims = (n_aux, n_pair, blocks_dev, band, freq_count)
    scale = 128.0 / n_pair
    record = jnp.concatenate([locality[0, 0].reshape(-1), live_blocks[0]])
    records = [record] + [
        lax.ppermute(record, "aux", [(s, (s + k) % n_aux) for s in range(n_aux)]) for k in range(1, n_aux)
    ]
    two = chunks_of(blocks_dev, SPLIT)
    whole = list(range(n_aux))
    evens, odds = whole[::2], whole[1::2]
    plan = [(2, 2, first, count) for first, count in two] + [(1, 1, 0, blocks_dev)]
    first_slot, rest, near_two, far_two, to_one = pack(tiles, plan)
    own = (first_slot, rest)
    down2 = [(s, (s - 2) % n_aux) for s in whole]
    c2 = [lax.ppermute(near_two, "aux", down2)]
    (far_two,) = tie([far_two], records[1:] + c2)
    c2.append(lax.ppermute(far_two, "aux", down2))
    to_even = lax.ppermute(rest, "aux", [(s, s - 1) for s in odds])
    table = virt_energy.reshape(1, -1)
    rows0, rows_even, roots = first_rows(dims, records, occ_energy, frequencies, table, own, to_even, [far_two])
    b1 = lax.ppermute(tie([to_one], [roots])[0], "aux", [(s, (s - 1) % n_aux) for s in evens])
    bits0, z0 = totals(rows0, pair_col, n_pair, whole, scale)
    bits_even, z_even = totals(rows_even, pair_col, n_pair, evens, scale)
    rows2, rows_next = second_rows(dims, roots, own, to_even, c2, [bits0[-1], bits_even[-1]])
    bits2, z2 = totals(rows2, pair_col, n_pair, whole, scale)
    term = lax.ppermute((rows_next * scale).astype(jnp.float16), "aux", [(s, s + 1) for s in evens])
    rows_odd = band_rows(dims, 1, [0], roots, own, [[b1]], [bits2[0]])
    rows_odd = rows_odd + term.astype(jnp.float32) * (1.0 / scale)
    _, z_odd = totals(rows_odd, pair_col, n_pair, odds, scale)
    even = lax.axis_index("aux").astype(jnp.uint32) & jnp.uint32(1) == 0
    out = jnp.concatenate([z0, jnp.where(even, z_even, z_odd), z2], axis=-1)
    return out[:, :, None]


def solution(mesh):
    return jax.shard_map(
        on_device,
        mesh=mesh,
        in_specs=(
            P(("grp", "aux"), "pair", None, None, None, None, None),
            P(("grp", "aux"), "pair", None, None, None),
            P(("grp", "aux"), "pair"),
            P("grp"),
            P("grp"),
            P("grp"),
        ),
        out_specs=P(None, None, ("grp", "aux"), "pair", None),
        check_vma=False,
    )
```

```python
import functools

import jax
import jax.numpy as jnp
from jax import lax
from jax.experimental import pallas as pl
from jax.experimental.pallas import tpu as pltpu
from jax.sharding import PartitionSpec as P

LIMIT = 16 << 20
SPLIT = (1, 7)
COST = pl.CostEstimate(flops=1000, bytes_accessed=1000, transcendentals=0)
PARAMS = pltpu.CompilerParams(vmem_limit_bytes=LIMIT)
ANY = pl.BlockSpec(memory_space=pl.ANY)
HBM = pl.BlockSpec(memory_space=pltpu.HBM)
SMEM = pl.BlockSpec(memory_space=pltpu.SMEM)
VMEM = pl.BlockSpec(memory_space=pltpu.VMEM)
DMA = pltpu.SemaphoreType.DMA


def chunks_of(count, sizes):
    ends = [count * sum(sizes[: n + 1]) // sum(sizes) for n in range(len(sizes))]
    return [(a, b - a) for a, b in zip([0] + ends[:-1], ends)]


def dot(a, b):
    return lax.dot_general(a, b, (((1,), (1,)), ((), ())), preferred_element_type=jnp.float32)


def pack_kernel(plan, tiles, first_slot, rest, *outs):
    blocks_dev, band = tiles.shape[:2]
    aux_pos = lax.axis_index("aux")
    for out, (slot, back, first, count) in zip(outs, plan):
        shift = (aux_pos < back).astype(jnp.int32)
        for i in range(count):
            out[i] = tiles[jnp.minimum(first + i + shift, blocks_dev - 1), slot]
    for m in range(blocks_dev):
        first_slot[m] = tiles[m, 0]
        for slot in range(1, band):
            rest[(slot - 1) * blocks_dev + m] = tiles[m, slot]


def pack(tiles, plan):
    blocks_dev, band, aux_rows, pair_rows = tiles.shape
    counts = [blocks_dev, (band - 1) * blocks_dev] + [part[3] for part in plan]
    return pl.pallas_call(
        functools.partial(pack_kernel, plan),
        out_shape=[jax.ShapeDtypeStruct((count, aux_rows, pair_rows), tiles.dtype) for count in counts],
        in_specs=[VMEM],
        out_specs=[VMEM] * len(counts),
        compiler_params=PARAMS,
        cost_estimate=COST,
    )(tiles)


def tie(arrays, after):
    return pl.pallas_call(
        lambda *refs: None,
        out_shape=[jax.ShapeDtypeStruct(array.shape, array.dtype) for array in arrays],
        in_specs=[ANY] * (len(arrays) + len(after)),
        out_specs=[ANY] * len(arrays),
        input_output_aliases={n: n for n in range(len(arrays))},
        compiler_params=PARAMS,
        cost_estimate=COST,
    )(*arrays, *after)


def root_row(band, freq_count, delta, slot, w):
    before = 0 if delta is None else band + sum(band - d for d in range(1, delta))
    return (before + slot) * freq_count + w


def root_rows(band, freq_count):
    return -(-(root_row(band, freq_count, band, 0, 0) + freq_count) // 8) * 8


def own_tile(own, slot, m, blocks_dev):
    return own[0][m] if slot == 0 else own[1][(slot - 1) * blocks_dev + m]


def first_kernel(dims, *refs):
    n_aux, n_pair, blocks_dev, band, freq_count = dims
    records = refs[:n_aux]
    occ, freq, table = refs[n_aux : n_aux + 3]
    own, far = refs[n_aux + 3 : n_aux + 5], refs[n_aux + 5]
    out, out_one, roots = refs[-3:]
    pair_rows = own[0].shape[-1]
    virt_blocks = table.shape[1] // pair_rows
    aux_pos, pair_col = lax.axis_index("aux"), lax.axis_index("pair")

    def of_region(region):
        live = records[0][blocks_dev * band]
        for k in range(1, n_aux):
            live = jnp.where(lax.rem(aux_pos - region + n_aux, n_aux) == k, records[k][blocks_dev * band], live)
        return live

    masked, plain, one = {}, {}, {}
    for m in range(blocks_dev):
        block = m * n_aux + aux_pos
        for slot in range(band):
            centre = block - slot
            safe = jnp.maximum(centre, 0)
            region = safe // blocks_dev
            number = lax.rem(safe, blocks_dev)
            pair_block = (region * n_pair + pair_col) * blocks_dev + number
            start = pl.multiple_of(lax.rem(pair_block, virt_blocks) * pair_rows, pair_rows)
            gap = table[:, pl.ds(start, pair_rows)] - occ[pair_block // virt_blocks]
            alive = (centre >= 0) & (number < of_region(region)) & (records[0][m * band + slot] > 0)
            for w in range(freq_count):
                omega = freq[w]
                root = jnp.sqrt(2.0 * gap / (gap * gap + omega * omega))
                roots[m, pl.ds(root_row(band, freq_count, None, slot, w), 1), :] = root
                masked[m, slot, w] = root * alive.astype(jnp.float32)
                plain[m, slot, w] = root
                for delta in range(1, band - slot):
                    there = m + ((aux_pos + delta) >= n_aux).astype(jnp.int32)
                    row = jnp.minimum(there, blocks_dev - 1) * band + slot + delta
                    both = alive & (there < blocks_dev) & (records[(n_aux - delta) % n_aux][row] > 0)
                    spot = root_row(band, freq_count, delta, slot, w)
                    kept = root * both.astype(jnp.float32)
                    roots[m, pl.ds(spot, 1), :] = kept
                    if delta == 1:
                        one[m, slot, w] = kept
                if slot == 0:
                    there = m + ((aux_pos + 2) >= n_aux).astype(jnp.int32)
                    row = jnp.minimum(there, blocks_dev - 1) * band + 2
                    both = (centre >= 0) & (number < of_region(region)) & (there < blocks_dev)
                    both = both & (records[n_aux - 1][m * band + 1] > 0) & (records[n_aux - 2][row] > 0)
                    spot = root_row(band, freq_count, band, 0, w)
                    roots[m, pl.ds(spot, 1), :] = root * both.astype(jnp.float32)
    for m in range(blocks_dev):
        for w in range(freq_count):
            total = None
            for slot in range(band):
                a = (own_tile(own, slot, m, blocks_dev).astype(jnp.float32) * masked[m, slot, w]).astype(jnp.bfloat16)
                term = dot(a, a)
                total = term if total is None else total + term
            out[w, m] = total
            total = None
            for slot in range(band - 1):
                a = (own_tile(own, slot, m, blocks_dev).astype(jnp.float32) * one[m, slot, w]).astype(jnp.bfloat16)
                b = (far[slot * blocks_dev + m].astype(jnp.float32) * plain[m, slot, w]).astype(jnp.bfloat16)
                term = dot(a, b)
                total = term if total is None else total + term
            out_one[w, m] = total


def first_rows(dims, records, occ, freq, table, own, far, after):
    n_aux, n_pair, blocks_dev, band, freq_count = dims
    aux_rows, pair_rows = own[0].shape[-2:]
    return pl.pallas_call(
        functools.partial(first_kernel, dims),
        out_shape=[
            jax.ShapeDtypeStruct((freq_count, blocks_dev, aux_rows, aux_rows), jnp.float32),
            jax.ShapeDtypeStruct((freq_count, blocks_dev, aux_rows, aux_rows), jnp.float32),
            jax.ShapeDtypeStruct((blocks_dev, root_rows(band, freq_count), pair_rows), jnp.float32),
        ],
        in_specs=[SMEM] * (n_aux + 2) + [VMEM] * 4 + [ANY] * len(after),
        out_specs=[VMEM, VMEM, VMEM],
        compiler_params=PARAMS,
        cost_estimate=COST,
    )(*records, occ, freq, table, *own, far, *after)


def band_kernel(dims, delta, slots, rights, add, roots, *refs):
    n_aux, n_pair, blocks_dev, band, freq_count = dims
    out = refs[-1]
    for m in range(blocks_dev):
        sums = [refs[add][w, m] if add is not None else None for w in range(freq_count)]
        for s, slot in enumerate(slots):
            n, row = rights[s][m]
            left = own_tile(refs, slot, m, blocks_dev).astype(jnp.float32)
            right = refs[n][row].astype(jnp.float32)
            for w in range(freq_count):
                kept = roots[m, pl.ds(root_row(band, freq_count, delta, slot, w), 1), :]
                root = roots[m, pl.ds(root_row(band, freq_count, None, slot, w), 1), :]
                term = dot((left * kept).astype(jnp.bfloat16), (right * root).astype(jnp.bfloat16))
                sums[w] = term if sums[w] is None else sums[w] + term
        for w in range(freq_count):
            out[w, m] = sums[w]


def band_rows(dims, delta, slots, roots, own, far, after, add=None):
    n_aux, n_pair, blocks_dev, band, freq_count = dims
    aux_rows = own[0].shape[-2]
    arrays = list(own)
    rights = []
    for group in far:
        rows = [(len(arrays) + n, row) for n, array in enumerate(group) for row in range(array.shape[0])]
        rights.append(rows[-blocks_dev:] if len(rights) > 0 else rows[:blocks_dev])
        arrays += group
    spot = None if add is None else len(arrays)
    arrays += [] if add is None else [add]
    return pl.pallas_call(
        functools.partial(band_kernel, dims, delta, slots, rights, spot),
        out_shape=jax.ShapeDtypeStruct((freq_count, blocks_dev, aux_rows, aux_rows), jnp.float32),
        in_specs=[VMEM] * (1 + len(arrays)) + [ANY] * len(after),
        out_specs=VMEM,
        compiler_params=PARAMS,
        cost_estimate=COST,
    )(roots, *arrays, *after)


def second_kernel(dims, pieces, roots, own, lower, *refs):
    n_aux, n_pair, blocks_dev, band, freq_count = dims
    out, out_next = refs[-2:]
    for m in range(blocks_dev):
        n, row = pieces[m]
        left = own[m].astype(jnp.float32)
        right = refs[n][row].astype(jnp.float32)
        other = lower[m].astype(jnp.float32)
        for w in range(freq_count):
            kept = roots[m, pl.ds(root_row(band, freq_count, 2, 0, w), 1), :]
            root = roots[m, pl.ds(root_row(band, freq_count, None, 0, w), 1), :]
            next_kept = roots[m, pl.ds(root_row(band, freq_count, band, 0, w), 1), :]
            scaled = (right * root).astype(jnp.bfloat16)
            out[w, m] = dot((left * kept).astype(jnp.bfloat16), scaled)
            out_next[w, m] = dot((other * next_kept).astype(jnp.bfloat16), scaled)


def second_rows(dims, roots, own, lower, c2, after):
    n_aux, n_pair, blocks_dev, band, freq_count = dims
    aux_rows = own[0].shape[-2]
    pieces = [(n, row) for n, array in enumerate(c2) for row in range(array.shape[0])]
    return pl.pallas_call(
        functools.partial(second_kernel, dims, pieces),
        out_shape=[jax.ShapeDtypeStruct((freq_count, blocks_dev, aux_rows, aux_rows), jnp.float32)] * 2,
        in_specs=[VMEM] * (3 + len(c2)) + [ANY] * len(after),
        out_specs=[VMEM] * 2,
        compiler_params=PARAMS,
        cost_estimate=COST,
    )(roots, own[0], lower, *c2, *after)


def halve(keep, pair_col, step, n_pair, rings, scale):
    freq_count, count, shares, height, width = keep.shape
    keep = keep.reshape(freq_count, count, shares // 2, 2, height, width)
    bit = lax.shift_right_logical(pair_col, jnp.uint32(step.bit_length() - 1)) & jnp.uint32(1)

    def pick(which):
        zero = jnp.uint32(0)
        sizes = (freq_count, count, shares // 2, 1, height, width)
        return lax.dynamic_slice(keep, [zero, zero, zero, which, zero, zero], sizes)[:, :, :, 0]

    part, mine = pick(bit ^ jnp.uint32(1)), pick(bit)
    sent = (part * scale).astype(jnp.float16)
    pairs = [(ring * n_pair + s, ring * n_pair + (s ^ step)) for ring in rings for s in range(n_pair)]
    got = lax.ppermute(sent, ("aux", "pair"), pairs)
    return mine + got.astype(jnp.float32) * (1.0 / scale), got


def totals(rows, pair_col, n_pair, rings, scale):
    freq_count, count, aux_rows, width = rows.shape
    keep = rows.reshape(freq_count, count, n_pair, aux_rows // n_pair, width)
    stages, step = [], 1
    while step < n_pair:
        keep, got = halve(keep, pair_col, step, n_pair, rings, scale)
        stages.append(got[0, 0, 0].astype(jnp.float32))
        step *= 2
    return stages, keep[:, :, 0]


def on_device(three_centre, locality, live_blocks, occ_energy, virt_energy, frequencies):
    n_aux = lax.axis_size("aux")
    n_pair = lax.axis_size("pair")
    pair_col = lax.axis_index("pair").astype(jnp.uint32)
    tiles = three_centre[0, 0, :, :, 0]
    blocks_dev, band, aux_rows, pair_rows = tiles.shape
    freq_count = frequencies.shape[0]
    dims = (n_aux, n_pair, blocks_dev, band, freq_count)
    scale = 128.0 / n_pair
    record = jnp.concatenate([locality[0, 0].reshape(-1), live_blocks[0]])
    records = [record] + [
        lax.ppermute(record, "aux", [(s, (s + k) % n_aux) for s in range(n_aux)]) for k in range(1, n_aux)
    ]
    two = chunks_of(blocks_dev, SPLIT)
    whole = list(range(n_aux))
    evens, odds = whole[::2], whole[1::2]
    plan = [(2, 2, first, count) for first, count in two] + [(1, 1, 0, blocks_dev)]
    first_slot, rest, near_two, far_two, to_one = pack(tiles, plan)
    own = (first_slot, rest)
    down2 = [(s, (s - 2) % n_aux) for s in whole]
    c2 = [lax.ppermute(near_two, "aux", down2)]
    (far_two,) = tie([far_two], records[1:] + c2)
    c2.append(lax.ppermute(far_two, "aux", down2))
    to_even = lax.ppermute(rest, "aux", [(s, s - 1) for s in odds])
    table = virt_energy.reshape(1, -1)
    rows0, rows_even, roots = first_rows(dims, records, occ_energy, frequencies, table, own, to_even, [far_two])
    b1 = lax.ppermute(tie([to_one], [roots])[0], "aux", [(s, (s - 1) % n_aux) for s in evens])
    bits0, z0 = totals(rows0, pair_col, n_pair, whole, scale)
    bits_even, z_even = totals(rows_even, pair_col, n_pair, evens, scale)
    rows2, rows_next = second_rows(dims, roots, own, to_even, c2, [bits_even[-1], bits0[-1]])
    bits2, z2 = totals(rows2, pair_col, n_pair, whole, scale)
    term = lax.ppermute((rows_next * scale).astype(jnp.float16), "aux", [(s, s + 1) for s in evens])
    rows_odd = band_rows(dims, 1, [0], roots, own, [[b1]], [rows2, z0])
    (rows_odd,) = tie([rows_odd], [bits2[0]])
    rows_odd = rows_odd + term.astype(jnp.float32) * (1.0 / scale)
    _, z_odd = totals(rows_odd, pair_col, n_pair, odds, scale)
    even = lax.axis_index("aux").astype(jnp.uint32) & jnp.uint32(1) == 0
    out = jnp.concatenate([z0, jnp.where(even, z_even, z_odd), z2], axis=-1)
    return out[:, :, None]


def solution(mesh):
    return jax.shard_map(
        on_device,
        mesh=mesh,
        in_specs=(
            P(("grp", "aux"), "pair", None, None, None, None, None),
            P(("grp", "aux"), "pair", None, None, None),
            P(("grp", "aux"), "pair"),
            P("grp"),
            P("grp"),
            P("grp"),
        ),
        out_specs=P(None, None, ("grp", "aux"), "pair", None),
        check_vma=False,
    )
```

```python
import functools

import jax
import jax.numpy as jnp
from jax import lax
from jax.experimental import pallas as pl
from jax.experimental.pallas import tpu as pltpu
from jax.sharding import PartitionSpec as P

LIMIT = 16 << 20
SPLIT = (1, 7)
COST = pl.CostEstimate(flops=1000, bytes_accessed=1000, transcendentals=0)
PARAMS = pltpu.CompilerParams(vmem_limit_bytes=LIMIT)
ANY = pl.BlockSpec(memory_space=pl.ANY)
HBM = pl.BlockSpec(memory_space=pltpu.HBM)
SMEM = pl.BlockSpec(memory_space=pltpu.SMEM)
VMEM = pl.BlockSpec(memory_space=pltpu.VMEM)
DMA = pltpu.SemaphoreType.DMA


def chunks_of(count, sizes):
    ends = [count * sum(sizes[: n + 1]) // sum(sizes) for n in range(len(sizes))]
    return [(a, b - a) for a, b in zip([0] + ends[:-1], ends)]


def dot(a, b):
    return lax.dot_general(a, b, (((1,), (1,)), ((), ())), preferred_element_type=jnp.float32)


def pack_kernel(plan, tiles, first_slot, rest, *outs):
    blocks_dev, band = tiles.shape[:2]
    aux_pos = lax.axis_index("aux")
    for out, (slot, back, first, count) in zip(outs, plan):
        shift = (aux_pos < back).astype(jnp.int32)
        for i in range(count):
            out[i] = tiles[jnp.minimum(first + i + shift, blocks_dev - 1), slot]
    for m in range(blocks_dev):
        first_slot[m] = tiles[m, 0]
        for slot in range(1, band):
            rest[(slot - 1) * blocks_dev + m] = tiles[m, slot]


def pack(tiles, plan):
    blocks_dev, band, aux_rows, pair_rows = tiles.shape
    counts = [blocks_dev, (band - 1) * blocks_dev] + [part[3] for part in plan]
    return pl.pallas_call(
        functools.partial(pack_kernel, plan),
        out_shape=[jax.ShapeDtypeStruct((count, aux_rows, pair_rows), tiles.dtype) for count in counts],
        in_specs=[VMEM],
        out_specs=[VMEM] * len(counts),
        compiler_params=PARAMS,
        cost_estimate=COST,
    )(tiles)


def tie(arrays, after):
    return pl.pallas_call(
        lambda *refs: None,
        out_shape=[jax.ShapeDtypeStruct(array.shape, array.dtype) for array in arrays],
        in_specs=[ANY] * (len(arrays) + len(after)),
        out_specs=[ANY] * len(arrays),
        input_output_aliases={n: n for n in range(len(arrays))},
        compiler_params=PARAMS,
        cost_estimate=COST,
    )(*arrays, *after)


def root_row(band, freq_count, delta, slot, w):
    before = 0 if delta is None else band + sum(band - d for d in range(1, delta))
    return (before + slot) * freq_count + w


def root_rows(band, freq_count):
    return -(-(root_row(band, freq_count, band, 0, 0) + freq_count) // 8) * 8


def own_tile(own, slot, m, blocks_dev):
    return own[0][m] if slot == 0 else own[1][(slot - 1) * blocks_dev + m]


def first_kernel(dims, *refs):
    n_aux, n_pair, blocks_dev, band, freq_count = dims
    records = refs[:n_aux]
    occ, freq, table = refs[n_aux : n_aux + 3]
    own, far = refs[n_aux + 3 : n_aux + 5], refs[n_aux + 5]
    out, out_one, roots = refs[-3:]
    pair_rows = own[0].shape[-1]
    virt_blocks = table.shape[1] // pair_rows
    aux_pos, pair_col = lax.axis_index("aux"), lax.axis_index("pair")

    def of_region(region):
        live = records[0][blocks_dev * band]
        for k in range(1, n_aux):
            live = jnp.where(lax.rem(aux_pos - region + n_aux, n_aux) == k, records[k][blocks_dev * band], live)
        return live

    masked, plain, one = {}, {}, {}
    for m in range(blocks_dev):
        block = m * n_aux + aux_pos
        for slot in range(band):
            centre = block - slot
            safe = jnp.maximum(centre, 0)
            region = safe // blocks_dev
            number = lax.rem(safe, blocks_dev)
            pair_block = (region * n_pair + pair_col) * blocks_dev + number
            start = pl.multiple_of(lax.rem(pair_block, virt_blocks) * pair_rows, pair_rows)
            gap = table[:, pl.ds(start, pair_rows)] - occ[pair_block // virt_blocks]
            alive = (centre >= 0) & (number < of_region(region)) & (records[0][m * band + slot] > 0)
            for w in range(freq_count):
                omega = freq[w]
                root = jnp.sqrt(2.0 * gap / (gap * gap + omega * omega))
                roots[m, pl.ds(root_row(band, freq_count, None, slot, w), 1), :] = root
                masked[m, slot, w] = root * alive.astype(jnp.float32)
                plain[m, slot, w] = root
                for delta in range(1, band - slot):
                    there = m + ((aux_pos + delta) >= n_aux).astype(jnp.int32)
                    row = jnp.minimum(there, blocks_dev - 1) * band + slot + delta
                    both = alive & (there < blocks_dev) & (records[(n_aux - delta) % n_aux][row] > 0)
                    spot = root_row(band, freq_count, delta, slot, w)
                    kept = root * both.astype(jnp.float32)
                    roots[m, pl.ds(spot, 1), :] = kept
                    if delta == 1:
                        one[m, slot, w] = kept
                if slot == 0:
                    there = m + ((aux_pos + 2) >= n_aux).astype(jnp.int32)
                    row = jnp.minimum(there, blocks_dev - 1) * band + 2
                    both = (centre >= 0) & (number < of_region(region)) & (there < blocks_dev)
                    both = both & (records[n_aux - 1][m * band + 1] > 0) & (records[n_aux - 2][row] > 0)
                    spot = root_row(band, freq_count, band, 0, w)
                    roots[m, pl.ds(spot, 1), :] = root * both.astype(jnp.float32)
    for m in range(blocks_dev):
        for w in range(freq_count):
            total = None
            for slot in range(band):
                a = (own_tile(own, slot, m, blocks_dev).astype(jnp.float32) * masked[m, slot, w]).astype(jnp.bfloat16)
                term = dot(a, a)
                total = term if total is None else total + term
            out[w, m] = total
            total = None
            for slot in range(band - 1):
                a = (own_tile(own, slot, m, blocks_dev).astype(jnp.float32) * one[m, slot, w]).astype(jnp.bfloat16)
                b = (far[slot * blocks_dev + m].astype(jnp.float32) * plain[m, slot, w]).astype(jnp.bfloat16)
                term = dot(a, b)
                total = term if total is None else total + term
            out_one[w, m] = total


def first_rows(dims, records, occ, freq, table, own, far, after):
    n_aux, n_pair, blocks_dev, band, freq_count = dims
    aux_rows, pair_rows = own[0].shape[-2:]
    return pl.pallas_call(
        functools.partial(first_kernel, dims),
        out_shape=[
            jax.ShapeDtypeStruct((freq_count, blocks_dev, aux_rows, aux_rows), jnp.float32),
            jax.ShapeDtypeStruct((freq_count, blocks_dev, aux_rows, aux_rows), jnp.float32),
            jax.ShapeDtypeStruct((blocks_dev, root_rows(band, freq_count), pair_rows), jnp.float32),
        ],
        in_specs=[SMEM] * (n_aux + 2) + [VMEM] * 4 + [ANY] * len(after),
        out_specs=[VMEM, VMEM, VMEM],
        compiler_params=PARAMS,
        cost_estimate=COST,
    )(*records, occ, freq, table, *own, far, *after)


def band_kernel(dims, delta, slots, rights, add, roots, *refs):
    n_aux, n_pair, blocks_dev, band, freq_count = dims
    out, zeros = refs[-2:]
    zeros[...] = jnp.zeros_like(zeros)
    for m in range(blocks_dev):
        sums = [refs[add][w, m] if add is not None else None for w in range(freq_count)]
        for s, slot in enumerate(slots):
            n, row = rights[s][m]
            left = own_tile(refs, slot, m, blocks_dev).astype(jnp.float32)
            right = refs[n][row].astype(jnp.float32)
            for w in range(freq_count):
                kept = roots[m, pl.ds(root_row(band, freq_count, delta, slot, w), 1), :]
                root = roots[m, pl.ds(root_row(band, freq_count, None, slot, w), 1), :]
                term = dot((left * kept).astype(jnp.bfloat16), (right * root).astype(jnp.bfloat16))
                sums[w] = term if sums[w] is None else sums[w] + term
        for w in range(freq_count):
            out[w, m] = sums[w]


def band_rows(dims, delta, slots, roots, own, far, after, add=None):
    n_aux, n_pair, blocks_dev, band, freq_count = dims
    aux_rows = own[0].shape[-2]
    arrays = list(own)
    rights = []
    for group in far:
        rows = [(len(arrays) + n, row) for n, array in enumerate(group) for row in range(array.shape[0])]
        rights.append(rows[-blocks_dev:] if len(rights) > 0 else rows[:blocks_dev])
        arrays += group
    spot = None if add is None else len(arrays)
    arrays += [] if add is None else [add]
    return pl.pallas_call(
        functools.partial(band_kernel, dims, delta, slots, rights, spot),
        out_shape=[
            jax.ShapeDtypeStruct((freq_count, blocks_dev, aux_rows, aux_rows), jnp.float32),
            jax.ShapeDtypeStruct((aux_rows // n_pair, aux_rows), jnp.float32),
        ],
        in_specs=[VMEM] * (1 + len(arrays)) + [ANY] * len(after),
        out_specs=[VMEM] * 2,
        compiler_params=PARAMS,
        cost_estimate=COST,
    )(roots, *arrays, *after)


def second_kernel(dims, pieces, roots, own, lower, *refs):
    n_aux, n_pair, blocks_dev, band, freq_count = dims
    out, out_next = refs[-2:]
    for m in range(blocks_dev):
        n, row = pieces[m]
        left = own[m].astype(jnp.float32)
        right = refs[n][row].astype(jnp.float32)
        other = lower[m].astype(jnp.float32)
        for w in range(freq_count):
            kept = roots[m, pl.ds(root_row(band, freq_count, 2, 0, w), 1), :]
            root = roots[m, pl.ds(root_row(band, freq_count, None, 0, w), 1), :]
            next_kept = roots[m, pl.ds(root_row(band, freq_count, band, 0, w), 1), :]
            scaled = (right * root).astype(jnp.bfloat16)
            out[w, m] = dot((left * kept).astype(jnp.bfloat16), scaled)
            out_next[w, m] = dot((other * next_kept).astype(jnp.bfloat16), scaled)


def second_rows(dims, roots, own, lower, c2, after):
    n_aux, n_pair, blocks_dev, band, freq_count = dims
    aux_rows = own[0].shape[-2]
    pieces = [(n, row) for n, array in enumerate(c2) for row in range(array.shape[0])]
    return pl.pallas_call(
        functools.partial(second_kernel, dims, pieces),
        out_shape=[jax.ShapeDtypeStruct((freq_count, blocks_dev, aux_rows, aux_rows), jnp.float32)] * 2,
        in_specs=[VMEM] * (3 + len(c2)) + [ANY] * len(after),
        out_specs=[VMEM] * 2,
        compiler_params=PARAMS,
        cost_estimate=COST,
    )(roots, own[0], lower, *c2, *after)


def halve(keep, pair_col, step, n_pair, rings, scale):
    freq_count, count, shares, height, width = keep.shape
    keep = keep.reshape(freq_count, count, shares // 2, 2, height, width)
    bit = lax.shift_right_logical(pair_col, jnp.uint32(step.bit_length() - 1)) & jnp.uint32(1)

    def pick(which):
        zero = jnp.uint32(0)
        sizes = (freq_count, count, shares // 2, 1, height, width)
        return lax.dynamic_slice(keep, [zero, zero, zero, which, zero, zero], sizes)[:, :, :, 0]

    part, mine = pick(bit ^ jnp.uint32(1)), pick(bit)
    sent = (part * scale).astype(jnp.float16)
    pairs = [(ring * n_pair + s, ring * n_pair + (s ^ step)) for ring in rings for s in range(n_pair)]
    got = lax.ppermute(sent, ("aux", "pair"), pairs)
    return mine + got.astype(jnp.float32) * (1.0 / scale), got


def totals(rows, pair_col, n_pair, rings, scale):
    freq_count, count, aux_rows, width = rows.shape
    keep = rows.reshape(freq_count, count, n_pair, aux_rows // n_pair, width)
    stages, step = [], 1
    while step < n_pair:
        keep, got = halve(keep, pair_col, step, n_pair, rings, scale)
        stages.append(got[0, 0, 0].astype(jnp.float32))
        step *= 2
    return stages, keep[:, :, 0]


def on_device(three_centre, locality, live_blocks, occ_energy, virt_energy, frequencies):
    n_aux = lax.axis_size("aux")
    n_pair = lax.axis_size("pair")
    pair_col = lax.axis_index("pair").astype(jnp.uint32)
    tiles = three_centre[0, 0, :, :, 0]
    blocks_dev, band, aux_rows, pair_rows = tiles.shape
    freq_count = frequencies.shape[0]
    dims = (n_aux, n_pair, blocks_dev, band, freq_count)
    scale = 128.0 / n_pair
    record = jnp.concatenate([locality[0, 0].reshape(-1), live_blocks[0]])
    records = [record] + [
        lax.ppermute(record, "aux", [(s, (s + k) % n_aux) for s in range(n_aux)]) for k in range(1, n_aux)
    ]
    two = chunks_of(blocks_dev, SPLIT)
    whole = list(range(n_aux))
    evens, odds = whole[::2], whole[1::2]
    plan = [(2, 2, first, count) for first, count in two] + [(1, 1, 0, blocks_dev)]
    first_slot, rest, near_two, far_two, to_one = pack(tiles, plan)
    own = (first_slot, rest)
    down2 = [(s, (s - 2) % n_aux) for s in whole]
    c2 = [lax.ppermute(near_two, "aux", down2)]
    (far_two,) = tie([far_two], records[1:] + c2)
    c2.append(lax.ppermute(far_two, "aux", down2))
    to_even = lax.ppermute(rest, "aux", [(s, s - 1) for s in odds])
    table = virt_energy.reshape(1, -1)
    rows0, rows_even, roots = first_rows(dims, records, occ_energy, frequencies, table, own, to_even, [far_two])
    b1 = lax.ppermute(tie([to_one], [roots])[0], "aux", [(s, (s - 1) % n_aux) for s in evens])
    bits0, z0 = totals(rows0, pair_col, n_pair, whole, scale)
    bits_even, z_even = totals(rows_even, pair_col, n_pair, evens, scale)
    rows2, rows_next = second_rows(dims, roots, own, to_even, c2, [bits_even[-1], bits0[-1]])
    bits2, z2 = totals(rows2, pair_col, n_pair, whole, scale)
    term = lax.ppermute((rows_next * scale).astype(jnp.float16), "aux", [(s, s + 1) for s in evens])
    term = term.astype(jnp.float32) * (1.0 / scale)
    rows_odd, zeros = band_rows(dims, 1, [0], roots, own, [[b1]], [], term)
    (rows_odd,) = tie([rows_odd], [bits2[-1] + zeros])
    _, z_odd = totals(rows_odd, pair_col, n_pair, odds, scale)
    even = lax.axis_index("aux").astype(jnp.uint32) & jnp.uint32(1) == 0
    out = jnp.concatenate([z0, jnp.where(even, z_even, z_odd), z2], axis=-1)
    return out[:, :, None]


def solution(mesh):
    return jax.shard_map(
        on_device,
        mesh=mesh,
        in_specs=(
            P(("grp", "aux"), "pair", None, None, None, None, None),
            P(("grp", "aux"), "pair", None, None, None),
            P(("grp", "aux"), "pair"),
            P("grp"),
            P("grp"),
            P("grp"),
        ),
        out_specs=P(None, None, ("grp", "aux"), "pair", None),
        check_vma=False,
    )
```

```python
import functools

import jax
import jax.numpy as jnp
from jax import lax
from jax.experimental import pallas as pl
from jax.experimental.pallas import tpu as pltpu
from jax.sharding import PartitionSpec as P

LIMIT = 16 << 20
SPLIT = (1, 7)
COST = pl.CostEstimate(flops=1000, bytes_accessed=1000, transcendentals=0)
PARAMS = pltpu.CompilerParams(vmem_limit_bytes=LIMIT)
ANY = pl.BlockSpec(memory_space=pl.ANY)
HBM = pl.BlockSpec(memory_space=pltpu.HBM)
SMEM = pl.BlockSpec(memory_space=pltpu.SMEM)
VMEM = pl.BlockSpec(memory_space=pltpu.VMEM)
DMA = pltpu.SemaphoreType.DMA


def chunks_of(count, sizes):
    ends = [count * sum(sizes[: n + 1]) // sum(sizes) for n in range(len(sizes))]
    return [(a, b - a) for a, b in zip([0] + ends[:-1], ends)]


def dot(a, b):
    return lax.dot_general(a, b, (((1,), (1,)), ((), ())), preferred_element_type=jnp.float32)


def pack_kernel(plan, tiles, first_slot, rest, *outs):
    blocks_dev, band = tiles.shape[:2]
    aux_pos = lax.axis_index("aux")
    for out, (slot, back, first, count) in zip(outs, plan):
        shift = (aux_pos < back).astype(jnp.int32)
        for i in range(count):
            out[i] = tiles[jnp.minimum(first + i + shift, blocks_dev - 1), slot]
    for m in range(blocks_dev):
        first_slot[m] = tiles[m, 0]
        for slot in range(1, band):
            rest[(slot - 1) * blocks_dev + m] = tiles[m, slot]


def pack(tiles, plan):
    blocks_dev, band, aux_rows, pair_rows = tiles.shape
    counts = [blocks_dev, (band - 1) * blocks_dev] + [part[3] for part in plan]
    return pl.pallas_call(
        functools.partial(pack_kernel, plan),
        out_shape=[jax.ShapeDtypeStruct((count, aux_rows, pair_rows), tiles.dtype) for count in counts],
        in_specs=[VMEM],
        out_specs=[VMEM] * len(counts),
        compiler_params=PARAMS,
        cost_estimate=COST,
    )(tiles)


def tie(arrays, after):
    return pl.pallas_call(
        lambda *refs: None,
        out_shape=[jax.ShapeDtypeStruct(array.shape, array.dtype) for array in arrays],
        in_specs=[ANY] * (len(arrays) + len(after)),
        out_specs=[ANY] * len(arrays),
        input_output_aliases={n: n for n in range(len(arrays))},
        compiler_params=PARAMS,
        cost_estimate=COST,
    )(*arrays, *after)


def root_row(band, freq_count, delta, slot, w):
    before = 0 if delta is None else band + sum(band - d for d in range(1, delta))
    return (before + slot) * freq_count + w


def root_rows(band, freq_count):
    return -(-(root_row(band, freq_count, band, 0, 0) + freq_count) // 8) * 8


def own_tile(own, slot, m, blocks_dev):
    return own[0][m] if slot == 0 else own[1][(slot - 1) * blocks_dev + m]


def first_kernel(dims, *refs):
    n_aux, n_pair, blocks_dev, band, freq_count = dims
    records = refs[:n_aux]
    occ, freq, table = refs[n_aux : n_aux + 3]
    own, far = refs[n_aux + 3 : n_aux + 5], refs[n_aux + 5]
    out, out_one, roots = refs[-3:]
    pair_rows = own[0].shape[-1]
    virt_blocks = table.shape[1] // pair_rows
    aux_pos, pair_col = lax.axis_index("aux"), lax.axis_index("pair")

    def of_region(region):
        live = records[0][blocks_dev * band]
        for k in range(1, n_aux):
            live = jnp.where(lax.rem(aux_pos - region + n_aux, n_aux) == k, records[k][blocks_dev * band], live)
        return live

    masked, plain, one = {}, {}, {}
    for m in range(blocks_dev):
        block = m * n_aux + aux_pos
        for slot in range(band):
            centre = block - slot
            safe = jnp.maximum(centre, 0)
            region = safe // blocks_dev
            number = lax.rem(safe, blocks_dev)
            pair_block = (region * n_pair + pair_col) * blocks_dev + number
            start = pl.multiple_of(lax.rem(pair_block, virt_blocks) * pair_rows, pair_rows)
            gap = table[:, pl.ds(start, pair_rows)] - occ[pair_block // virt_blocks]
            alive = (centre >= 0) & (number < of_region(region)) & (records[0][m * band + slot] > 0)
            for w in range(freq_count):
                omega = freq[w]
                root = jnp.sqrt(2.0 * gap / (gap * gap + omega * omega))
                roots[m, pl.ds(root_row(band, freq_count, None, slot, w), 1), :] = root
                masked[m, slot, w] = root * alive.astype(jnp.float32)
                plain[m, slot, w] = root
                for delta in range(1, band - slot):
                    there = m + ((aux_pos + delta) >= n_aux).astype(jnp.int32)
                    row = jnp.minimum(there, blocks_dev - 1) * band + slot + delta
                    both = alive & (there < blocks_dev) & (records[(n_aux - delta) % n_aux][row] > 0)
                    spot = root_row(band, freq_count, delta, slot, w)
                    kept = root * both.astype(jnp.float32)
                    roots[m, pl.ds(spot, 1), :] = kept
                    if delta == 1:
                        one[m, slot, w] = kept
                if slot == 0:
                    there = m + ((aux_pos + 2) >= n_aux).astype(jnp.int32)
                    row = jnp.minimum(there, blocks_dev - 1) * band + 2
                    both = (centre >= 0) & (number < of_region(region)) & (there < blocks_dev)
                    both = both & (records[n_aux - 1][m * band + 1] > 0) & (records[n_aux - 2][row] > 0)
                    spot = root_row(band, freq_count, band, 0, w)
                    roots[m, pl.ds(spot, 1), :] = root * both.astype(jnp.float32)
    for m in range(blocks_dev):
        for w in range(freq_count):
            total = None
            for slot in range(band):
                a = (own_tile(own, slot, m, blocks_dev).astype(jnp.float32) * masked[m, slot, w]).astype(jnp.bfloat16)
                term = dot(a, a)
                total = term if total is None else total + term
            out[w, m] = total
            total = None
            for slot in range(band - 1):
                a = (own_tile(own, slot, m, blocks_dev).astype(jnp.float32) * one[m, slot, w]).astype(jnp.bfloat16)
                b = (far[slot * blocks_dev + m].astype(jnp.float32) * plain[m, slot, w]).astype(jnp.bfloat16)
                term = dot(a, b)
                total = term if total is None else total + term
            out_one[w, m] = total


def first_rows(dims, records, occ, freq, table, own, far, after):
    n_aux, n_pair, blocks_dev, band, freq_count = dims
    aux_rows, pair_rows = own[0].shape[-2:]
    return pl.pallas_call(
        functools.partial(first_kernel, dims),
        out_shape=[
            jax.ShapeDtypeStruct((freq_count, blocks_dev, aux_rows, aux_rows), jnp.float32),
            jax.ShapeDtypeStruct((freq_count, blocks_dev, aux_rows, aux_rows), jnp.float32),
            jax.ShapeDtypeStruct((blocks_dev, root_rows(band, freq_count), pair_rows), jnp.float32),
        ],
        in_specs=[SMEM] * (n_aux + 2) + [VMEM] * 4 + [ANY] * len(after),
        out_specs=[VMEM, VMEM, VMEM],
        compiler_params=PARAMS,
        cost_estimate=COST,
    )(*records, occ, freq, table, *own, far, *after)


def band_kernel(dims, delta, slots, rights, add, roots, *refs):
    n_aux, n_pair, blocks_dev, band, freq_count = dims
    out, zeros = refs[-2:]
    zeros[...] = jnp.zeros_like(zeros)
    for m in range(blocks_dev):
        sums = [refs[add][w, m] if add is not None else None for w in range(freq_count)]
        for s, slot in enumerate(slots):
            n, row = rights[s][m]
            left = own_tile(refs, slot, m, blocks_dev).astype(jnp.float32)
            right = refs[n][row].astype(jnp.float32)
            for w in range(freq_count):
                kept = roots[m, pl.ds(root_row(band, freq_count, delta, slot, w), 1), :]
                root = roots[m, pl.ds(root_row(band, freq_count, None, slot, w), 1), :]
                term = dot((left * kept).astype(jnp.bfloat16), (right * root).astype(jnp.bfloat16))
                sums[w] = term if sums[w] is None else sums[w] + term
        for w in range(freq_count):
            out[w, m] = sums[w]


def band_rows(dims, delta, slots, roots, own, far, after, add=None):
    n_aux, n_pair, blocks_dev, band, freq_count = dims
    aux_rows = own[0].shape[-2]
    arrays = list(own)
    rights = []
    for group in far:
        rows = [(len(arrays) + n, row) for n, array in enumerate(group) for row in range(array.shape[0])]
        rights.append(rows[-blocks_dev:] if len(rights) > 0 else rows[:blocks_dev])
        arrays += group
    spot = None if add is None else len(arrays)
    arrays += [] if add is None else [add]
    return pl.pallas_call(
        functools.partial(band_kernel, dims, delta, slots, rights, spot),
        out_shape=[
            jax.ShapeDtypeStruct((freq_count, blocks_dev, aux_rows, aux_rows), jnp.float32),
            jax.ShapeDtypeStruct((aux_rows // n_pair, aux_rows), jnp.float32),
        ],
        in_specs=[VMEM] * (1 + len(arrays)) + [ANY] * len(after),
        out_specs=[VMEM] * 2,
        compiler_params=PARAMS,
        cost_estimate=COST,
    )(roots, *arrays, *after)


def second_kernel(dims, pieces, roots, own, lower, *refs):
    n_aux, n_pair, blocks_dev, band, freq_count = dims
    out, out_next = refs[-2:]
    for m in range(blocks_dev):
        n, row = pieces[m]
        left = own[m].astype(jnp.float32)
        right = refs[n][row].astype(jnp.float32)
        other = lower[m].astype(jnp.float32)
        for w in range(freq_count):
            kept = roots[m, pl.ds(root_row(band, freq_count, 2, 0, w), 1), :]
            root = roots[m, pl.ds(root_row(band, freq_count, None, 0, w), 1), :]
            next_kept = roots[m, pl.ds(root_row(band, freq_count, band, 0, w), 1), :]
            scaled = (right * root).astype(jnp.bfloat16)
            out[w, m] = dot((left * kept).astype(jnp.bfloat16), scaled)
            out_next[w, m] = dot((other * next_kept).astype(jnp.bfloat16), scaled)


def second_rows(dims, roots, own, lower, c2, after):
    n_aux, n_pair, blocks_dev, band, freq_count = dims
    aux_rows = own[0].shape[-2]
    pieces = [(n, row) for n, array in enumerate(c2) for row in range(array.shape[0])]
    return pl.pallas_call(
        functools.partial(second_kernel, dims, pieces),
        out_shape=[jax.ShapeDtypeStruct((freq_count, blocks_dev, aux_rows, aux_rows), jnp.float32)] * 2,
        in_specs=[VMEM] * (3 + len(c2)) + [ANY] * len(after),
        out_specs=[VMEM] * 2,
        compiler_params=PARAMS,
        cost_estimate=COST,
    )(roots, own[0], lower, *c2, *after)


def halve(keep, pair_col, step, n_pair, rings, scale):
    freq_count, count, shares, height, width = keep.shape
    keep = keep.reshape(freq_count, count, shares // 2, 2, height, width)
    bit = lax.shift_right_logical(pair_col, jnp.uint32(step.bit_length() - 1)) & jnp.uint32(1)

    def pick(which):
        zero = jnp.uint32(0)
        sizes = (freq_count, count, shares // 2, 1, height, width)
        return lax.dynamic_slice(keep, [zero, zero, zero, which, zero, zero], sizes)[:, :, :, 0]

    part, mine = pick(bit ^ jnp.uint32(1)), pick(bit)
    sent = (part * scale).astype(jnp.float16)
    pairs = [(ring * n_pair + s, ring * n_pair + (s ^ step)) for ring in rings for s in range(n_pair)]
    got = lax.ppermute(sent, ("aux", "pair"), pairs)
    return mine + got.astype(jnp.float32) * (1.0 / scale), got


def totals(rows, pair_col, n_pair, rings, scale):
    freq_count, count, aux_rows, width = rows.shape
    keep = rows.reshape(freq_count, count, n_pair, aux_rows // n_pair, width)
    stages, step = [], 1
    while step < n_pair:
        keep, got = halve(keep, pair_col, step, n_pair, rings, scale)
        stages.append(got[0, 0, 0].astype(jnp.float32))
        step *= 2
    return stages, keep[:, :, 0]


def total_at_once(rows, pair_col, n_pair, rings, scale):
    freq_count, count, aux_rows, width = rows.shape
    height = aux_rows // n_pair

    def share(column):
        zero = jnp.uint32(0)
        start = column * jnp.uint32(height)
        return lax.dynamic_slice(rows, [zero, zero, start, zero], (freq_count, count, height, width))

    far = []
    for k in reversed(range(1, n_pair)):
        sent = (share(pair_col ^ jnp.uint32(k)) * scale).astype(jnp.float16)
        pairs = [(ring * n_pair + s, ring * n_pair + (s ^ k)) for ring in rings for s in range(n_pair)]
        far.append(lax.ppermute(sent, ("aux", "pair"), pairs).astype(jnp.float32))
    return share(pair_col) + sum(far) * (1.0 / scale)


def on_device(three_centre, locality, live_blocks, occ_energy, virt_energy, frequencies):
    n_aux = lax.axis_size("aux")
    n_pair = lax.axis_size("pair")
    pair_col = lax.axis_index("pair").astype(jnp.uint32)
    tiles = three_centre[0, 0, :, :, 0]
    blocks_dev, band, aux_rows, pair_rows = tiles.shape
    freq_count = frequencies.shape[0]
    dims = (n_aux, n_pair, blocks_dev, band, freq_count)
    scale = 128.0 / n_pair
    record = jnp.concatenate([locality[0, 0].reshape(-1), live_blocks[0]])
    records = [record] + [
        lax.ppermute(record, "aux", [(s, (s + k) % n_aux) for s in range(n_aux)]) for k in range(1, n_aux)
    ]
    two = chunks_of(blocks_dev, SPLIT)
    whole = list(range(n_aux))
    evens, odds = whole[::2], whole[1::2]
    plan = [(2, 2, first, count) for first, count in two] + [(1, 1, 0, blocks_dev)]
    first_slot, rest, near_two, far_two, to_one = pack(tiles, plan)
    own = (first_slot, rest)
    down2 = [(s, (s - 2) % n_aux) for s in whole]
    c2 = [lax.ppermute(near_two, "aux", down2)]
    (far_two,) = tie([far_two], records[1:] + c2)
    c2.append(lax.ppermute(far_two, "aux", down2))
    to_even = lax.ppermute(rest, "aux", [(s, s - 1) for s in odds])
    table = virt_energy.reshape(1, -1)
    rows0, rows_even, roots = first_rows(dims, records, occ_energy, frequencies, table, own, to_even, [far_two])
    b1 = lax.ppermute(tie([to_one], [roots])[0], "aux", [(s, (s - 1) % n_aux) for s in evens])
    bits0, z0 = totals(rows0, pair_col, n_pair, whole, scale)
    bits_even, z_even = totals(rows_even, pair_col, n_pair, evens, scale)
    rows2, rows_next = second_rows(dims, roots, own, to_even, c2, [bits_even[-1], bits0[-1]])
    bits2, z2 = totals(rows2, pair_col, n_pair, whole, scale)
    term = lax.ppermute((rows_next * scale).astype(jnp.float16), "aux", [(s, s + 1) for s in evens])
    term = term.astype(jnp.float32) * (1.0 / scale)
    rows_odd, zeros = band_rows(dims, 1, [0], roots, own, [[b1]], [], term)
    (rows_odd,) = tie([rows_odd], [bits2[-1] + zeros])
    z_odd = total_at_once(rows_odd, pair_col, n_pair, odds, scale)
    even = lax.axis_index("aux").astype(jnp.uint32) & jnp.uint32(1) == 0
    out = jnp.concatenate([z0, jnp.where(even, z_even, z_odd), z2], axis=-1)
    return out[:, :, None]


def solution(mesh):
    return jax.shard_map(
        on_device,
        mesh=mesh,
        in_specs=(
            P(("grp", "aux"), "pair", None, None, None, None, None),
            P(("grp", "aux"), "pair", None, None, None),
            P(("grp", "aux"), "pair"),
            P("grp"),
            P("grp"),
            P("grp"),
        ),
        out_specs=P(None, None, ("grp", "aux"), "pair", None),
        check_vma=False,
    )
```

```python
import functools

import jax
import jax.numpy as jnp
from jax import lax
from jax.experimental import pallas as pl
from jax.experimental.pallas import tpu as pltpu
from jax.sharding import PartitionSpec as P

LIMIT = 16 << 20
SPLIT = (1, 7)
COST = pl.CostEstimate(flops=1000, bytes_accessed=1000, transcendentals=0)
PARAMS = pltpu.CompilerParams(vmem_limit_bytes=LIMIT)
ANY = pl.BlockSpec(memory_space=pl.ANY)
HBM = pl.BlockSpec(memory_space=pltpu.HBM)
SMEM = pl.BlockSpec(memory_space=pltpu.SMEM)
VMEM = pl.BlockSpec(memory_space=pltpu.VMEM)
DMA = pltpu.SemaphoreType.DMA


def chunks_of(count, sizes):
    ends = [count * sum(sizes[: n + 1]) // sum(sizes) for n in range(len(sizes))]
    return [(a, b - a) for a, b in zip([0] + ends[:-1], ends)]


def dot(a, b):
    return lax.dot_general(a, b, (((1,), (1,)), ((), ())), preferred_element_type=jnp.float32)


def pack_kernel(plan, tiles, first_slot, rest, *outs):
    blocks_dev, band = tiles.shape[:2]
    aux_pos = lax.axis_index("aux")
    for out, (slot, back, first, count) in zip(outs, plan):
        shift = (aux_pos < back).astype(jnp.int32)
        for i in range(count):
            out[i] = tiles[jnp.minimum(first + i + shift, blocks_dev - 1), slot]
    for m in range(blocks_dev):
        first_slot[m] = tiles[m, 0]
        for slot in range(1, band):
            rest[(slot - 1) * blocks_dev + m] = tiles[m, slot]


def pack(tiles, plan):
    blocks_dev, band, aux_rows, pair_rows = tiles.shape
    counts = [blocks_dev, (band - 1) * blocks_dev] + [part[3] for part in plan]
    return pl.pallas_call(
        functools.partial(pack_kernel, plan),
        out_shape=[jax.ShapeDtypeStruct((count, aux_rows, pair_rows), tiles.dtype) for count in counts],
        in_specs=[VMEM],
        out_specs=[VMEM] * len(counts),
        compiler_params=PARAMS,
        cost_estimate=COST,
    )(tiles)


def tie(arrays, after):
    return pl.pallas_call(
        lambda *refs: None,
        out_shape=[jax.ShapeDtypeStruct(array.shape, array.dtype) for array in arrays],
        in_specs=[ANY] * (len(arrays) + len(after)),
        out_specs=[ANY] * len(arrays),
        input_output_aliases={n: n for n in range(len(arrays))},
        compiler_params=PARAMS,
        cost_estimate=COST,
    )(*arrays, *after)


def root_row(band, freq_count, delta, slot, w):
    before = 0 if delta is None else band + sum(band - d for d in range(1, delta))
    return (before + slot) * freq_count + w


def root_rows(band, freq_count):
    return -(-(root_row(band, freq_count, band, 0, 0) + freq_count) // 8) * 8


def own_tile(own, slot, m, blocks_dev):
    return own[0][m] if slot == 0 else own[1][(slot - 1) * blocks_dev + m]


def first_kernel(dims, *refs):
    n_aux, n_pair, blocks_dev, band, freq_count = dims
    records = refs[:n_aux]
    occ, freq, table = refs[n_aux : n_aux + 3]
    own, far = refs[n_aux + 3 : n_aux + 5], refs[n_aux + 5]
    out, out_one, roots = refs[-3:]
    pair_rows = own[0].shape[-1]
    virt_blocks = table.shape[1] // pair_rows
    aux_pos, pair_col = lax.axis_index("aux"), lax.axis_index("pair")

    def of_region(region):
        live = records[0][blocks_dev * band]
        for k in range(1, n_aux):
            live = jnp.where(lax.rem(aux_pos - region + n_aux, n_aux) == k, records[k][blocks_dev * band], live)
        return live

    masked, plain, one = {}, {}, {}
    for m in range(blocks_dev):
        block = m * n_aux + aux_pos
        for slot in range(band):
            centre = block - slot
            safe = jnp.maximum(centre, 0)
            region = safe // blocks_dev
            number = lax.rem(safe, blocks_dev)
            pair_block = (region * n_pair + pair_col) * blocks_dev + number
            start = pl.multiple_of(lax.rem(pair_block, virt_blocks) * pair_rows, pair_rows)
            gap = table[:, pl.ds(start, pair_rows)] - occ[pair_block // virt_blocks]
            alive = (centre >= 0) & (number < of_region(region)) & (records[0][m * band + slot] > 0)
            for w in range(freq_count):
                omega = freq[w]
                root = jnp.sqrt(2.0 * gap / (gap * gap + omega * omega))
                roots[m, pl.ds(root_row(band, freq_count, None, slot, w), 1), :] = root
                masked[m, slot, w] = root * alive.astype(jnp.float32)
                plain[m, slot, w] = root
                for delta in range(1, band - slot):
                    there = m + ((aux_pos + delta) >= n_aux).astype(jnp.int32)
                    row = jnp.minimum(there, blocks_dev - 1) * band + slot + delta
                    both = alive & (there < blocks_dev) & (records[(n_aux - delta) % n_aux][row] > 0)
                    spot = root_row(band, freq_count, delta, slot, w)
                    kept = root * both.astype(jnp.float32)
                    roots[m, pl.ds(spot, 1), :] = kept
                    if delta == 1:
                        one[m, slot, w] = kept
                if slot == 0:
                    there = m + ((aux_pos + 2) >= n_aux).astype(jnp.int32)
                    row = jnp.minimum(there, blocks_dev - 1) * band + 2
                    both = (centre >= 0) & (number < of_region(region)) & (there < blocks_dev)
                    both = both & (records[n_aux - 1][m * band + 1] > 0) & (records[n_aux - 2][row] > 0)
                    spot = root_row(band, freq_count, band, 0, w)
                    roots[m, pl.ds(spot, 1), :] = root * both.astype(jnp.float32)
    for m in range(blocks_dev):
        for w in range(freq_count):
            total = None
            for slot in range(band):
                a = (own_tile(own, slot, m, blocks_dev).astype(jnp.float32) * masked[m, slot, w]).astype(jnp.bfloat16)
                term = dot(a, a)
                total = term if total is None else total + term
            out[w, m] = total
            total = None
            for slot in range(band - 1):
                a = (own_tile(own, slot, m, blocks_dev).astype(jnp.float32) * one[m, slot, w]).astype(jnp.bfloat16)
                b = (far[slot * blocks_dev + m].astype(jnp.float32) * plain[m, slot, w]).astype(jnp.bfloat16)
                term = dot(a, b)
                total = term if total is None else total + term
            out_one[w, m] = total


def first_rows(dims, records, occ, freq, table, own, far, after):
    n_aux, n_pair, blocks_dev, band, freq_count = dims
    aux_rows, pair_rows = own[0].shape[-2:]
    return pl.pallas_call(
        functools.partial(first_kernel, dims),
        out_shape=[
            jax.ShapeDtypeStruct((freq_count, blocks_dev, aux_rows, aux_rows), jnp.float32),
            jax.ShapeDtypeStruct((freq_count, blocks_dev, aux_rows, aux_rows), jnp.float32),
            jax.ShapeDtypeStruct((blocks_dev, root_rows(band, freq_count), pair_rows), jnp.float32),
        ],
        in_specs=[SMEM] * (n_aux + 2) + [VMEM] * 4 + [ANY] * len(after),
        out_specs=[VMEM, VMEM, VMEM],
        compiler_params=PARAMS,
        cost_estimate=COST,
    )(*records, occ, freq, table, *own, far, *after)


def odd_kernel(dims, roots, own, far, add, out, zeros):
    n_aux, n_pair, blocks_dev, band, freq_count = dims
    zeros[...] = jnp.zeros_like(zeros)
    for m in range(blocks_dev):
        left = own[m].astype(jnp.float32)
        right = far[m].astype(jnp.float32)
        for w in range(freq_count):
            kept = roots[m, pl.ds(root_row(band, freq_count, 1, 0, w), 1), :]
            root = roots[m, pl.ds(root_row(band, freq_count, None, 0, w), 1), :]
            term = dot((left * kept).astype(jnp.bfloat16), (right * root).astype(jnp.bfloat16))
            out[w, m] = add[w, m] + term


def odd_rows(dims, roots, own, far, add):
    n_aux, n_pair, blocks_dev, band, freq_count = dims
    aux_rows = own.shape[-2]
    return pl.pallas_call(
        functools.partial(odd_kernel, dims),
        out_shape=[
            jax.ShapeDtypeStruct((freq_count, blocks_dev, aux_rows, aux_rows), jnp.float32),
            jax.ShapeDtypeStruct((aux_rows // n_pair, aux_rows), jnp.float32),
        ],
        in_specs=[VMEM] * 4,
        out_specs=[VMEM] * 2,
        compiler_params=PARAMS,
        cost_estimate=COST,
    )(roots, own, far, add)


def second_kernel(dims, pieces, roots, own, lower, *refs):
    n_aux, n_pair, blocks_dev, band, freq_count = dims
    out, out_next = refs[-2:]
    for m in range(blocks_dev):
        n, row = pieces[m]
        left = own[m].astype(jnp.float32)
        right = refs[n][row].astype(jnp.float32)
        other = lower[m].astype(jnp.float32)
        for w in range(freq_count):
            kept = roots[m, pl.ds(root_row(band, freq_count, 2, 0, w), 1), :]
            root = roots[m, pl.ds(root_row(band, freq_count, None, 0, w), 1), :]
            next_kept = roots[m, pl.ds(root_row(band, freq_count, band, 0, w), 1), :]
            scaled = (right * root).astype(jnp.bfloat16)
            out[w, m] = dot((left * kept).astype(jnp.bfloat16), scaled)
            out_next[w, m] = dot((other * next_kept).astype(jnp.bfloat16), scaled)


def second_rows(dims, roots, own, lower, c2, after):
    n_aux, n_pair, blocks_dev, band, freq_count = dims
    aux_rows = own[0].shape[-2]
    pieces = [(n, row) for n, array in enumerate(c2) for row in range(array.shape[0])]
    return pl.pallas_call(
        functools.partial(second_kernel, dims, pieces),
        out_shape=[jax.ShapeDtypeStruct((freq_count, blocks_dev, aux_rows, aux_rows), jnp.float32)] * 2,
        in_specs=[VMEM] * (3 + len(c2)) + [ANY] * len(after),
        out_specs=[VMEM] * 2,
        compiler_params=PARAMS,
        cost_estimate=COST,
    )(roots, own[0], lower, *c2, *after)


def halve(keep, pair_col, step, n_pair, rings, scale):
    freq_count, count, shares, height, width = keep.shape
    keep = keep.reshape(freq_count, count, shares // 2, 2, height, width)
    bit = lax.shift_right_logical(pair_col, jnp.uint32(step.bit_length() - 1)) & jnp.uint32(1)

    def pick(which):
        zero = jnp.uint32(0)
        sizes = (freq_count, count, shares // 2, 1, height, width)
        return lax.dynamic_slice(keep, [zero, zero, zero, which, zero, zero], sizes)[:, :, :, 0]

    part, mine = pick(bit ^ jnp.uint32(1)), pick(bit)
    sent = (part * scale).astype(jnp.float16)
    pairs = [(ring * n_pair + s, ring * n_pair + (s ^ step)) for ring in rings for s in range(n_pair)]
    got = lax.ppermute(sent, ("aux", "pair"), pairs)
    return mine + got.astype(jnp.float32) * (1.0 / scale), got


def totals(rows, pair_col, n_pair, rings, scale):
    freq_count, count, aux_rows, width = rows.shape
    keep = rows.reshape(freq_count, count, n_pair, aux_rows // n_pair, width)
    stages, step = [], 1
    while step < n_pair:
        keep, got = halve(keep, pair_col, step, n_pair, rings, scale)
        stages.append(got[0, 0, 0].astype(jnp.float32))
        step *= 2
    return stages, keep[:, :, 0]


def total_at_once(rows, pair_col, n_pair, rings, scale):
    freq_count, count, aux_rows, width = rows.shape
    height = aux_rows // n_pair

    def share(column):
        zero = jnp.uint32(0)
        start = column * jnp.uint32(height)
        return lax.dynamic_slice(rows, [zero, zero, start, zero], (freq_count, count, height, width))

    far = []
    for k in reversed(range(1, n_pair)):
        sent = (share(pair_col ^ jnp.uint32(k)) * scale).astype(jnp.float16)
        pairs = [(ring * n_pair + s, ring * n_pair + (s ^ k)) for ring in rings for s in range(n_pair)]
        far.append(lax.ppermute(sent, ("aux", "pair"), pairs).astype(jnp.float32))
    return share(pair_col) + sum(far) * (1.0 / scale)


def on_device(three_centre, locality, live_blocks, occ_energy, virt_energy, frequencies):
    n_aux = lax.axis_size("aux")
    n_pair = lax.axis_size("pair")
    pair_col = lax.axis_index("pair").astype(jnp.uint32)
    tiles = three_centre[0, 0, :, :, 0]
    blocks_dev, band, aux_rows, pair_rows = tiles.shape
    freq_count = frequencies.shape[0]
    dims = (n_aux, n_pair, blocks_dev, band, freq_count)
    scale = 128.0 / n_pair
    record = jnp.concatenate([locality[0, 0].reshape(-1), live_blocks[0]])
    records = [record] + [
        lax.ppermute(record, "aux", [(s, (s + k) % n_aux) for s in range(n_aux)]) for k in range(1, n_aux)
    ]
    two = chunks_of(blocks_dev, SPLIT)
    whole = list(range(n_aux))
    evens, odds = whole[::2], whole[1::2]
    plan = [(2, 2, first, count) for first, count in two] + [(1, 1, 0, blocks_dev)]
    first_slot, rest, near_two, far_two, to_one = pack(tiles, plan)
    own = (first_slot, rest)
    down2 = [(s, (s - 2) % n_aux) for s in whole]
    c2 = [lax.ppermute(near_two, "aux", down2)]
    (far_two,) = tie([far_two], records[1:] + c2)
    c2.append(lax.ppermute(far_two, "aux", down2))
    to_even = lax.ppermute(rest, "aux", [(s, s - 1) for s in odds])
    table = virt_energy.reshape(1, -1)
    rows0, rows_even, roots = first_rows(dims, records, occ_energy, frequencies, table, own, to_even, [far_two])
    b1 = lax.ppermute(tie([to_one], [roots])[0], "aux", [(s, (s - 1) % n_aux) for s in evens])
    bits0, z0 = totals(rows0, pair_col, n_pair, whole, scale)
    bits_even, z_even = totals(rows_even, pair_col, n_pair, evens, scale)
    rows2, rows_next = second_rows(dims, roots, own, to_even, c2, [bits_even[-1], bits0[-1]])
    bits2, z2 = totals(rows2, pair_col, n_pair, whole, scale)
    term = lax.ppermute((rows_next * scale).astype(jnp.float16), "aux", [(s, s + 1) for s in evens])
    term = term.astype(jnp.float32) * (1.0 / scale)
    rows_odd, zeros = odd_rows(dims, roots, first_slot, b1, term)
    (rows_odd,) = tie([rows_odd], [bits2[-1] + zeros])
    z_odd = total_at_once(rows_odd, pair_col, n_pair, odds, scale)
    even = lax.axis_index("aux").astype(jnp.uint32) & jnp.uint32(1) == 0
    out = jnp.concatenate([z0, jnp.where(even, z_even, z_odd), z2], axis=-1)
    return out[:, :, None]


def solution(mesh):
    return jax.shard_map(
        on_device,
        mesh=mesh,
        in_specs=(
            P(("grp", "aux"), "pair", None, None, None, None, None),
            P(("grp", "aux"), "pair", None, None, None),
            P(("grp", "aux"), "pair"),
            P("grp"),
            P("grp"),
            P("grp"),
        ),
        out_specs=P(None, None, ("grp", "aux"), "pair", None),
        check_vma=False,
    )
```

```python
import functools

import jax
import jax.numpy as jnp
from jax import lax
from jax.experimental import pallas as pl
from jax.experimental.pallas import tpu as pltpu
from jax.sharding import PartitionSpec as P

LIMIT = 16 << 20
SPLIT = (1, 7)
COST = pl.CostEstimate(flops=1000, bytes_accessed=1000, transcendentals=0)
PARAMS = pltpu.CompilerParams(vmem_limit_bytes=LIMIT)
ANY = pl.BlockSpec(memory_space=pl.ANY)
HBM = pl.BlockSpec(memory_space=pltpu.HBM)
SMEM = pl.BlockSpec(memory_space=pltpu.SMEM)
VMEM = pl.BlockSpec(memory_space=pltpu.VMEM)
DMA = pltpu.SemaphoreType.DMA


def chunks_of(count, sizes):
    ends = [count * sum(sizes[: n + 1]) // sum(sizes) for n in range(len(sizes))]
    return [(a, b - a) for a, b in zip([0] + ends[:-1], ends)]


def dot(a, b):
    return lax.dot_general(a, b, (((1,), (1,)), ((), ())), preferred_element_type=jnp.float32)


def pack_kernel(plan, tiles, first_slot, rest, *outs):
    blocks_dev, band = tiles.shape[:2]
    aux_pos = lax.axis_index("aux")
    for out, (slot, back, first, count) in zip(outs, plan):
        shift = (aux_pos < back).astype(jnp.int32)
        for i in range(count):
            out[i] = tiles[jnp.minimum(first + i + shift, blocks_dev - 1), slot]
    for m in range(blocks_dev):
        first_slot[m] = tiles[m, 0]
        for slot in range(1, band):
            rest[(slot - 1) * blocks_dev + m] = tiles[m, slot]


def pack(tiles, plan):
    blocks_dev, band, aux_rows, pair_rows = tiles.shape
    counts = [blocks_dev, (band - 1) * blocks_dev] + [part[3] for part in plan]
    return pl.pallas_call(
        functools.partial(pack_kernel, plan),
        out_shape=[jax.ShapeDtypeStruct((count, aux_rows, pair_rows), tiles.dtype) for count in counts],
        in_specs=[VMEM],
        out_specs=[VMEM] * len(counts),
        compiler_params=PARAMS,
        cost_estimate=COST,
    )(tiles)


def tie(arrays, after):
    return pl.pallas_call(
        lambda *refs: None,
        out_shape=[jax.ShapeDtypeStruct(array.shape, array.dtype) for array in arrays],
        in_specs=[ANY] * (len(arrays) + len(after)),
        out_specs=[ANY] * len(arrays),
        input_output_aliases={n: n for n in range(len(arrays))},
        compiler_params=PARAMS,
        cost_estimate=COST,
    )(*arrays, *after)


def root_row(band, freq_count, delta, slot, w):
    before = 0 if delta is None else band + sum(band - d for d in range(1, delta))
    return (before + slot) * freq_count + w


def root_rows(band, freq_count):
    return -(-(root_row(band, freq_count, band, 0, 0) + freq_count) // 8) * 8


def own_tile(own, slot, m, blocks_dev):
    return own[0][m] if slot == 0 else own[1][(slot - 1) * blocks_dev + m]


def first_kernel(dims, *refs):
    n_aux, n_pair, blocks_dev, band, freq_count = dims
    records = refs[:n_aux]
    occ, freq, table = refs[n_aux : n_aux + 3]
    own, far = refs[n_aux + 3 : n_aux + 5], refs[n_aux + 5]
    out, out_one, roots, to_one = refs[-4:]
    pair_rows = own[0].shape[-1]
    virt_blocks = table.shape[1] // pair_rows
    aux_pos, pair_col = lax.axis_index("aux"), lax.axis_index("pair")

    def of_region(region):
        live = records[0][blocks_dev * band]
        for k in range(1, n_aux):
            live = jnp.where(lax.rem(aux_pos - region + n_aux, n_aux) == k, records[k][blocks_dev * band], live)
        return live

    for m in range(blocks_dev):
        to_one[m] = own[1][jnp.minimum(m + (aux_pos < 1).astype(jnp.int32), blocks_dev - 1)]

    masked, plain, one = {}, {}, {}
    for m in range(blocks_dev):
        block = m * n_aux + aux_pos
        for slot in range(band):
            centre = block - slot
            safe = jnp.maximum(centre, 0)
            region = safe // blocks_dev
            number = lax.rem(safe, blocks_dev)
            pair_block = (region * n_pair + pair_col) * blocks_dev + number
            start = pl.multiple_of(lax.rem(pair_block, virt_blocks) * pair_rows, pair_rows)
            gap = table[:, pl.ds(start, pair_rows)] - occ[pair_block // virt_blocks]
            alive = (centre >= 0) & (number < of_region(region)) & (records[0][m * band + slot] > 0)
            for w in range(freq_count):
                omega = freq[w]
                root = jnp.sqrt(2.0 * gap / (gap * gap + omega * omega))
                roots[m, pl.ds(root_row(band, freq_count, None, slot, w), 1), :] = root
                masked[m, slot, w] = root * alive.astype(jnp.float32)
                plain[m, slot, w] = root
                for delta in range(1, band - slot):
                    there = m + ((aux_pos + delta) >= n_aux).astype(jnp.int32)
                    row = jnp.minimum(there, blocks_dev - 1) * band + slot + delta
                    both = alive & (there < blocks_dev) & (records[(n_aux - delta) % n_aux][row] > 0)
                    spot = root_row(band, freq_count, delta, slot, w)
                    kept = root * both.astype(jnp.float32)
                    roots[m, pl.ds(spot, 1), :] = kept
                    if delta == 1:
                        one[m, slot, w] = kept
                if slot == 0:
                    there = m + ((aux_pos + 2) >= n_aux).astype(jnp.int32)
                    row = jnp.minimum(there, blocks_dev - 1) * band + 2
                    both = (centre >= 0) & (number < of_region(region)) & (there < blocks_dev)
                    both = both & (records[n_aux - 1][m * band + 1] > 0) & (records[n_aux - 2][row] > 0)
                    spot = root_row(band, freq_count, band, 0, w)
                    roots[m, pl.ds(spot, 1), :] = root * both.astype(jnp.float32)
    for m in range(blocks_dev):
        for w in range(freq_count):
            total = None
            for slot in range(band):
                a = (own_tile(own, slot, m, blocks_dev).astype(jnp.float32) * masked[m, slot, w]).astype(jnp.bfloat16)
                term = dot(a, a)
                total = term if total is None else total + term
            out[w, m] = total
            total = None
            for slot in range(band - 1):
                a = (own_tile(own, slot, m, blocks_dev).astype(jnp.float32) * one[m, slot, w]).astype(jnp.bfloat16)
                b = (far[slot * blocks_dev + m].astype(jnp.float32) * plain[m, slot, w]).astype(jnp.bfloat16)
                term = dot(a, b)
                total = term if total is None else total + term
            out_one[w, m] = total


def first_rows(dims, records, occ, freq, table, own, far, after):
    n_aux, n_pair, blocks_dev, band, freq_count = dims
    aux_rows, pair_rows = own[0].shape[-2:]
    return pl.pallas_call(
        functools.partial(first_kernel, dims),
        out_shape=[
            jax.ShapeDtypeStruct((freq_count, blocks_dev, aux_rows, aux_rows), jnp.float32),
            jax.ShapeDtypeStruct((freq_count, blocks_dev, aux_rows, aux_rows), jnp.float32),
            jax.ShapeDtypeStruct((blocks_dev, root_rows(band, freq_count), pair_rows), jnp.float32),
            jax.ShapeDtypeStruct(own[0].shape, own[0].dtype),
        ],
        in_specs=[SMEM] * (n_aux + 2) + [VMEM] * 4 + [ANY] * len(after),
        out_specs=[VMEM] * 4,
        compiler_params=PARAMS,
        cost_estimate=COST,
    )(*records, occ, freq, table, *own, far, *after)


def odd_kernel(dims, roots, own, far, add, out, zeros):
    n_aux, n_pair, blocks_dev, band, freq_count = dims
    zeros[...] = jnp.zeros_like(zeros)
    for m in range(blocks_dev):
        left = own[m].astype(jnp.float32)
        right = far[m].astype(jnp.float32)
        for w in range(freq_count):
            kept = roots[m, pl.ds(root_row(band, freq_count, 1, 0, w), 1), :]
            root = roots[m, pl.ds(root_row(band, freq_count, None, 0, w), 1), :]
            term = dot((left * kept).astype(jnp.bfloat16), (right * root).astype(jnp.bfloat16))
            out[w, m] = add[w, m] + term


def odd_rows(dims, roots, own, far, add):
    n_aux, n_pair, blocks_dev, band, freq_count = dims
    aux_rows = own.shape[-2]
    return pl.pallas_call(
        functools.partial(odd_kernel, dims),
        out_shape=[
            jax.ShapeDtypeStruct((freq_count, blocks_dev, aux_rows, aux_rows), jnp.float32),
            jax.ShapeDtypeStruct((aux_rows // n_pair, aux_rows), jnp.float32),
        ],
        in_specs=[VMEM] * 4,
        out_specs=[VMEM] * 2,
        compiler_params=PARAMS,
        cost_estimate=COST,
    )(roots, own, far, add)


def second_kernel(dims, pieces, roots, own, lower, *refs):
    n_aux, n_pair, blocks_dev, band, freq_count = dims
    out, out_next = refs[-2:]
    for m in range(blocks_dev):
        n, row = pieces[m]
        left = own[m].astype(jnp.float32)
        right = refs[n][row].astype(jnp.float32)
        other = lower[m].astype(jnp.float32)
        for w in range(freq_count):
            kept = roots[m, pl.ds(root_row(band, freq_count, 2, 0, w), 1), :]
            root = roots[m, pl.ds(root_row(band, freq_count, None, 0, w), 1), :]
            next_kept = roots[m, pl.ds(root_row(band, freq_count, band, 0, w), 1), :]
            scaled = (right * root).astype(jnp.bfloat16)
            out[w, m] = dot((left * kept).astype(jnp.bfloat16), scaled)
            out_next[w, m] = dot((other * next_kept).astype(jnp.bfloat16), scaled)


def second_rows(dims, roots, own, lower, c2, after):
    n_aux, n_pair, blocks_dev, band, freq_count = dims
    aux_rows = own[0].shape[-2]
    pieces = [(n, row) for n, array in enumerate(c2) for row in range(array.shape[0])]
    return pl.pallas_call(
        functools.partial(second_kernel, dims, pieces),
        out_shape=[jax.ShapeDtypeStruct((freq_count, blocks_dev, aux_rows, aux_rows), jnp.float32)] * 2,
        in_specs=[VMEM] * (3 + len(c2)) + [ANY] * len(after),
        out_specs=[VMEM] * 2,
        compiler_params=PARAMS,
        cost_estimate=COST,
    )(roots, own[0], lower, *c2, *after)


def halve(keep, pair_col, step, n_pair, rings, scale):
    freq_count, count, shares, height, width = keep.shape
    keep = keep.reshape(freq_count, count, shares // 2, 2, height, width)
    bit = lax.shift_right_logical(pair_col, jnp.uint32(step.bit_length() - 1)) & jnp.uint32(1)

    def pick(which):
        zero = jnp.uint32(0)
        sizes = (freq_count, count, shares // 2, 1, height, width)
        return lax.dynamic_slice(keep, [zero, zero, zero, which, zero, zero], sizes)[:, :, :, 0]

    part, mine = pick(bit ^ jnp.uint32(1)), pick(bit)
    sent = (part * scale).astype(jnp.float16)
    pairs = [(ring * n_pair + s, ring * n_pair + (s ^ step)) for ring in rings for s in range(n_pair)]
    got = lax.ppermute(sent, ("aux", "pair"), pairs)
    return mine + got.astype(jnp.float32) * (1.0 / scale), got


def totals(rows, pair_col, n_pair, rings, scale):
    freq_count, count, aux_rows, width = rows.shape
    keep = rows.reshape(freq_count, count, n_pair, aux_rows // n_pair, width)
    stages, step = [], 1
    while step < n_pair:
        keep, got = halve(keep, pair_col, step, n_pair, rings, scale)
        stages.append(got[0, 0, 0].astype(jnp.float32))
        step *= 2
    return stages, keep[:, :, 0]


def total_at_once(rows, pair_col, n_pair, rings, scale):
    freq_count, count, aux_rows, width = rows.shape
    height = aux_rows // n_pair

    def share(column):
        zero = jnp.uint32(0)
        start = column * jnp.uint32(height)
        return lax.dynamic_slice(rows, [zero, zero, start, zero], (freq_count, count, height, width))

    far = []
    for k in reversed(range(1, n_pair)):
        sent = (share(pair_col ^ jnp.uint32(k)) * scale).astype(jnp.float16)
        pairs = [(ring * n_pair + s, ring * n_pair + (s ^ k)) for ring in rings for s in range(n_pair)]
        far.append(lax.ppermute(sent, ("aux", "pair"), pairs).astype(jnp.float32))
    return share(pair_col) + sum(far) * (1.0 / scale)


def on_device(three_centre, locality, live_blocks, occ_energy, virt_energy, frequencies):
    n_aux = lax.axis_size("aux")
    n_pair = lax.axis_size("pair")
    pair_col = lax.axis_index("pair").astype(jnp.uint32)
    tiles = three_centre[0, 0, :, :, 0]
    blocks_dev, band, aux_rows, pair_rows = tiles.shape
    freq_count = frequencies.shape[0]
    dims = (n_aux, n_pair, blocks_dev, band, freq_count)
    scale = 128.0 / n_pair
    record = jnp.concatenate([locality[0, 0].reshape(-1), live_blocks[0]])
    records = [record] + [
        lax.ppermute(record, "aux", [(s, (s + k) % n_aux) for s in range(n_aux)]) for k in range(1, n_aux)
    ]
    two = chunks_of(blocks_dev, SPLIT)
    whole = list(range(n_aux))
    evens, odds = whole[::2], whole[1::2]
    plan = [(2, 2, first, count) for first, count in two]
    first_slot, rest, near_two, far_two = pack(tiles, plan)
    own = (first_slot, rest)
    down2 = [(s, (s - 2) % n_aux) for s in whole]
    c2 = [lax.ppermute(near_two, "aux", down2)]
    (far_two,) = tie([far_two], records[1:] + c2)
    c2.append(lax.ppermute(far_two, "aux", down2))
    to_even = lax.ppermute(rest, "aux", [(s, s - 1) for s in odds])
    table = virt_energy.reshape(1, -1)
    rows0, rows_even, roots, to_one = first_rows(dims, records, occ_energy, frequencies, table, own, to_even, [far_two])
    b1 = lax.ppermute(to_one, "aux", [(s, (s - 1) % n_aux) for s in evens])
    bits0, z0 = totals(rows0, pair_col, n_pair, whole, scale)
    bits_even, z_even = totals(rows_even, pair_col, n_pair, evens, scale)
    rows2, rows_next = second_rows(dims, roots, own, to_even, c2, [bits_even[-1], bits0[-1]])
    bits2, z2 = totals(rows2, pair_col, n_pair, whole, scale)
    term = lax.ppermute((rows_next * scale).astype(jnp.float16), "aux", [(s, s + 1) for s in evens])
    term = term.astype(jnp.float32) * (1.0 / scale)
    rows_odd, zeros = odd_rows(dims, roots, first_slot, b1, term)
    (rows_odd,) = tie([rows_odd], [bits2[-1] + zeros])
    z_odd = total_at_once(rows_odd, pair_col, n_pair, odds, scale)
    even = lax.axis_index("aux").astype(jnp.uint32) & jnp.uint32(1) == 0
    out = jnp.concatenate([z0, jnp.where(even, z_even, z_odd), z2], axis=-1)
    return out[:, :, None]


def solution(mesh):
    return jax.shard_map(
        on_device,
        mesh=mesh,
        in_specs=(
            P(("grp", "aux"), "pair", None, None, None, None, None),
            P(("grp", "aux"), "pair", None, None, None),
            P(("grp", "aux"), "pair"),
            P("grp"),
            P("grp"),
            P("grp"),
        ),
        out_specs=P(None, None, ("grp", "aux"), "pair", None),
        check_vma=False,
    )
```

```python
import functools

import jax
import jax.numpy as jnp
from jax import lax
from jax.experimental import pallas as pl
from jax.experimental.pallas import tpu as pltpu
from jax.sharding import PartitionSpec as P

LIMIT = 16 << 20
SPLIT = (1, 7)
COST = pl.CostEstimate(flops=1000, bytes_accessed=1000, transcendentals=0)
PARAMS = pltpu.CompilerParams(vmem_limit_bytes=LIMIT)
ANY = pl.BlockSpec(memory_space=pl.ANY)
HBM = pl.BlockSpec(memory_space=pltpu.HBM)
SMEM = pl.BlockSpec(memory_space=pltpu.SMEM)
VMEM = pl.BlockSpec(memory_space=pltpu.VMEM)
DMA = pltpu.SemaphoreType.DMA


def chunks_of(count, sizes):
    ends = [count * sum(sizes[: n + 1]) // sum(sizes) for n in range(len(sizes))]
    return [(a, b - a) for a, b in zip([0] + ends[:-1], ends)]


def dot(a, b):
    return lax.dot_general(a, b, (((1,), (1,)), ((), ())), preferred_element_type=jnp.float32)


def pack_kernel(plan, tiles, first_slot, rest, *outs):
    blocks_dev, band = tiles.shape[:2]
    aux_pos = lax.axis_index("aux")
    for out, (slot, back, first, count) in zip(outs, plan):
        shift = (aux_pos < back).astype(jnp.int32)
        for i in range(count):
            out[i] = tiles[jnp.minimum(first + i + shift, blocks_dev - 1), slot]
    for m in range(blocks_dev):
        first_slot[m] = tiles[m, 0]
        for slot in range(1, band):
            rest[(slot - 1) * blocks_dev + m] = tiles[m, slot]


def pack(tiles, plan):
    blocks_dev, band, aux_rows, pair_rows = tiles.shape
    counts = [blocks_dev, (band - 1) * blocks_dev] + [part[3] for part in plan]
    return pl.pallas_call(
        functools.partial(pack_kernel, plan),
        out_shape=[jax.ShapeDtypeStruct((count, aux_rows, pair_rows), tiles.dtype) for count in counts],
        in_specs=[VMEM],
        out_specs=[VMEM] * len(counts),
        compiler_params=PARAMS,
        cost_estimate=COST,
    )(tiles)


def tie(arrays, after):
    return pl.pallas_call(
        lambda *refs: None,
        out_shape=[jax.ShapeDtypeStruct(array.shape, array.dtype) for array in arrays],
        in_specs=[ANY] * (len(arrays) + len(after)),
        out_specs=[ANY] * len(arrays),
        input_output_aliases={n: n for n in range(len(arrays))},
        compiler_params=PARAMS,
        cost_estimate=COST,
    )(*arrays, *after)


def root_row(band, freq_count, delta, slot, w):
    before = 0 if delta is None else band + sum(band - d for d in range(1, delta))
    return (before + slot) * freq_count + w


def root_rows(band, freq_count):
    return -(-(root_row(band, freq_count, band, 0, 0) + freq_count) // 8) * 8


def own_tile(own, slot, m, blocks_dev):
    return own[0][m] if slot == 0 else own[1][(slot - 1) * blocks_dev + m]


def first_kernel(dims, *refs):
    n_aux, n_pair, blocks_dev, band, freq_count = dims
    records = refs[:n_aux]
    occ, freq, table = refs[n_aux : n_aux + 3]
    own, far = refs[n_aux + 3 : n_aux + 5], refs[n_aux + 5]
    out, out_one, roots, to_one = refs[-4:]
    pair_rows = own[0].shape[-1]
    virt_blocks = table.shape[1] // pair_rows
    aux_pos, pair_col = lax.axis_index("aux"), lax.axis_index("pair")

    def of_region(region):
        live = records[0][blocks_dev * band]
        for k in range(1, n_aux):
            live = jnp.where(lax.rem(aux_pos - region + n_aux, n_aux) == k, records[k][blocks_dev * band], live)
        return live

    for m in range(blocks_dev):
        to_one[m] = own[1][jnp.minimum(m + (aux_pos < 1).astype(jnp.int32), blocks_dev - 1)]

    masked, plain, one = {}, {}, {}
    for m in range(blocks_dev):
        block = m * n_aux + aux_pos
        for slot in range(band):
            centre = block - slot
            safe = jnp.maximum(centre, 0)
            region = safe // blocks_dev
            number = lax.rem(safe, blocks_dev)
            pair_block = (region * n_pair + pair_col) * blocks_dev + number
            start = pl.multiple_of(lax.rem(pair_block, virt_blocks) * pair_rows, pair_rows)
            gap = table[:, pl.ds(start, pair_rows)] - occ[pair_block // virt_blocks]
            alive = (centre >= 0) & (number < of_region(region)) & (records[0][m * band + slot] > 0)
            for w in range(freq_count):
                omega = freq[w]
                root = jnp.sqrt(2.0 * gap / (gap * gap + omega * omega))
                roots[m, pl.ds(root_row(band, freq_count, None, slot, w), 1), :] = root
                masked[m, slot, w] = root * alive.astype(jnp.float32)
                plain[m, slot, w] = root
                for delta in range(1, band - slot):
                    there = m + ((aux_pos + delta) >= n_aux).astype(jnp.int32)
                    row = jnp.minimum(there, blocks_dev - 1) * band + slot + delta
                    both = alive & (there < blocks_dev) & (records[(n_aux - delta) % n_aux][row] > 0)
                    spot = root_row(band, freq_count, delta, slot, w)
                    kept = root * both.astype(jnp.float32)
                    roots[m, pl.ds(spot, 1), :] = kept
                    if delta == 1:
                        one[m, slot, w] = kept
                if slot == 0:
                    there = m + ((aux_pos + 2) >= n_aux).astype(jnp.int32)
                    row = jnp.minimum(there, blocks_dev - 1) * band + 2
                    both = (centre >= 0) & (number < of_region(region)) & (there < blocks_dev)
                    both = both & (records[n_aux - 1][m * band + 1] > 0) & (records[n_aux - 2][row] > 0)
                    spot = root_row(band, freq_count, band, 0, w)
                    roots[m, pl.ds(spot, 1), :] = root * both.astype(jnp.float32)
    for m in range(blocks_dev):
        for w in range(freq_count):
            total = None
            for slot in range(band):
                a = (own_tile(own, slot, m, blocks_dev).astype(jnp.float32) * masked[m, slot, w]).astype(jnp.bfloat16)
                term = dot(a, a)
                total = term if total is None else total + term
            out[w, m] = total
            total = None
            for slot in range(band - 1):
                a = (own_tile(own, slot, m, blocks_dev).astype(jnp.float32) * one[m, slot, w]).astype(jnp.bfloat16)
                b = (far[slot * blocks_dev + m].astype(jnp.float32) * plain[m, slot, w]).astype(jnp.bfloat16)
                term = dot(a, b)
                total = term if total is None else total + term
            out_one[w, m] = total


def first_rows(dims, records, occ, freq, table, own, far, after):
    n_aux, n_pair, blocks_dev, band, freq_count = dims
    aux_rows, pair_rows = own[0].shape[-2:]
    return pl.pallas_call(
        functools.partial(first_kernel, dims),
        out_shape=[
            jax.ShapeDtypeStruct((freq_count, blocks_dev, aux_rows, aux_rows), jnp.float32),
            jax.ShapeDtypeStruct((freq_count, blocks_dev, aux_rows, aux_rows), jnp.float32),
            jax.ShapeDtypeStruct((blocks_dev, root_rows(band, freq_count), pair_rows), jnp.float32),
            jax.ShapeDtypeStruct(own[0].shape, own[0].dtype),
        ],
        in_specs=[SMEM] * (n_aux + 2) + [VMEM] * 4 + [ANY] * len(after),
        out_specs=[VMEM] * 4,
        compiler_params=PARAMS,
        cost_estimate=COST,
    )(*records, occ, freq, table, *own, far, *after)


def odd_kernel(dims, roots, own, far, add, out, zeros):
    n_aux, n_pair, blocks_dev, band, freq_count = dims
    zeros[...] = jnp.zeros_like(zeros)
    for m in range(blocks_dev):
        left = own[m].astype(jnp.float32)
        right = far[m].astype(jnp.float32)
        for w in range(freq_count):
            kept = roots[m, pl.ds(root_row(band, freq_count, 1, 0, w), 1), :]
            root = roots[m, pl.ds(root_row(band, freq_count, None, 0, w), 1), :]
            term = dot((left * kept).astype(jnp.bfloat16), (right * root).astype(jnp.bfloat16))
            out[w, m] = add[w, m] + term


def odd_rows(dims, roots, own, far, add):
    n_aux, n_pair, blocks_dev, band, freq_count = dims
    aux_rows = own.shape[-2]
    return pl.pallas_call(
        functools.partial(odd_kernel, dims),
        out_shape=[
            jax.ShapeDtypeStruct((freq_count, blocks_dev, aux_rows, aux_rows), jnp.float32),
            jax.ShapeDtypeStruct((aux_rows // n_pair, aux_rows), jnp.float32),
        ],
        in_specs=[VMEM] * 4,
        out_specs=[VMEM] * 2,
        compiler_params=PARAMS,
        cost_estimate=COST,
    )(roots, own, far, add)


def second_kernel(dims, pieces, roots, own, lower, *refs):
    n_aux, n_pair, blocks_dev, band, freq_count = dims
    out, out_next = refs[-2:]
    for m in range(blocks_dev):
        n, row = pieces[m]
        left = own[m].astype(jnp.float32)
        right = refs[n][row].astype(jnp.float32)
        other = lower[m].astype(jnp.float32)
        for w in range(freq_count):
            kept = roots[m, pl.ds(root_row(band, freq_count, 2, 0, w), 1), :]
            root = roots[m, pl.ds(root_row(band, freq_count, None, 0, w), 1), :]
            next_kept = roots[m, pl.ds(root_row(band, freq_count, band, 0, w), 1), :]
            scaled = (right * root).astype(jnp.bfloat16)
            out[w, m] = dot((left * kept).astype(jnp.bfloat16), scaled)
            out_next[w, m] = dot((other * next_kept).astype(jnp.bfloat16), scaled)


def second_rows(dims, roots, own, lower, c2, after):
    n_aux, n_pair, blocks_dev, band, freq_count = dims
    aux_rows = own[0].shape[-2]
    pieces = [(n, row) for n, array in enumerate(c2) for row in range(array.shape[0])]
    return pl.pallas_call(
        functools.partial(second_kernel, dims, pieces),
        out_shape=[jax.ShapeDtypeStruct((freq_count, blocks_dev, aux_rows, aux_rows), jnp.float32)] * 2,
        in_specs=[VMEM] * (3 + len(c2)) + [ANY] * len(after),
        out_specs=[VMEM] * 2,
        compiler_params=PARAMS,
        cost_estimate=COST,
    )(roots, own[0], lower, *c2, *after)


def halve(keep, pair_col, step, n_pair, rings, scale):
    freq_count, count, shares, height, width = keep.shape
    keep = keep.reshape(freq_count, count, shares // 2, 2, height, width)
    bit = lax.shift_right_logical(pair_col, jnp.uint32(step.bit_length() - 1)) & jnp.uint32(1)

    def pick(which):
        zero = jnp.uint32(0)
        sizes = (freq_count, count, shares // 2, 1, height, width)
        return lax.dynamic_slice(keep, [zero, zero, zero, which, zero, zero], sizes)[:, :, :, 0]

    part, mine = pick(bit ^ jnp.uint32(1)), pick(bit)
    sent = (part * scale).astype(jnp.float16)
    pairs = [(ring * n_pair + s, ring * n_pair + (s ^ step)) for ring in rings for s in range(n_pair)]
    got = lax.ppermute(sent, ("aux", "pair"), pairs)
    return mine + got.astype(jnp.float32) * (1.0 / scale), got


def totals(rows, pair_col, n_pair, rings, scale):
    freq_count, count, aux_rows, width = rows.shape
    keep = rows.reshape(freq_count, count, n_pair, aux_rows // n_pair, width)
    stages, step = [], 1
    while step < n_pair:
        keep, got = halve(keep, pair_col, step, n_pair, rings, scale)
        stages.append(got[0, 0, 0].astype(jnp.float32))
        step *= 2
    return stages, keep[:, :, 0]


def total_at_once(rows, pair_col, n_pair, rings, scale):
    freq_count, count, aux_rows, width = rows.shape
    height = aux_rows // n_pair

    def share(column):
        zero = jnp.uint32(0)
        start = column * jnp.uint32(height)
        return lax.dynamic_slice(rows, [zero, zero, start, zero], (freq_count, count, height, width))

    far = []
    for k in range(1, n_pair):
        sent = (share(pair_col ^ jnp.uint32(k)) * scale).astype(jnp.float16)
        pairs = [(ring * n_pair + s, ring * n_pair + (s ^ k)) for ring in rings for s in range(n_pair)]
        far.append(lax.ppermute(sent, ("aux", "pair"), pairs).astype(jnp.float32))
    return share(pair_col) + sum(far) * (1.0 / scale)


def on_device(three_centre, locality, live_blocks, occ_energy, virt_energy, frequencies):
    n_aux = lax.axis_size("aux")
    n_pair = lax.axis_size("pair")
    pair_col = lax.axis_index("pair").astype(jnp.uint32)
    tiles = three_centre[0, 0, :, :, 0]
    blocks_dev, band, aux_rows, pair_rows = tiles.shape
    freq_count = frequencies.shape[0]
    dims = (n_aux, n_pair, blocks_dev, band, freq_count)
    scale = 128.0 / n_pair
    record = jnp.concatenate([locality[0, 0].reshape(-1), live_blocks[0]])
    records = [record] + [
        lax.ppermute(record, "aux", [(s, (s + k) % n_aux) for s in range(n_aux)]) for k in range(1, n_aux)
    ]
    two = chunks_of(blocks_dev, SPLIT)
    whole = list(range(n_aux))
    evens, odds = whole[::2], whole[1::2]
    plan = [(2, 2, first, count) for first, count in two]
    first_slot, rest, near_two, far_two = pack(tiles, plan)
    own = (first_slot, rest)
    down2 = [(s, (s - 2) % n_aux) for s in whole]
    c2 = [lax.ppermute(near_two, "aux", down2)]
    (far_two,) = tie([far_two], records[1:] + c2)
    c2.append(lax.ppermute(far_two, "aux", down2))
    to_even = lax.ppermute(rest, "aux", [(s, s - 1) for s in odds])
    table = virt_energy.reshape(1, -1)
    rows0, rows_even, roots, to_one = first_rows(dims, records, occ_energy, frequencies, table, own, to_even, [far_two])
    b1 = lax.ppermute(to_one, "aux", [(s, (s - 1) % n_aux) for s in evens])
    bits0, z0 = totals(rows0, pair_col, n_pair, whole, scale)
    bits_even, z_even = totals(rows_even, pair_col, n_pair, evens, scale)
    rows2, rows_next = second_rows(dims, roots, own, to_even, c2, [bits_even[-1], bits0[-1]])
    bits2, z2 = totals(rows2, pair_col, n_pair, whole, scale)
    term = lax.ppermute((rows_next * scale).astype(jnp.float16), "aux", [(s, s + 1) for s in evens])
    term = term.astype(jnp.float32) * (1.0 / scale)
    rows_odd, zeros = odd_rows(dims, roots, first_slot, b1, term)
    (rows_odd,) = tie([rows_odd], [bits2[-1] + zeros])
    z_odd = total_at_once(rows_odd, pair_col, n_pair, odds, scale)
    even = lax.axis_index("aux").astype(jnp.uint32) & jnp.uint32(1) == 0
    out = jnp.concatenate([z0, jnp.where(even, z_even, z_odd), z2], axis=-1)
    return out[:, :, None]


def solution(mesh):
    return jax.shard_map(
        on_device,
        mesh=mesh,
        in_specs=(
            P(("grp", "aux"), "pair", None, None, None, None, None),
            P(("grp", "aux"), "pair", None, None, None),
            P(("grp", "aux"), "pair"),
            P("grp"),
            P("grp"),
            P("grp"),
        ),
        out_specs=P(None, None, ("grp", "aux"), "pair", None),
        check_vma=False,
    )
```

```python
import functools

import jax
import jax.numpy as jnp
from jax import lax
from jax.experimental import pallas as pl
from jax.experimental.pallas import tpu as pltpu
from jax.sharding import PartitionSpec as P

LIMIT = 16 << 20
SPLIT = (2, 6)
COST = pl.CostEstimate(flops=1000, bytes_accessed=1000, transcendentals=0)
PARAMS = pltpu.CompilerParams(vmem_limit_bytes=LIMIT)
ANY = pl.BlockSpec(memory_space=pl.ANY)
HBM = pl.BlockSpec(memory_space=pltpu.HBM)
SMEM = pl.BlockSpec(memory_space=pltpu.SMEM)
VMEM = pl.BlockSpec(memory_space=pltpu.VMEM)
DMA = pltpu.SemaphoreType.DMA


def chunks_of(count, sizes):
    ends = [count * sum(sizes[: n + 1]) // sum(sizes) for n in range(len(sizes))]
    return [(a, b - a) for a, b in zip([0] + ends[:-1], ends)]


def dot(a, b):
    return lax.dot_general(a, b, (((1,), (1,)), ((), ())), preferred_element_type=jnp.float32)


def pack_kernel(plan, tiles, first_slot, rest, *outs):
    blocks_dev, band = tiles.shape[:2]
    aux_pos = lax.axis_index("aux")
    for out, (slot, back, first, count) in zip(outs, plan):
        shift = (aux_pos < back).astype(jnp.int32)
        for i in range(count):
            out[i] = tiles[jnp.minimum(first + i + shift, blocks_dev - 1), slot]
    for m in range(blocks_dev):
        first_slot[m] = tiles[m, 0]
        for slot in range(1, band):
            rest[(slot - 1) * blocks_dev + m] = tiles[m, slot]


def pack(tiles, plan):
    blocks_dev, band, aux_rows, pair_rows = tiles.shape
    counts = [blocks_dev, (band - 1) * blocks_dev] + [part[3] for part in plan]
    return pl.pallas_call(
        functools.partial(pack_kernel, plan),
        out_shape=[jax.ShapeDtypeStruct((count, aux_rows, pair_rows), tiles.dtype) for count in counts],
        in_specs=[VMEM],
        out_specs=[VMEM] * len(counts),
        compiler_params=PARAMS,
        cost_estimate=COST,
    )(tiles)


def tie(arrays, after):
    return pl.pallas_call(
        lambda *refs: None,
        out_shape=[jax.ShapeDtypeStruct(array.shape, array.dtype) for array in arrays],
        in_specs=[ANY] * (len(arrays) + len(after)),
        out_specs=[ANY] * len(arrays),
        input_output_aliases={n: n for n in range(len(arrays))},
        compiler_params=PARAMS,
        cost_estimate=COST,
    )(*arrays, *after)


def root_row(band, freq_count, delta, slot, w):
    before = 0 if delta is None else band + sum(band - d for d in range(1, delta))
    return (before + slot) * freq_count + w


def root_rows(band, freq_count):
    return -(-(root_row(band, freq_count, band, 0, 0) + freq_count) // 8) * 8


def own_tile(own, slot, m, blocks_dev):
    return own[0][m] if slot == 0 else own[1][(slot - 1) * blocks_dev + m]


def first_kernel(dims, *refs):
    n_aux, n_pair, blocks_dev, band, freq_count = dims
    records = refs[:n_aux]
    occ, freq, table = refs[n_aux : n_aux + 3]
    own, far = refs[n_aux + 3 : n_aux + 5], refs[n_aux + 5]
    out, out_one, roots, to_one = refs[-4:]
    pair_rows = own[0].shape[-1]
    virt_blocks = table.shape[1] // pair_rows
    aux_pos, pair_col = lax.axis_index("aux"), lax.axis_index("pair")

    def of_region(region):
        live = records[0][blocks_dev * band]
        for k in range(1, n_aux):
            live = jnp.where(lax.rem(aux_pos - region + n_aux, n_aux) == k, records[k][blocks_dev * band], live)
        return live

    for m in range(blocks_dev):
        to_one[m] = own[1][jnp.minimum(m + (aux_pos < 1).astype(jnp.int32), blocks_dev - 1)]

    masked, plain, one = {}, {}, {}
    for m in range(blocks_dev):
        block = m * n_aux + aux_pos
        for slot in range(band):
            centre = block - slot
            safe = jnp.maximum(centre, 0)
            region = safe // blocks_dev
            number = lax.rem(safe, blocks_dev)
            pair_block = (region * n_pair + pair_col) * blocks_dev + number
            start = pl.multiple_of(lax.rem(pair_block, virt_blocks) * pair_rows, pair_rows)
            gap = table[:, pl.ds(start, pair_rows)] - occ[pair_block // virt_blocks]
            alive = (centre >= 0) & (number < of_region(region)) & (records[0][m * band + slot] > 0)
            for w in range(freq_count):
                omega = freq[w]
                root = jnp.sqrt(2.0 * gap / (gap * gap + omega * omega))
                roots[m, pl.ds(root_row(band, freq_count, None, slot, w), 1), :] = root
                masked[m, slot, w] = root * alive.astype(jnp.float32)
                plain[m, slot, w] = root
                for delta in range(1, band - slot):
                    there = m + ((aux_pos + delta) >= n_aux).astype(jnp.int32)
                    row = jnp.minimum(there, blocks_dev - 1) * band + slot + delta
                    both = alive & (there < blocks_dev) & (records[(n_aux - delta) % n_aux][row] > 0)
                    spot = root_row(band, freq_count, delta, slot, w)
                    kept = root * both.astype(jnp.float32)
                    roots[m, pl.ds(spot, 1), :] = kept
                    if delta == 1:
                        one[m, slot, w] = kept
                if slot == 0:
                    there = m + ((aux_pos + 2) >= n_aux).astype(jnp.int32)
                    row = jnp.minimum(there, blocks_dev - 1) * band + 2
                    both = (centre >= 0) & (number < of_region(region)) & (there < blocks_dev)
                    both = both & (records[n_aux - 1][m * band + 1] > 0) & (records[n_aux - 2][row] > 0)
                    spot = root_row(band, freq_count, band, 0, w)
                    roots[m, pl.ds(spot, 1), :] = root * both.astype(jnp.float32)
    for m in range(blocks_dev):
        for w in range(freq_count):
            total = None
            for slot in range(band):
                a = (own_tile(own, slot, m, blocks_dev).astype(jnp.float32) * masked[m, slot, w]).astype(jnp.bfloat16)
                term = dot(a, a)
                total = term if total is None else total + term
            out[w, m] = total
            total = None
            for slot in range(band - 1):
                a = (own_tile(own, slot, m, blocks_dev).astype(jnp.float32) * one[m, slot, w]).astype(jnp.bfloat16)
                b = (far[slot * blocks_dev + m].astype(jnp.float32) * plain[m, slot, w]).astype(jnp.bfloat16)
                term = dot(a, b)
                total = term if total is None else total + term
            out_one[w, m] = total


def first_rows(dims, records, occ, freq, table, own, far, after):
    n_aux, n_pair, blocks_dev, band, freq_count = dims
    aux_rows, pair_rows = own[0].shape[-2:]
    return pl.pallas_call(
        functools.partial(first_kernel, dims),
        out_shape=[
            jax.ShapeDtypeStruct((freq_count, blocks_dev, aux_rows, aux_rows), jnp.float32),
            jax.ShapeDtypeStruct((freq_count, blocks_dev, aux_rows, aux_rows), jnp.float32),
            jax.ShapeDtypeStruct((blocks_dev, root_rows(band, freq_count), pair_rows), jnp.float32),
            jax.ShapeDtypeStruct(own[0].shape, own[0].dtype),
        ],
        in_specs=[SMEM] * (n_aux + 2) + [VMEM] * 4 + [ANY] * len(after),
        out_specs=[VMEM] * 4,
        compiler_params=PARAMS,
        cost_estimate=COST,
    )(*records, occ, freq, table, *own, far, *after)


def odd_kernel(dims, roots, own, far, add, out, zeros):
    n_aux, n_pair, blocks_dev, band, freq_count = dims
    zeros[...] = jnp.zeros_like(zeros)
    for m in range(blocks_dev):
        left = own[m].astype(jnp.float32)
        right = far[m].astype(jnp.float32)
        for w in range(freq_count):
            kept = roots[m, pl.ds(root_row(band, freq_count, 1, 0, w), 1), :]
            root = roots[m, pl.ds(root_row(band, freq_count, None, 0, w), 1), :]
            term = dot((left * kept).astype(jnp.bfloat16), (right * root).astype(jnp.bfloat16))
            out[w, m] = add[w, m] + term


def odd_rows(dims, roots, own, far, add):
    n_aux, n_pair, blocks_dev, band, freq_count = dims
    aux_rows = own.shape[-2]
    return pl.pallas_call(
        functools.partial(odd_kernel, dims),
        out_shape=[
            jax.ShapeDtypeStruct((freq_count, blocks_dev, aux_rows, aux_rows), jnp.float32),
            jax.ShapeDtypeStruct((aux_rows // n_pair, aux_rows), jnp.float32),
        ],
        in_specs=[VMEM] * 4,
        out_specs=[VMEM] * 2,
        compiler_params=PARAMS,
        cost_estimate=COST,
    )(roots, own, far, add)


def second_kernel(dims, pieces, roots, own, lower, *refs):
    n_aux, n_pair, blocks_dev, band, freq_count = dims
    out, out_next = refs[-2:]
    for m in range(blocks_dev):
        n, row = pieces[m]
        left = own[m].astype(jnp.float32)
        right = refs[n][row].astype(jnp.float32)
        other = lower[m].astype(jnp.float32)
        for w in range(freq_count):
            kept = roots[m, pl.ds(root_row(band, freq_count, 2, 0, w), 1), :]
            root = roots[m, pl.ds(root_row(band, freq_count, None, 0, w), 1), :]
            next_kept = roots[m, pl.ds(root_row(band, freq_count, band, 0, w), 1), :]
            scaled = (right * root).astype(jnp.bfloat16)
            out[w, m] = dot((left * kept).astype(jnp.bfloat16), scaled)
            out_next[w, m] = dot((other * next_kept).astype(jnp.bfloat16), scaled)


def second_rows(dims, roots, own, lower, c2, after):
    n_aux, n_pair, blocks_dev, band, freq_count = dims
    aux_rows = own[0].shape[-2]
    pieces = [(n, row) for n, array in enumerate(c2) for row in range(array.shape[0])]
    return pl.pallas_call(
        functools.partial(second_kernel, dims, pieces),
        out_shape=[jax.ShapeDtypeStruct((freq_count, blocks_dev, aux_rows, aux_rows), jnp.float32)] * 2,
        in_specs=[VMEM] * (3 + len(c2)) + [ANY] * len(after),
        out_specs=[VMEM] * 2,
        compiler_params=PARAMS,
        cost_estimate=COST,
    )(roots, own[0], lower, *c2, *after)


def halve(keep, pair_col, step, n_pair, rings, scale):
    freq_count, count, shares, height, width = keep.shape
    keep = keep.reshape(freq_count, count, shares // 2, 2, height, width)
    bit = lax.shift_right_logical(pair_col, jnp.uint32(step.bit_length() - 1)) & jnp.uint32(1)

    def pick(which):
        zero = jnp.uint32(0)
        sizes = (freq_count, count, shares // 2, 1, height, width)
        return lax.dynamic_slice(keep, [zero, zero, zero, which, zero, zero], sizes)[:, :, :, 0]

    part, mine = pick(bit ^ jnp.uint32(1)), pick(bit)
    sent = (part * scale).astype(jnp.float16)
    pairs = [(ring * n_pair + s, ring * n_pair + (s ^ step)) for ring in rings for s in range(n_pair)]
    got = lax.ppermute(sent, ("aux", "pair"), pairs)
    return mine + got.astype(jnp.float32) * (1.0 / scale), got


def totals(rows, pair_col, n_pair, rings, scale):
    freq_count, count, aux_rows, width = rows.shape
    keep = rows.reshape(freq_count, count, n_pair, aux_rows // n_pair, width)
    stages, step = [], 1
    while step < n_pair:
        keep, got = halve(keep, pair_col, step, n_pair, rings, scale)
        stages.append(got[0, 0, 0].astype(jnp.float32))
        step *= 2
    return stages, keep[:, :, 0]


def total_at_once(rows, pair_col, n_pair, rings, scale):
    freq_count, count, aux_rows, width = rows.shape
    height = aux_rows // n_pair

    def share(column):
        zero = jnp.uint32(0)
        start = column * jnp.uint32(height)
        return lax.dynamic_slice(rows, [zero, zero, start, zero], (freq_count, count, height, width))

    far = []
    for k in reversed(range(1, n_pair)):
        sent = (share(pair_col ^ jnp.uint32(k)) * scale).astype(jnp.float16)
        pairs = [(ring * n_pair + s, ring * n_pair + (s ^ k)) for ring in rings for s in range(n_pair)]
        far.append(lax.ppermute(sent, ("aux", "pair"), pairs).astype(jnp.float32))
    return share(pair_col) + sum(far) * (1.0 / scale)


def on_device(three_centre, locality, live_blocks, occ_energy, virt_energy, frequencies):
    n_aux = lax.axis_size("aux")
    n_pair = lax.axis_size("pair")
    pair_col = lax.axis_index("pair").astype(jnp.uint32)
    tiles = three_centre[0, 0, :, :, 0]
    blocks_dev, band, aux_rows, pair_rows = tiles.shape
    freq_count = frequencies.shape[0]
    dims = (n_aux, n_pair, blocks_dev, band, freq_count)
    scale = 128.0 / n_pair
    record = jnp.concatenate([locality[0, 0].reshape(-1), live_blocks[0]])
    records = [record] + [
        lax.ppermute(record, "aux", [(s, (s + k) % n_aux) for s in range(n_aux)]) for k in range(1, n_aux)
    ]
    two = chunks_of(blocks_dev, SPLIT)
    whole = list(range(n_aux))
    evens, odds = whole[::2], whole[1::2]
    plan = [(2, 2, first, count) for first, count in two]
    first_slot, rest, near_two, far_two = pack(tiles, plan)
    own = (first_slot, rest)
    down2 = [(s, (s - 2) % n_aux) for s in whole]
    c2 = [lax.ppermute(near_two, "aux", down2)]
    (far_two,) = tie([far_two], records[1:] + c2)
    c2.append(lax.ppermute(far_two, "aux", down2))
    to_even = lax.ppermute(rest, "aux", [(s, s - 1) for s in odds])
    table = virt_energy.reshape(1, -1)
    rows0, rows_even, roots, to_one = first_rows(dims, records, occ_energy, frequencies, table, own, to_even, [far_two])
    b1 = lax.ppermute(to_one, "aux", [(s, (s - 1) % n_aux) for s in evens])
    bits0, z0 = totals(rows0, pair_col, n_pair, whole, scale)
    bits_even, z_even = totals(rows_even, pair_col, n_pair, evens, scale)
    rows2, rows_next = second_rows(dims, roots, own, to_even, c2, [bits_even[-1], bits0[-1]])
    bits2, z2 = totals(rows2, pair_col, n_pair, whole, scale)
    term = lax.ppermute((rows_next * scale).astype(jnp.float16), "aux", [(s, s + 1) for s in evens])
    term = term.astype(jnp.float32) * (1.0 / scale)
    rows_odd, zeros = odd_rows(dims, roots, first_slot, b1, term)
    (rows_odd,) = tie([rows_odd], [bits2[-1] + zeros])
    z_odd = total_at_once(rows_odd, pair_col, n_pair, odds, scale)
    even = lax.axis_index("aux").astype(jnp.uint32) & jnp.uint32(1) == 0
    out = jnp.concatenate([z0, jnp.where(even, z_even, z_odd), z2], axis=-1)
    return out[:, :, None]


def solution(mesh):
    return jax.shard_map(
        on_device,
        mesh=mesh,
        in_specs=(
            P(("grp", "aux"), "pair", None, None, None, None, None),
            P(("grp", "aux"), "pair", None, None, None),
            P(("grp", "aux"), "pair"),
            P("grp"),
            P("grp"),
            P("grp"),
        ),
        out_specs=P(None, None, ("grp", "aux"), "pair", None),
        check_vma=False,
    )
```
